32 devices in a mesh: band: 4 (over y, x), dom: 8 (over z, core).
Axes of the slice: x: 2, y: 2, z: 4, core: 2. Of those that a mesh axis runs over, the one named last changes fastest.
Arguments:
- partial_density: float32 [4, 48, 96, 128], P('band', 'dom'), may hold values from 0.002 to 0.1
- moments: bfloat16 [9, 64], P(None, 'dom'), may hold values from 0.0099487305 to 0.099609375
- shape_functions: bfloat16 [64, 9, 6912], P('dom'), may hold values from 0.099609375 to 1
- sphere_offsets: int32 [3, 64], P(None, 'dom'), may hold values from 0 to 232, as said below
- owned_count: int32 [8], P('dom'), may hold values from 1 to 8, as said below
Outputs:
- potential: float32 [48, 96, 128], P('dom')
The draws below stay inside these ranges and needn't reach their ends.
Inputs may be any that keep to these rules, and one draw needn't show every extreme that they name: `sphere_offsets`: row 0 lies in 0 to 11, and in 0 to 0 for the last slab; row 1 in 0 to 168; row 2 in 0 to 232; each upper end is reached. `owned_count`: some slab owns exactly 8 atoms.
All inputs are finite; a program needn't handle non-finite values.
Results may differ from the reference program's by a relative error of at most 0.0003.
Values sent between devices are 32-bit elements; how exact they have to be, the bound alone decides.
A program may use at most 64 MiB of HBM per device.

```python
import math
import jax
import jax.numpy as jnp
from jax import lax

CX = 6
CY = 96
CZ = 128
SLOTS = 8
NL = 9
SBX = 12
SBY = 24
SBZ = 24
BLOCK = 6912
GROUPS = 4
NX = 48
SLOTS_ALL = 64
N_DOM = 8


def draw_owned_count(key, part):
    key = jax.random.fold_in(key, 11)
    first_key, second_key = jax.random.split(key)
    raw_counts = jax.random.randint(first_key, (N_DOM,), 0, SLOTS)
    counts = 1 + raw_counts * raw_counts // SLOTS
    chosen = jax.random.randint(second_key, (), 0, N_DOM)
    return jnp.where(jnp.arange(N_DOM) == chosen, SLOTS, counts).astype(jnp.int32)


def draw_sphere_offsets(key, part):
    key = jax.random.fold_in(key, 23)
    first_key, second_key, third_key = jax.random.split(key, 3)
    slot_total = SLOTS * N_DOM
    brick = jnp.arange(slot_total) // SLOTS
    upper_row = jnp.where(brick == N_DOM - 1, 2 * CX - SBX + 1, 2 * CX)
    row_offset = jax.random.randint(first_key, (slot_total,), 0, upper_row)
    row_offset = row_offset.at[0].set(jnp.where(N_DOM == 1, 2 * CX - SBX, 2 * CX - 1))
    col_offset = jax.random.randint(second_key, (slot_total,), 0, 2 * CY - SBY + 1)
    col_offset = col_offset.at[0].set(2 * CY - SBY)
    depth_offset = jax.random.randint(third_key, (slot_total,), 0, 2 * CZ - SBZ + 1)
    depth_offset = depth_offset.at[0].set(2 * CZ - SBZ).at[1].set(0)
    return jnp.stack([row_offset, col_offset, depth_offset]).astype(jnp.int32)


def block_scale(own_key, extent, shards, low, high):
    def one(axis_at, blocks):
        steps = jax.random.uniform(jax.random.fold_in(jax.random.fold_in(own_key, 6), axis_at), (blocks,), jnp.float32, low / len(shards), high / len(shards))
        return jnp.repeat(jnp.exp(steps), extent[axis_at] // blocks).reshape((-1,) + (1,) * (len(extent) - axis_at - 1))

    level = one(*shards[0])
    for cut in shards[1:]:
        level = level * one(*cut)
    return level


def setup_inputs(seed: int = 0) -> dict:
    key_of = jax.random.split(jax.random.key(seed), 6)
    return {
        "partial_density": jnp.clip(jnp.exp(math.log(0.1) - 3.912023 * jax.random.uniform(key_of[0], (GROUPS, NX, CY, CZ), jnp.float32) ** block_scale(key_of[0], (GROUPS, NX, CY, CZ), ((0, 4), (1, 8)), -0.2, 0.2)), 0.002, 0.1),
        "moments": jnp.clip(jnp.exp(math.log(0.099609375) - 2.3038113 * jax.random.uniform(key_of[1], (NL, SLOTS_ALL), jnp.float32) ** block_scale(key_of[1], (NL, SLOTS_ALL), ((1, 8),), -0.2, 0.2)), 0.0099487305, 0.099609375).astype(jnp.bfloat16),
        "shape_functions": jnp.clip(jnp.exp(math.log(1.0) - 2.306499 * jax.random.uniform(key_of[2], (SLOTS_ALL, NL, BLOCK), jnp.float32) ** block_scale(key_of[2], (SLOTS_ALL, NL, BLOCK), ((0, 8),), -0.2, 0.2)), 0.099609375, 1.0).astype(jnp.bfloat16),
        "sphere_offsets": draw_sphere_offsets(jax.random.fold_in(key_of[5], 71), 0),
        "owned_count": draw_owned_count(jax.random.fold_in(key_of[5], 71), 0),
    }


kappa_pbe = 0.804
mu_pbe = 0.2195
exchange_prefactor = -0.75 * (3.0 / 3.141592653589793) ** (1.0 / 3.0)
gradient_scale = 4.0 * (3.0 * 3.141592653589793 ** 2) ** (2.0 / 3.0)
half_inverse = 0.5 / 0.2


def refine(extended, direction):
    length = extended.shape[direction] - 2
    lower_cells = lax.slice_in_dim(extended, 0, length, axis=direction)
    middle_cells = lax.slice_in_dim(extended, 1, length + 1, axis=direction)
    upper_cells = lax.slice_in_dim(extended, 2, length + 2, axis=direction)
    even_cells = 0.75 * middle_cells + 0.25 * lower_cells
    odd_cells = 0.75 * middle_cells + 0.25 * upper_cells
    joined = jnp.stack([even_cells, odd_cells], axis=direction + 1)
    target = list(middle_cells.shape)
    target[direction] = 2 * length
    return joined.reshape(target)


def restrict(extended, direction):
    doubled = extended.shape[direction] - 2
    halved = doubled // 2

    def paired(start):
        piece = lax.slice_in_dim(extended, start, start + doubled, axis=direction)
        target = list(piece.shape)
        target[direction:direction + 1] = [halved, 2]
        return piece.reshape(target)

    centre = paired(1)
    outer_low = lax.index_in_dim(paired(0), 0, direction + 1, keepdims=False)
    outer_high = lax.index_in_dim(paired(2), 1, direction + 1, keepdims=False)
    first_half = lax.index_in_dim(centre, 0, direction + 1, keepdims=False)
    second_half = lax.index_in_dim(centre, 1, direction + 1, keepdims=False)
    return 0.125 * outer_low + 0.375 * (first_half + second_half) + 0.125 * outer_high


def exchange_parts(density, sigma):
    cube_root = jnp.cbrt(density)
    four_thirds = density * cube_root
    reduced = sigma / (gradient_scale * four_thirds * four_thirds)
    damped = 1.0 + mu_pbe * reduced / kappa_pbe
    enhance = 1.0 + kappa_pbe - kappa_pbe / damped
    slope = mu_pbe / (damped * damped)
    by_density = exchange_prefactor * cube_root * ((4.0 / 3.0) * enhance - (8.0 / 3.0) * reduced * slope)
    by_sigma = exchange_prefactor * slope / (gradient_scale * four_thirds)
    return by_density, by_sigma


def gradients(extended):
    grad_x = (extended[2:, 1:-1, 1:-1] - extended[:-2, 1:-1, 1:-1]) * half_inverse
    grad_y = (extended[1:-1, 2:, 1:-1] - extended[1:-1, :-2, 1:-1]) * half_inverse
    grad_z = (extended[1:-1, 1:-1, 2:] - extended[1:-1, 1:-1, :-2]) * half_inverse
    return grad_x, grad_y, grad_z


def divergence(extended):
    total = extended[0, 2:, 1:-1, 1:-1] - extended[0, :-2, 1:-1, 1:-1]
    total = total + extended[1, 1:-1, 2:, 1:-1] - extended[1, 1:-1, :-2, 1:-1]
    total = total + extended[2, 1:-1, 1:-1, 2:] - extended[2, 1:-1, 1:-1, :-2]
    return total * half_inverse


def reference(partial_density, moments, shape_functions, sphere_offsets, owned_count):
    coarse = jnp.sum(partial_density, axis=0)
    fine = jnp.pad(coarse, 1)
    for direction in range(3):
        fine = refine(fine, direction)
    fine_x, fine_y, fine_z = fine.shape
    slab_rows = 2 * CX
    slot_total = moments.shape[1]
    slot_index = jnp.arange(slot_total).astype(jnp.int32)
    owner = slot_index // SLOTS
    live = ((slot_index % SLOTS) < owned_count[owner]).astype(jnp.float32)
    weights = moments.astype(jnp.float32) * live[None, :]
    blocks = jnp.einsum("ls,slk->sk", weights, shape_functions.astype(jnp.float32))
    position = jnp.arange(BLOCK).astype(jnp.int32)
    along_x = position // (SBY * SBZ)
    along_y = (position // SBZ) % SBY
    along_z = position % SBZ
    rows = (owner * slab_rows + sphere_offsets[0])[:, None] + along_x[None, :]
    cols = sphere_offsets[1][:, None] + along_y[None, :]
    depth = sphere_offsets[2][:, None] + along_z[None, :]
    flat_index = (rows * fine_y + cols) * fine_z + depth
    spheres = jnp.zeros((fine_x * fine_y * fine_z,), jnp.float32).at[flat_index.reshape(-1)].add(blocks.reshape(-1))
    density = fine + spheres.reshape(fine_x, fine_y, fine_z)
    grad_x, grad_y, grad_z = gradients(jnp.pad(density, 1))
    sigma = grad_x * grad_x + grad_y * grad_y + grad_z * grad_z
    by_density, by_sigma = exchange_parts(density, sigma)
    flux = jnp.stack([2.0 * by_sigma * grad_x, 2.0 * by_sigma * grad_y, 2.0 * by_sigma * grad_z])
    fine_potential = by_density - divergence(jnp.pad(flux, ((0, 0), (1, 1), (1, 1), (1, 1))))
    potential = jnp.pad(fine_potential, 1)
    for direction in range(3):
        potential = restrict(potential, direction)
    return potential
```

```python
import functools

import jax
import jax.numpy as jnp
from jax import lax
from jax.experimental import pallas as pl
from jax.experimental.pallas import tpu as pltpu
from jax.sharding import PartitionSpec as P

SBX = 12
SBY = 24
SBZ = 24
GROUP = 384
LINES = 16
PAD = 32
HALO = 3

kappa_pbe = 0.804
mu_pbe = 0.2195
exchange_prefactor = -0.75 * (3.0 / 3.141592653589793) ** (1.0 / 3.0)
gradient_scale = 4.0 * (3.0 * 3.141592653589793**2) ** (2.0 / 3.0)
half_inverse = 0.5 / 0.2

f32 = jnp.float32
bf16 = jnp.bfloat16
MESH = pl.DeviceIdType.MESH


def iota(shape, dim):
    return lax.broadcasted_iota(jnp.int32, shape, dim)


def split(x):
    high = x.astype(bf16).astype(f32)
    return high, x - high


def weights(shape, terms):
    total = jnp.zeros(shape, f32)
    for mask, value in terms:
        total = jnp.where(mask, value, total)
    return total


def sources(fx):
    return (
        (0, 18, SBX, 0, 0, fx + HALO, 0),
        (0, 18, SBX, 0, -HALO, SBX - 1 + HALO, -1),
        (5760, 3, 2, 10, -HALO, 2, -2),
        (0, 5, 3, 0, fx, HALO, 1),
    )


def kernel(
    G, N, Q,
    part, mom, shp, off, cnt,
    out,
    win, recv, cext, v0, v1, v2, v3, offs, p0, p1, p2, p3, dens, flux, pot, zc,
    win_sem, ps_sem, pr_sem, cs_sem, cr_sem, vs_sem, vr_sem, os_sem, or_sem, gs_sem, gr_sem,
):
    _, cx, cy, cz = part.shape
    fx, fy, fz = 2 * cx, 2 * cy, 2 * cz
    yc = cy // Q
    yw = yc + 16
    fw = 2 * yc + 16
    j = lax.axis_index("band")
    d = lax.axis_index("dom")
    q = lax.rem(j, Q)

    def window_start(chunk):
        start = jnp.minimum(jnp.maximum(chunk * yc - 8, 0), cy - yw)
        return pl.multiple_of(start, 8)

    wstart = window_start(q)
    own = pltpu.make_async_copy(part.at[0, :, pl.ds(wstart, yw), :], win, win_sem)
    own.start()

    barrier = pltpu.get_barrier_semaphore()
    for k in range(1, G):
        pl.semaphore_signal(barrier, inc=1, device_id=(lax.rem(j + k, G), d), device_id_type=MESH)
    inside = {}
    for step in (-2, -1, 1, 2):
        inside[step] = jnp.logical_and(d + step >= 0, d + step < N)

        @pl.when(inside[step])
        def _(step=step):
            pl.semaphore_signal(barrier, inc=1, device_id=(j, d + step), device_id_type=MESH)

    count = G - 1
    for step in (-2, -1, 1, 2):
        count = count + jnp.where(inside[step], 1, 0)
    pl.semaphore_wait(barrier, count)

    part_copies = []
    for k in range(1, G):
        peer = lax.rem(j + k, G)
        copy = pltpu.make_async_remote_copy(
            src_ref=part.at[0, :, pl.ds(window_start(lax.rem(peer, Q)), yw), :],
            dst_ref=recv.at[k - 1],
            send_sem=ps_sem.at[k - 1],
            recv_sem=pr_sem.at[k - 1],
            device_id=(peer, d),
            device_id_type=MESH,
        )
        copy.start()
        part_copies.append(copy)

    slots = shp.shape[0]
    moments = mom[...].astype(f32)
    moments = jnp.where(iota(moments.shape, 1) < cnt[0], moments, 0.0)
    for s in range(slots):
        v0[s : s + 1, :] = jnp.sum(shp[s].astype(f32) * moments[:, s : s + 1], axis=0, keepdims=True)

    plan = sources(fx)
    blocks = (v0, v1, v2, v3)
    placed = (p0, p1, p2, p3)
    block_copies = [None]
    offset_copies = [None]
    for k in (1, 2, 3):
        lane, groups = plan[k][0], plan[k][1]
        step = -plan[k][6]
        block_copies.append(pltpu.make_async_remote_copy(
            src_ref=v0.at[:, pl.ds(lane, groups * GROUP)],
            dst_ref=blocks[k],
            send_sem=vs_sem.at[k], recv_sem=vr_sem.at[k],
            device_id=(j, d + step), device_id_type=MESH,
        ))
        offset_copies.append(pltpu.make_async_remote_copy(
            src_ref=off,
            dst_ref=offs.at[k],
            send_sem=os_sem.at[k], recv_sem=or_sem.at[k],
            device_id=(j, d + step), device_id_type=MESH,
        ))

        @pl.when(inside[step])
        def _(k=k):
            offset_copies[k].start()
            block_copies[k].start()

    line_mask = ((iota((LINES, GROUP), 1) * 2731) >> 16) == iota((LINES, GROUP), 0)
    k_rows = iota((GROUP, fz), 0)
    depth_in_line = iota((GROUP, fz), 1) - (k_rows - ((k_rows * 2731) >> 16) * SBZ)
    ystart = 2 * yc * q - 8

    def offset_of(k, row, s):
        return off[row, s] if k == 0 else offs[k, row, s]

    def unfold(k):
        _, groups, na, _, _, _, _ = plan[k]

        def one(s, carry):
            pick = jnp.where(depth_in_line == offset_of(k, 2, s), 1.0, 0.0).astype(bf16)
            pick = jnp.concatenate([pick, pick], axis=0)
            pieces = []
            for g in range(groups):
                line = blocks[k][pl.ds(s, 1), g * GROUP : (g + 1) * GROUP]
                high, low = split(line)
                wide = jnp.concatenate([
                    jnp.where(line_mask, jnp.broadcast_to(high, (LINES, GROUP)), 0.0),
                    jnp.where(line_mask, jnp.broadcast_to(low, (LINES, GROUP)), 0.0),
                ], axis=1)
                pieces.append(wide.astype(bf16))
            spread = jnp.dot(jnp.concatenate(pieces, axis=0), pick, preferred_element_type=f32)
            spread = spread[: na * SBY].reshape(na, SBY, fz)
            high, low = split(spread)
            gap = jnp.zeros((na, PAD - SBY, fz), f32)
            placed[k][s] = jnp.concatenate([high, gap, low, gap], axis=1).astype(bf16)
            return carry

        lax.fori_loop(0, slots, one, 0)

    def place(k, first):
        _, _, na, a0, x0, rows, slab = plan[k]
        width = slots * 2 * PAD
        lane = iota((1, width), 1)
        row_lane = jnp.zeros((1, width), jnp.int32)
        col_lane = jnp.zeros((1, width), jnp.int32)
        for s in range(slots):
            at = (lane >> 6) == s
            row_lane = jnp.where(at, offset_of(k, 0, s), row_lane)
            col_lane = jnp.where(at, offset_of(k, 1, s), col_lane)
        line = lane & (PAD - 1)
        target = jnp.where(line < SBY, col_lane + line, -1000)
        cols = jnp.where(iota((fw, width), 0) + ystart == target, 1.0, 0.0)

        def one(i, carry):
            x = x0 + i
            local = x - slab * fx - a0
            at = local - row_lane
            valid = jnp.logical_and(at >= 0, at < na)
            left = jnp.where(valid, cols, 0.0).astype(bf16)
            pieces = []
            for s in range(slots):
                index = jnp.clip(local - offset_of(k, 0, s), 0, na - 1)
                pieces.append(placed[k][s, index])
            right = jnp.concatenate(pieces, axis=0)
            value = jnp.dot(left, right, preferred_element_type=f32)
            if first:
                dens[x + HALO] = value
            else:
                dens[x + HALO] = dens[x + HALO] + value
            return carry

        lax.fori_loop(0, rows, one, 0)

    dens[0:HALO] = jnp.zeros((HALO, fw, fz), f32)
    unfold(0)
    place(0, True)

    own.wait()
    for copy in part_copies:
        copy.wait_recv()
    total = win[...]
    for k in range(1, G):
        total = total + recv[k - 1]
    cext[2 : cx + 2] = total
    rise = pltpu.make_async_remote_copy(
        src_ref=cext.at[pl.ds(cx, 2)], dst_ref=cext.at[pl.ds(0, 2)],
        send_sem=cs_sem.at[0], recv_sem=cr_sem.at[0],
        device_id=(j, d + 1), device_id_type=MESH,
    )
    sink = pltpu.make_async_remote_copy(
        src_ref=cext.at[pl.ds(2, 2)], dst_ref=cext.at[pl.ds(cx + 2, 2)],
        send_sem=cs_sem.at[1], recv_sem=cr_sem.at[1],
        device_id=(j, d - 1), device_id_type=MESH,
    )

    @pl.when(inside[1])
    def _():
        rise.start()

    @pl.when(inside[-1])
    def _():
        sink.start()

    for k in (3, 2, 1):

        @pl.when(inside[plan[k][6]])
        def _(k=k):
            offset_copies[k].wait_recv()
            block_copies[k].wait_recv()
            unfold(k)
            place(k, False)

    @pl.when(inside[-1])
    def _():
        rise.wait_recv()

    @pl.when(jnp.logical_not(inside[-1]))
    def _():
        cext[0:2] = jnp.zeros((2, yw, cz), f32)

    @pl.when(inside[1])
    def _():
        sink.wait_recv()

    @pl.when(jnp.logical_not(inside[1]))
    def _():
        cext[cx + 2 : cx + 4] = jnp.zeros((2, yw, cz), f32)

    rows = []
    for x in range(-HALO, fx + HALO):
        middle = (x >> 1) + 2
        other = middle + (1 if x % 2 else -1)
        rows.append(0.75 * cext[middle] + 0.25 * cext[other])
    count_x = fx + 2 * HALO
    stacked = jnp.concatenate(rows, axis=0)
    zi, zo = iota((cz, fz), 0), iota((cz, fz), 1)
    zm = zo >> 1
    zn = zm + ((zo & 1) << 1) - 1
    refine_z = weights((cz, fz), ((zi == zm, 0.75), (zi == zn, 0.25))).astype(bf16)
    refine_z = jnp.concatenate([refine_z, refine_z], axis=0)
    high, low = split(stacked)
    zc[...] = jnp.dot(
        jnp.concatenate([high, low], axis=1).astype(bf16), refine_z, preferred_element_type=f32
    ).reshape(count_x, yw, fz)
    yo = iota((fw, yw), 0) + ystart
    yi = iota((fw, yw), 1) + wstart
    ym = yo >> 1
    yn = ym + ((yo & 1) << 1) - 1
    grid = jnp.logical_and(yo >= 0, yo < fy)
    refine_y = weights(
        (fw, yw), ((jnp.logical_and(grid, yi == ym), 0.75), (jnp.logical_and(grid, yi == yn), 0.25))
    )
    refine_y = jnp.concatenate([refine_y, refine_y], axis=1).astype(bf16)

    def in_grid(x):
        g = d * fx + x
        return jnp.where(jnp.logical_and(g >= 0, g < N * fx), 1.0, 0.0).astype(f32)

    def refine_row(i, carry):
        high, low = split(zc[i])
        right = jnp.concatenate([high, low], axis=0).astype(bf16)
        value = jnp.dot(refine_y, right, preferred_element_type=f32)
        dens[i] = (dens[i] + value) * in_grid(i - HALO)
        return carry

    lax.fori_loop(0, count_x, refine_row, 0)

    lanes = iota((fw, fz), 1)
    first_lane, last_lane = lanes == 0, lanes == fz - 1

    def diff_z(f):
        after = jnp.where(last_lane, 0.0, pltpu.roll(f, fz - 1, 1))
        before = jnp.where(first_lane, 0.0, pltpu.roll(f, 1, 1))
        return (after - before) * half_inverse

    def diff_y(f):
        return (pltpu.roll(f, fw - 1, 0) - pltpu.roll(f, 1, 0)) * half_inverse

    def exchange_row(i, carry):
        n = dens[i + 1]
        gx = (dens[i + 2] - dens[i]) * half_inverse
        gy = diff_y(n)
        gz = diff_z(n)
        sigma = gx * gx + gy * gy + gz * gz
        live = n > 0.0
        log_n = jnp.log(jnp.where(live, n, 1.0))
        cube_root = jnp.exp(log_n * (1.0 / 3.0))
        inv_ft = jnp.exp(log_n * (-4.0 / 3.0))
        reduced = sigma * (inv_ft * inv_ft) * (1.0 / gradient_scale)
        inv_d = 1.0 / (1.0 + (mu_pbe / kappa_pbe) * reduced)
        slope = mu_pbe * inv_d * inv_d
        by_density = (exchange_prefactor * cube_root) * (
            (4.0 / 3.0) * (1.0 + kappa_pbe - kappa_pbe * inv_d) - (8.0 / 3.0) * reduced * slope
        )
        twice = jnp.where(live, (2.0 * exchange_prefactor / gradient_scale) * slope * inv_ft, 0.0)
        flux[i] = twice * gx
        pot[i] = by_density - (diff_y(twice * gy) + diff_z(twice * gz))
        return carry

    lax.fori_loop(0, fx + 4, exchange_row, 0)

    ro, ri = iota((yc, fw), 0), iota((yc, fw), 1)
    at = ri - 8 - 2 * ro
    grid = jnp.logical_and(ri + ystart >= 0, ri + ystart < fy)
    inner = jnp.logical_and(grid, jnp.logical_or(at == 0, at == 1))
    outer = jnp.logical_and(grid, jnp.logical_or(at == -1, at == 2))
    restrict_y = weights((yc, fw), ((inner, 0.375), (outer, 0.125)))
    restrict_y = jnp.concatenate([restrict_y, restrict_y], axis=1).astype(bf16)
    at = iota((fz, cz), 0) - 2 * iota((fz, cz), 1)
    inner = jnp.logical_or(at == 0, at == 1)
    outer = jnp.logical_or(at == -1, at == 2)
    restrict_z = weights((fz, cz), ((inner, 0.375), (outer, 0.125))).astype(bf16)
    restrict_z = jnp.concatenate([restrict_z, restrict_z], axis=0)

    def full(x):
        return (pot[x + 2] - (flux[x + 3] - flux[x + 1]) * half_inverse) * in_grid(x)

    ymine = pl.multiple_of(q * yc, 8)

    def restrict_row(i, carry):
        x = 2 * i
        mixed = 0.125 * (full(x - 1) + full(x + 2)) + 0.375 * (full(x) + full(x + 1))
        high, low = split(mixed)
        narrow = jnp.dot(
            restrict_y, jnp.concatenate([high, low], axis=0).astype(bf16), preferred_element_type=f32
        )
        high, low = split(narrow)
        out[i, pl.ds(ymine, yc), :] = jnp.dot(
            jnp.concatenate([high, low], axis=1).astype(bf16), restrict_z, preferred_element_type=f32
        )
        return carry

    lax.fori_loop(0, cx, restrict_row, 0)

    base = j - q
    gather = []
    for k in range(1, Q):
        copy = pltpu.make_async_remote_copy(
            src_ref=out.at[:, pl.ds(ymine, yc), :],
            dst_ref=out.at[:, pl.ds(ymine, yc), :],
            send_sem=gs_sem.at[k - 1], recv_sem=gr_sem.at[k - 1],
            device_id=(base + lax.rem(q + k, Q), d), device_id_type=MESH,
        )
        copy.start()
        gather.append(copy)
    for copy in part_copies:
        copy.wait_send()
    for k in (1, 2, 3):

        @pl.when(inside[-plan[k][6]])
        def _(k=k):
            offset_copies[k].wait_send()
            block_copies[k].wait_send()

    @pl.when(inside[1])
    def _():
        rise.wait_send()

    @pl.when(inside[-1])
    def _():
        sink.wait_send()

    for copy in gather:
        copy.wait()


def body(G, N, Q, partial_density, moments, shape_functions, sphere_offsets, owned_count):
    _, cx, cy, cz = partial_density.shape
    slots, _, block = shape_functions.shape
    fx, fz = 2 * cx, 2 * cz
    yc = cy // Q
    yw, fw = yc + 16, 2 * yc + 16
    plan = sources(fx)
    vmem = pl.BlockSpec(memory_space=pltpu.VMEM)
    smem = pl.BlockSpec(memory_space=pltpu.SMEM)
    return pl.pallas_call(
        functools.partial(kernel, G, N, Q),
        out_shape=jax.ShapeDtypeStruct((cx, cy, cz), f32),
        in_specs=[pl.BlockSpec(memory_space=pl.ANY), vmem, vmem, smem, smem],
        out_specs=vmem,
        scratch_shapes=[
            pltpu.VMEM((cx, yw, cz), f32),
            pltpu.VMEM((G - 1, cx, yw, cz), f32),
            pltpu.VMEM((cx + 4, yw, cz), f32),
        ]
        + [pltpu.VMEM((slots, p[1] * GROUP), f32) for p in plan]
        + [pltpu.SMEM((4,) + sphere_offsets.shape, jnp.int32)]
        + [pltpu.VMEM((slots, p[2], 2 * PAD, fz), bf16) for p in plan]
        + [
            pltpu.VMEM((fx + 2 * HALO, fw, fz), f32),
            pltpu.VMEM((fx + 4, fw, fz), f32),
            pltpu.VMEM((fx + 4, fw, fz), f32),
            pltpu.VMEM((fx + 2 * HALO, yw, fz), f32),
            pltpu.SemaphoreType.DMA(()),
            pltpu.SemaphoreType.DMA((G - 1,)),
            pltpu.SemaphoreType.DMA((G - 1,)),
            pltpu.SemaphoreType.DMA((2,)),
            pltpu.SemaphoreType.DMA((2,)),
            pltpu.SemaphoreType.DMA((4,)),
            pltpu.SemaphoreType.DMA((4,)),
            pltpu.SemaphoreType.DMA((4,)),
            pltpu.SemaphoreType.DMA((4,)),
            pltpu.SemaphoreType.DMA((Q - 1,)),
            pltpu.SemaphoreType.DMA((Q - 1,)),
        ],
        compiler_params=pltpu.CompilerParams(
            collective_id=0, has_side_effects=True, vmem_limit_bytes=48 * 1024 * 1024
        ),
    )(partial_density, moments, shape_functions, sphere_offsets, owned_count)


def solution(mesh):
    G, N = mesh.shape["band"], mesh.shape["dom"]

    def run(partial_density, *rest):
        cy = partial_density.shape[2]
        Q = max(c for c in range(1, G + 1) if G % c == 0 and cy % (8 * c) == 0)
        return jax.shard_map(
            functools.partial(body, G, N, Q),
            mesh=mesh,
            in_specs=(
                P("band", "dom", None, None),
                P(None, "dom"),
                P("dom", None, None),
                P(None, "dom"),
                P("dom"),
            ),
            out_specs=P("dom", None, None),
            check_vma=False,
        )(partial_density, *rest)

    return run
```

```python
import functools

import jax
import jax.numpy as jnp
from jax import lax
from jax.experimental import pallas as pl
from jax.experimental.pallas import tpu as pltpu
from jax.sharding import PartitionSpec as P

SBX = 12
SBY = 24
SBZ = 24
GROUP = 384
LINES = 16
PAD = 32
HALO = 3

kappa_pbe = 0.804
mu_pbe = 0.2195
exchange_prefactor = -0.75 * (3.0 / 3.141592653589793) ** (1.0 / 3.0)
gradient_scale = 4.0 * (3.0 * 3.141592653589793**2) ** (2.0 / 3.0)
half_inverse = 0.5 / 0.2

f32 = jnp.float32
bf16 = jnp.bfloat16
MESH = pl.DeviceIdType.MESH


def iota(shape, dim):
    return lax.broadcasted_iota(jnp.int32, shape, dim)


def split(x):
    high = x.astype(bf16).astype(f32)
    return high, x - high


def weights(shape, terms):
    total = jnp.zeros(shape, f32)
    for mask, value in terms:
        total = jnp.where(mask, value, total)
    return total


def sources(fx):
    return (
        (0, 18, SBX, 0, 0, fx + HALO, 0),
        (0, 18, SBX, 0, -HALO, SBX - 1 + HALO, -1),
        (5760, 3, 2, 10, -HALO, 2, -2),
        (0, 5, 3, 0, fx, HALO, 1),
    )


def kernel(
    G, N, Q,
    part, mom, shp_hbm, off, cnt,
    out,
    shp, win, recv, cext, v0, v1, v2, v3, vh, vl, offs, p0, p1, p2, p3, dens, flux, pot, zc,
    shp_sem, win_sem, ps_sem, pr_sem, cs_sem, cr_sem, vs_sem, vr_sem, os_sem, or_sem, gs_sem, gr_sem,
):
    _, cx, cy, cz = part.shape
    fx, fy, fz = 2 * cx, 2 * cy, 2 * cz
    yc = cy // Q
    yw = yc + 16
    fw = 2 * yc + 8
    j = lax.axis_index("band")
    d = lax.axis_index("dom")
    q = lax.rem(j, Q)

    def window_start(chunk):
        start = jnp.minimum(jnp.maximum(chunk * yc - 8, 0), cy - yw)
        return pl.multiple_of(start, 8)

    wstart = window_start(q)
    own = pltpu.make_async_copy(part.at[0, :, pl.ds(wstart, yw), :], win, win_sem)
    own.start()
    fetch = pltpu.make_async_copy(shp_hbm, shp, shp_sem)
    fetch.start()

    barrier = pltpu.get_barrier_semaphore()
    for k in range(1, G):
        pl.semaphore_signal(barrier, inc=1, device_id=(lax.rem(j + k, G), d), device_id_type=MESH)
    inside = {}
    for step in (-2, -1, 1, 2):
        inside[step] = jnp.logical_and(d + step >= 0, d + step < N)

        @pl.when(inside[step])
        def _(step=step):
            pl.semaphore_signal(barrier, inc=1, device_id=(j, d + step), device_id_type=MESH)

    count = G - 1
    for step in (-2, -1, 1, 2):
        count = count + jnp.where(inside[step], 1, 0)
    pl.semaphore_wait(barrier, count)

    part_copies = []
    for k in range(1, G):
        peer = lax.rem(j + k, G)
        copy = pltpu.make_async_remote_copy(
            src_ref=part.at[0, :, pl.ds(window_start(lax.rem(peer, Q)), yw), :],
            dst_ref=recv.at[k - 1],
            send_sem=ps_sem.at[k - 1],
            recv_sem=pr_sem.at[k - 1],
            device_id=(peer, d),
            device_id_type=MESH,
        )
        copy.start()
        part_copies.append(copy)

    channels, slots, _ = shp.shape
    moments = mom[...].astype(f32)
    moments = jnp.where(iota(moments.shape, 0) < cnt[0], moments, 0.0)
    scales = [jnp.broadcast_to(moments[:, l : l + 1], (slots, GROUP)) for l in range(channels)]
    fetch.wait()
    for g in range(v0.shape[1] // GROUP):
        at = slice(g * GROUP, (g + 1) * GROUP)
        total = shp[0, :, at].astype(f32) * scales[0]
        for l in range(1, channels):
            total = total + shp[l, :, at].astype(f32) * scales[l]
        v0[:, at] = total

    plan = sources(fx)
    blocks = (v0, v1, v2, v3)
    placed = (p0, p1, p2, p3)
    block_copies = [None]
    offset_copies = [None]
    for k in (1, 2, 3):
        lane, groups = plan[k][0], plan[k][1]
        step = -plan[k][6]
        block_copies.append(pltpu.make_async_remote_copy(
            src_ref=v0.at[:, pl.ds(lane, groups * GROUP)],
            dst_ref=blocks[k],
            send_sem=vs_sem.at[k], recv_sem=vr_sem.at[k],
            device_id=(j, d + step), device_id_type=MESH,
        ))
        offset_copies.append(pltpu.make_async_remote_copy(
            src_ref=off,
            dst_ref=offs.at[k],
            send_sem=os_sem.at[k], recv_sem=or_sem.at[k],
            device_id=(j, d + step), device_id_type=MESH,
        ))

        @pl.when(inside[step])
        def _(k=k):
            offset_copies[k].start()
            block_copies[k].start()

    line_mask = ((iota((LINES, GROUP), 1) * 2731) >> 16) == iota((LINES, GROUP), 0)
    k_rows = iota((GROUP, fz), 0)
    depth_in_line = iota((GROUP, fz), 1) - (k_rows - ((k_rows * 2731) >> 16) * SBZ)
    ystart = 2 * yc * q - 4

    def offset_of(k, row, s):
        return off[row, s] if k == 0 else offs[k, row, s]

    def unfold(k):
        _, groups, na, _, _, _, _ = plan[k]
        width = groups * GROUP
        high, low = split(blocks[k][...])
        vh[:, :width] = high
        vl[:, :width] = low

        def one(s, carry):
            pick = jnp.where(depth_in_line == offset_of(k, 2, s), 1.0, 0.0).astype(bf16)
            pick = jnp.concatenate([pick, pick], axis=0)
            pieces = []
            for g in range(groups):
                high = vh[pl.ds(s, 1), g * GROUP : (g + 1) * GROUP]
                low = vl[pl.ds(s, 1), g * GROUP : (g + 1) * GROUP]
                wide = jnp.concatenate([
                    jnp.where(line_mask, jnp.broadcast_to(high, (LINES, GROUP)), 0.0),
                    jnp.where(line_mask, jnp.broadcast_to(low, (LINES, GROUP)), 0.0),
                ], axis=1)
                pieces.append(wide.astype(bf16))
            spread = jnp.dot(jnp.concatenate(pieces, axis=0), pick, preferred_element_type=f32)
            spread = spread[: na * SBY].reshape(na, SBY, fz)
            high, low = split(spread)
            gap = jnp.zeros((na, PAD - SBY, fz), f32)
            placed[k][s] = jnp.concatenate([high, gap, low, gap], axis=1).astype(bf16)
            return carry

        lax.fori_loop(0, slots, one, 0, unroll=2)

    def place(k, first):
        _, _, na, a0, x0, rows, slab = plan[k]
        width = slots * 2 * PAD
        lane = iota((1, width), 1)
        row_lane = jnp.zeros((1, width), jnp.int32)
        col_lane = jnp.zeros((1, width), jnp.int32)
        for s in range(slots):
            at = (lane >> 6) == s
            row_lane = jnp.where(at, offset_of(k, 0, s), row_lane)
            col_lane = jnp.where(at, offset_of(k, 1, s), col_lane)
        line = lane & (PAD - 1)
        target = jnp.where(line < SBY, col_lane + line, -1000)
        cols = jnp.where(iota((fw, width), 0) + ystart == target, 1.0, 0.0)

        def one(i, carry):
            x = x0 + i
            local = x - slab * fx - a0
            at = local - row_lane
            valid = jnp.logical_and(at >= 0, at < na)
            left = jnp.where(valid, cols, 0.0).astype(bf16)
            pieces = []
            for s in range(slots):
                index = jnp.clip(local - offset_of(k, 0, s), 0, na - 1)
                pieces.append(placed[k][s, index])
            right = jnp.concatenate(pieces, axis=0)
            value = jnp.dot(left, right, preferred_element_type=f32)
            if first:
                dens[x + HALO] = value
            else:
                dens[x + HALO] = dens[x + HALO] + value
            return carry

        lax.fori_loop(0, rows, one, 0, unroll=2 if rows % 2 == 0 else 3)

    dens[0:HALO] = jnp.zeros((HALO, fw, fz), f32)
    unfold(0)
    place(0, True)

    own.wait()
    for copy in part_copies:
        copy.wait_recv()
    total = win[...]
    for k in range(1, G):
        total = total + recv[k - 1]
    cext[2 : cx + 2] = total
    rise = pltpu.make_async_remote_copy(
        src_ref=cext.at[pl.ds(cx, 2)], dst_ref=cext.at[pl.ds(0, 2)],
        send_sem=cs_sem.at[0], recv_sem=cr_sem.at[0],
        device_id=(j, d + 1), device_id_type=MESH,
    )
    sink = pltpu.make_async_remote_copy(
        src_ref=cext.at[pl.ds(2, 2)], dst_ref=cext.at[pl.ds(cx + 2, 2)],
        send_sem=cs_sem.at[1], recv_sem=cr_sem.at[1],
        device_id=(j, d - 1), device_id_type=MESH,
    )

    @pl.when(inside[1])
    def _():
        rise.start()

    @pl.when(inside[-1])
    def _():
        sink.start()

    for k in (3, 2, 1):

        @pl.when(inside[plan[k][6]])
        def _(k=k):
            offset_copies[k].wait_recv()
            block_copies[k].wait_recv()
            unfold(k)
            place(k, False)

    @pl.when(inside[-1])
    def _():
        rise.wait_recv()

    @pl.when(jnp.logical_not(inside[-1]))
    def _():
        cext[0:2] = jnp.zeros((2, yw, cz), f32)

    @pl.when(inside[1])
    def _():
        sink.wait_recv()

    @pl.when(jnp.logical_not(inside[1]))
    def _():
        cext[cx + 2 : cx + 4] = jnp.zeros((2, yw, cz), f32)

    rows = []
    for x in range(-HALO, fx + HALO):
        middle = (x >> 1) + 2
        other = middle + (1 if x % 2 else -1)
        rows.append(0.75 * cext[middle] + 0.25 * cext[other])
    count_x = fx + 2 * HALO
    stacked = jnp.concatenate(rows, axis=0)
    zi, zo = iota((cz, fz), 0), iota((cz, fz), 1)
    zm = zo >> 1
    zn = zm + ((zo & 1) << 1) - 1
    refine_z = weights((cz, fz), ((zi == zm, 0.75), (zi == zn, 0.25))).astype(bf16)
    refine_z = jnp.concatenate([refine_z, refine_z], axis=0)
    high, low = split(stacked)
    zc[...] = jnp.dot(
        jnp.concatenate([high, low], axis=1).astype(bf16), refine_z, preferred_element_type=f32
    ).reshape(count_x, yw, fz)
    yo = iota((fw, yw), 0) + ystart
    yi = iota((fw, yw), 1) + wstart
    ym = yo >> 1
    yn = ym + ((yo & 1) << 1) - 1
    grid = jnp.logical_and(yo >= 0, yo < fy)
    refine_y = weights(
        (fw, yw), ((jnp.logical_and(grid, yi == ym), 0.75), (jnp.logical_and(grid, yi == yn), 0.25))
    )
    refine_y = jnp.concatenate([refine_y, refine_y], axis=1).astype(bf16)

    def in_grid(x):
        g = d * fx + x
        return jnp.where(jnp.logical_and(g >= 0, g < N * fx), 1.0, 0.0).astype(f32)

    def refine_row(i, carry):
        high, low = split(zc[i])
        right = jnp.concatenate([high, low], axis=0).astype(bf16)
        value = jnp.dot(refine_y, right, preferred_element_type=f32)
        dens[i] = (dens[i] + value) * in_grid(i - HALO)
        return carry

    lax.fori_loop(0, count_x, refine_row, 0, unroll=3)

    lanes = iota((fw, fz), 1)
    first_lane, last_lane = lanes == 0, lanes == fz - 1

    def diff_z(f):
        after = jnp.where(last_lane, 0.0, pltpu.roll(f, fz - 1, 1))
        before = jnp.where(first_lane, 0.0, pltpu.roll(f, 1, 1))
        return (after - before) * half_inverse

    def diff_y(f):
        return (pltpu.roll(f, fw - 1, 0) - pltpu.roll(f, 1, 0)) * half_inverse

    def exchange_row(i, carry):
        n = dens[i + 1]
        gx = (dens[i + 2] - dens[i]) * half_inverse
        gy = diff_y(n)
        gz = diff_z(n)
        sigma = gx * gx + gy * gy + gz * gz
        live = n > 0.0
        log_n = jnp.log(jnp.where(live, n, 1.0))
        cube_root = jnp.exp(log_n * (1.0 / 3.0))
        inv_ft = jnp.exp(log_n * (-4.0 / 3.0))
        reduced = sigma * (inv_ft * inv_ft) * (1.0 / gradient_scale)
        inv_d = 1.0 / (1.0 + (mu_pbe / kappa_pbe) * reduced)
        slope = mu_pbe * inv_d * inv_d
        by_density = (exchange_prefactor * cube_root) * (
            (4.0 / 3.0) * (1.0 + kappa_pbe - kappa_pbe * inv_d) - (8.0 / 3.0) * reduced * slope
        )
        twice = jnp.where(live, (2.0 * exchange_prefactor / gradient_scale) * slope * inv_ft, 0.0)
        flux[i] = twice * gx
        pot[i] = by_density - (diff_y(twice * gy) + diff_z(twice * gz))
        return carry


    ro, ri = iota((yc, fw), 0), iota((yc, fw), 1)
    at = ri - 4 - 2 * ro
    grid = jnp.logical_and(ri + ystart >= 0, ri + ystart < fy)
    inner = jnp.logical_and(grid, jnp.logical_or(at == 0, at == 1))
    outer = jnp.logical_and(grid, jnp.logical_or(at == -1, at == 2))
    restrict_y = weights((yc, fw), ((inner, 0.375), (outer, 0.125)))
    restrict_y = jnp.concatenate([restrict_y, restrict_y], axis=1).astype(bf16)
    at = iota((fz, cz), 0) - 2 * iota((fz, cz), 1)
    inner = jnp.logical_or(at == 0, at == 1)
    outer = jnp.logical_or(at == -1, at == 2)
    restrict_z = weights((fz, cz), ((inner, 0.375), (outer, 0.125))).astype(bf16)
    restrict_z = jnp.concatenate([restrict_z, restrict_z], axis=0)

    def full(x):
        return (pot[x + 2] - (flux[x + 3] - flux[x + 1]) * half_inverse) * in_grid(x)

    ymine = pl.multiple_of(q * yc, 8)

    def restrict_rows(low_row, high_row):
        pieces = []
        for i in range(low_row, high_row):
            x = 2 * i
            mixed = 0.125 * (full(x - 1) + full(x + 2)) + 0.375 * (full(x) + full(x + 1))
            high, low = split(mixed)
            pieces.append(jnp.dot(
                restrict_y,
                jnp.concatenate([high, low], axis=0).astype(bf16),
                preferred_element_type=f32,
            ))
        high, low = split(jnp.concatenate(pieces, axis=0))
        result = jnp.dot(
            jnp.concatenate([high, low], axis=1).astype(bf16), restrict_z, preferred_element_type=f32
        )
        out[low_row:high_row, pl.ds(ymine, yc), :] = result.reshape(high_row - low_row, yc, cz)

    base = j - q
    half = cx // 2
    gather = []
    done = 0
    for piece, (low_row, high_row) in enumerate(((0, half), (half, cx))):
        lax.fori_loop(done, 2 * high_row + 4, exchange_row, 0)
        done = 2 * high_row + 4
        restrict_rows(low_row, high_row)
        for k in range(1, Q):
            at = (pl.ds(low_row, high_row - low_row), pl.ds(ymine, yc), slice(None))
            copy = pltpu.make_async_remote_copy(
                src_ref=out.at[at],
                dst_ref=out.at[at],
                send_sem=gs_sem.at[piece, k - 1], recv_sem=gr_sem.at[piece, k - 1],
                device_id=(base + lax.rem(q + k, Q), d), device_id_type=MESH,
            )
            copy.start()
            gather.append(copy)
    for copy in part_copies:
        copy.wait_send()
    for k in (1, 2, 3):

        @pl.when(inside[-plan[k][6]])
        def _(k=k):
            offset_copies[k].wait_send()
            block_copies[k].wait_send()

    @pl.when(inside[1])
    def _():
        rise.wait_send()

    @pl.when(inside[-1])
    def _():
        sink.wait_send()

    for copy in gather:
        copy.wait()


def body(G, N, Q, partial_density, moments, shape_functions, sphere_offsets, owned_count):
    _, cx, cy, cz = partial_density.shape
    slots, channels, block = shape_functions.shape
    fx, fz = 2 * cx, 2 * cz
    yc = cy // Q
    yw, fw = yc + 16, 2 * yc + 8
    plan = sources(fx)
    hbm = pl.BlockSpec(memory_space=pl.ANY)
    vmem = pl.BlockSpec(memory_space=pltpu.VMEM)
    smem = pl.BlockSpec(memory_space=pltpu.SMEM)
    return pl.pallas_call(
        functools.partial(kernel, G, N, Q),
        out_shape=jax.ShapeDtypeStruct((cx, cy, cz), f32),
        in_specs=[hbm, vmem, hbm, smem, smem],
        out_specs=vmem,
        scratch_shapes=[
            pltpu.VMEM((channels, slots, block), bf16),
            pltpu.VMEM((cx, yw, cz), f32),
            pltpu.VMEM((G - 1, cx, yw, cz), f32),
            pltpu.VMEM((cx + 4, yw, cz), f32),
        ]
        + [pltpu.VMEM((slots, p[1] * GROUP), f32) for p in plan]
        + [pltpu.VMEM((slots, block), f32)] * 2
        + [pltpu.SMEM((4,) + sphere_offsets.shape, jnp.int32)]
        + [pltpu.VMEM((slots, p[2], 2 * PAD, fz), bf16) for p in plan]
        + [
            pltpu.VMEM((fx + 2 * HALO, fw, fz), f32),
            pltpu.VMEM((fx + 4, fw, fz), f32),
            pltpu.VMEM((fx + 4, fw, fz), f32),
            pltpu.VMEM((fx + 2 * HALO, yw, fz), f32),
            pltpu.SemaphoreType.DMA(()),
            pltpu.SemaphoreType.DMA(()),
            pltpu.SemaphoreType.DMA((G - 1,)),
            pltpu.SemaphoreType.DMA((G - 1,)),
            pltpu.SemaphoreType.DMA((2,)),
            pltpu.SemaphoreType.DMA((2,)),
            pltpu.SemaphoreType.DMA((4,)),
            pltpu.SemaphoreType.DMA((4,)),
            pltpu.SemaphoreType.DMA((4,)),
            pltpu.SemaphoreType.DMA((4,)),
            pltpu.SemaphoreType.DMA((2, Q - 1)),
            pltpu.SemaphoreType.DMA((2, Q - 1)),
        ],
        compiler_params=pltpu.CompilerParams(
            collective_id=0, has_side_effects=True, vmem_limit_bytes=60 * 1024 * 1024
        ),
    )(partial_density, moments.T, shape_functions.transpose(1, 0, 2), sphere_offsets, owned_count)


def solution(mesh):
    G, N = mesh.shape["band"], mesh.shape["dom"]

    def run(partial_density, *rest):
        cy = partial_density.shape[2]
        Q = max(c for c in range(1, G + 1) if G % c == 0 and cy % (8 * c) == 0)
        return jax.shard_map(
            functools.partial(body, G, N, Q),
            mesh=mesh,
            in_specs=(
                P("band", "dom", None, None),
                P(None, "dom"),
                P("dom", None, None),
                P(None, "dom"),
                P("dom"),
            ),
            out_specs=P("dom", None, None),
            check_vma=False,
        )(partial_density, *rest)

    return run
```

```python
import functools

import jax
import jax.numpy as jnp
from jax import lax
from jax.experimental import pallas as pl
from jax.experimental.pallas import tpu as pltpu
from jax.sharding import PartitionSpec as P

SBX = 12
SBY = 24
SBZ = 24
GROUP = 384
LINES = 8
SPAN = 256
SLOT_LANES = 32
HALO = 3

kappa_pbe = 0.804
mu_pbe = 0.2195
exchange_prefactor = -0.75 * (3.0 / 3.141592653589793) ** (1.0 / 3.0)
gradient_scale = 4.0 * (3.0 * 3.141592653589793**2) ** (2.0 / 3.0)
half_inverse = 0.5 / 0.2

f32 = jnp.float32
bf16 = jnp.bfloat16
MESH = pl.DeviceIdType.MESH


def iota(shape, dim):
    return lax.broadcasted_iota(jnp.int32, shape, dim)


def split(x):
    high = x.astype(bf16).astype(f32)
    return high, x - high


def weights(shape, terms):
    total = jnp.zeros(shape, f32)
    for mask, value in terms:
        total = jnp.where(mask, value, total)
    return total


def sources(fx):
    return (
        (0, 18, SBX, 0, 0, fx + HALO, 0),
        (0, 18, SBX, 0, -HALO, SBX - 1 + HALO, -1),
        (5760, 3, 2, 10, -HALO, 2, -2),
        (0, 5, 3, 0, fx, HALO, 1),
    )


def kernel(
    G, N, Q,
    part, mom, shp_hbm, off, cnt,
    out,
    shp, win, recv, cext, v0, v1, v2, v3, vh, vl, offs, unfolder, wide, u0, u1, u2, u3, lined, lined_coarse, dens, flux, pot,
    shp_sem, win_sem, ps_sem, pr_sem, cs_sem, cr_sem, vs_sem, vr_sem, os_sem, or_sem, gs_sem, gr_sem,
):
    _, cx, cy, cz = part.shape
    fx, fy, fz = 2 * cx, 2 * cy, 2 * cz
    yc = cy // Q
    yw = yc + 16
    fw = 2 * yc + 8
    j = lax.axis_index("band")
    d = lax.axis_index("dom")
    q = lax.rem(j, Q)

    def window_start(chunk):
        start = jnp.minimum(jnp.maximum(chunk * yc - 8, 0), cy - yw)
        return pl.multiple_of(start, 8)

    wstart = window_start(q)
    own = pltpu.make_async_copy(part.at[0, :, pl.ds(wstart, yw), :], win, win_sem)
    own.start()
    fetch = pltpu.make_async_copy(shp_hbm, shp, shp_sem)
    fetch.start()

    slots = shp.shape[1]
    k_rows, k_lanes = iota((SPAN, SPAN), 0), iota((SPAN, SPAN), 1)
    for h in range(2):
        k_rows_h = k_rows + 128 * h
        shift = k_lanes - (k_rows_h - ((k_rows_h * 2731) >> 16) * SBZ)
        for s in range(slots):
            unfolder[h, s] = jnp.where(shift == SLOT_LANES * s, 1.0, 0.0).astype(bf16)

    barrier = pltpu.get_barrier_semaphore()
    for k in range(1, G):
        pl.semaphore_signal(barrier, inc=1, device_id=(lax.rem(j + k, G), d), device_id_type=MESH)
    inside = {}
    for step in (-2, -1, 1, 2):
        inside[step] = jnp.logical_and(d + step >= 0, d + step < N)

        @pl.when(inside[step])
        def _(step=step):
            pl.semaphore_signal(barrier, inc=1, device_id=(j, d + step), device_id_type=MESH)

    count = G - 1
    for step in (-2, -1, 1, 2):
        count = count + jnp.where(inside[step], 1, 0)
    pl.semaphore_wait(barrier, count)

    part_copies = []
    for k in range(1, G):
        peer = lax.rem(j + k, G)
        copy = pltpu.make_async_remote_copy(
            src_ref=part.at[0, :, pl.ds(window_start(lax.rem(peer, Q)), yw), :],
            dst_ref=recv.at[k - 1],
            send_sem=ps_sem.at[k - 1],
            recv_sem=pr_sem.at[k - 1],
            device_id=(peer, d),
            device_id_type=MESH,
        )
        copy.start()
        part_copies.append(copy)

    channels, slots, _ = shp.shape
    moments = mom[...].astype(f32)
    moments = jnp.where(iota(moments.shape, 0) < cnt[0], moments, 0.0)
    scales = [jnp.broadcast_to(moments[:, l : l + 1], (slots, GROUP)) for l in range(channels)]
    fetch.wait()
    for g in range(v0.shape[1] // GROUP):
        at = slice(g * GROUP, (g + 1) * GROUP)
        total = shp[0, :, at].astype(f32) * scales[0]
        for l in range(1, channels):
            total = total + shp[l, :, at].astype(f32) * scales[l]
        v0[:, at] = total

    plan = sources(fx)
    blocks = (v0, v1, v2, v3)
    folded = (u0, u1, u2, u3)
    block_copies = [None]
    offset_copies = [None]
    for k in (1, 2, 3):
        lane, groups = plan[k][0], plan[k][1]
        step = -plan[k][6]
        block_copies.append(pltpu.make_async_remote_copy(
            src_ref=v0.at[:, pl.ds(lane, groups * GROUP)],
            dst_ref=blocks[k],
            send_sem=vs_sem.at[k], recv_sem=vr_sem.at[k],
            device_id=(j, d + step), device_id_type=MESH,
        ))
        offset_copies.append(pltpu.make_async_remote_copy(
            src_ref=off,
            dst_ref=offs.at[k],
            send_sem=os_sem.at[k], recv_sem=or_sem.at[k],
            device_id=(j, d + step), device_id_type=MESH,
        ))

        @pl.when(inside[step])
        def _(k=k):
            offset_copies[k].start()
            block_copies[k].start()

    line_masks = []
    for h in range(2):
        lane = iota((LINES, SPAN), 1) + 128 * h
        line_masks.append(((lane * 2731) >> 16) == iota((LINES, SPAN), 0) + LINES * h)
    ystart = 2 * yc * q - 4

    def offset_of(k, row, s):
        return off[row, s] if k == 0 else offs[k, row, s]

    def unfold(which):
        starts = []
        total = 0
        for k in which:
            starts.append(total)
            width = plan[k][1] * GROUP
            high, low = split(blocks[k][...])
            vh[:, total : total + width] = high
            vl[:, total : total + width] = low
            total += width
        groups = total // GROUP

        def one(s, carry):
            for h in range(2):
                for t, source in enumerate((vh, vl)):
                    pieces = []
                    for g in range(groups):
                        at = g * GROUP + 128 * h
                        line = source[pl.ds(s, 1), at : at + SPAN]
                        pieces.append(
                            jnp.where(line_masks[h], jnp.broadcast_to(line, (LINES, SPAN)), 0.0)
                        )
                    lane = pl.multiple_of(s * (2 * SPAN) + t * SPAN, SPAN)
                    wide[h, : groups * LINES, pl.ds(lane, SPAN)] = jnp.concatenate(
                        pieces, axis=0
                    ).astype(bf16)
            return carry

        lax.fori_loop(0, slots, one, 0, unroll=2)
        halves = []
        for h in range(2):
            right = []
            for s in range(slots):
                right += [unfolder[h, s]] * 2
            value = jnp.dot(
                wide[h, : groups * LINES, :], jnp.concatenate(right, axis=0),
                preferred_element_type=f32,
            )
            halves.append(value.reshape(groups, LINES, SPAN))
        lines = jnp.stack(halves, axis=1).reshape(groups * 2 * LINES, SPAN)
        for k, start in zip(which, starts):
            na = plan[k][2]
            at = start // GROUP * 2 * LINES
            high, low = split(lines[at : at + na * SBY].reshape(na, SBY, SPAN))
            folded[k][0:na] = jnp.concatenate([high, low], axis=1).astype(bf16)
            folded[k][na] = jnp.zeros((2 * SBY, SPAN), bf16)

    lane_tile = iota((16, 128), 1) >> 5
    slot_masks = []
    for s in range(4):
        mask = jnp.where(lane_tile == s, 1.0, 0.0).astype(bf16)
        slot_masks.append(jnp.concatenate([mask] * 3, axis=0))

    def place(k, first):
        _, _, na, a0, x0, rows, slab = plan[k]
        rows += rows % 2
        width = 4 * 2 * SBY
        lane = iota((1, width), 1)
        in_slot = (lane * 1366) >> 16
        b = lane - ((lane * 2731) >> 16) * SBY
        picks = []
        for h in range(2):
            target = b
            for s in range(4):
                target = target + jnp.where(in_slot == s, offset_of(k, 1, 4 * h + s), 0)
            picks.append(
                jnp.where(iota((fw, width), 0) + ystart == target, 1.0, 0.0).astype(bf16)
            )

        def one(i, carry):
            halves = []
            for h in range(2):
                columns = []
                for step in range(2):
                    local = x0 + 2 * i + step - slab * fx - a0
                    pieces = []
                    for s in range(4):
                        at = local - offset_of(k, 0, 4 * h + s)
                        at = jnp.where(jnp.logical_and(at >= 0, at < na), at, na)
                        pieces.append(folded[k][at, :, 128 * h : 128 * h + 128] * slot_masks[s])
                    columns.append(jnp.concatenate(pieces, axis=0))
                halves.append(jnp.dot(
                    picks[h], jnp.concatenate(columns, axis=1), preferred_element_type=f32
                ))
            parts = []
            for step in range(2):
                at = slice(128 * step, 128 * step + 128)
                value = jnp.concatenate([halves[0][:, at], halves[1][:, at]], axis=1)
                parts.append(jnp.concatenate(split(value), axis=1))
            lined[pl.ds(pl.multiple_of(i * (2 * fw), 2 * fw), 2 * fw), :] = jnp.concatenate(
                parts, axis=0
            ).astype(bf16)
            return carry

        lax.fori_loop(0, rows // 2, one, 0, unroll=2 if rows % 4 == 0 else 1)
        lane_row = iota((SPAN, fz), 0)
        depth = lane_row & (SLOT_LANES - 1)
        for s in range(slots):
            depth = depth + jnp.where((lane_row >> 5) == s, offset_of(k, 2, s), 0)
        inside_line = (lane_row & (SLOT_LANES - 1)) < SBZ
        hit = jnp.logical_and(inside_line, iota((SPAN, fz), 1) == depth)
        pick = jnp.where(hit, 1.0, 0.0).astype(bf16)
        pick = jnp.concatenate([pick, pick], axis=0)
        for start in range(0, rows, 4):
            size = min(4, rows - start)
            value = jnp.dot(
                lined[start * fw : (start + size) * fw, :], pick, preferred_element_type=f32
            ).reshape(size, fw, fz)
            at = x0 + HALO + start
            if first:
                dens[at : at + size] = value
            else:
                dens[at : at + size] = dens[at : at + size] + value

    dens[0:HALO] = jnp.zeros((HALO, fw, fz), f32)
    unfold((0,))
    place(0, True)

    own.wait()
    for copy in part_copies:
        copy.wait_recv()
    total = win[...]
    for k in range(1, G):
        total = total + recv[k - 1]
    cext[2 : cx + 2] = total
    rise = pltpu.make_async_remote_copy(
        src_ref=cext.at[pl.ds(cx, 2)], dst_ref=cext.at[pl.ds(0, 2)],
        send_sem=cs_sem.at[0], recv_sem=cr_sem.at[0],
        device_id=(j, d + 1), device_id_type=MESH,
    )
    sink = pltpu.make_async_remote_copy(
        src_ref=cext.at[pl.ds(2, 2)], dst_ref=cext.at[pl.ds(cx + 2, 2)],
        send_sem=cs_sem.at[1], recv_sem=cr_sem.at[1],
        device_id=(j, d - 1), device_id_type=MESH,
    )

    @pl.when(inside[1])
    def _():
        rise.start()

    @pl.when(inside[-1])
    def _():
        sink.start()

    for k in (1, 2, 3):

        @pl.when(inside[plan[k][6]])
        def _(k=k):
            offset_copies[k].wait_recv()
            block_copies[k].wait_recv()

        @pl.when(jnp.logical_not(inside[plan[k][6]]))
        def _(k=k):
            blocks[k][...] = jnp.zeros(blocks[k].shape, f32)
            for row in range(3):
                for s in range(slots):
                    offs[k, row, s] = 0

    unfold((1, 2, 3))
    for k in (1, 2, 3):
        place(k, False)

    @pl.when(inside[-1])
    def _():
        rise.wait_recv()

    @pl.when(jnp.logical_not(inside[-1]))
    def _():
        cext[0:2] = jnp.zeros((2, yw, cz), f32)

    @pl.when(inside[1])
    def _():
        sink.wait_recv()

    @pl.when(jnp.logical_not(inside[1]))
    def _():
        cext[cx + 2 : cx + 4] = jnp.zeros((2, yw, cz), f32)

    count_x = fx + 2 * HALO
    zi, zo = iota((cz, fz), 0), iota((cz, fz), 1)
    zm = zo >> 1
    zn = zm + ((zo & 1) << 1) - 1
    refine_z = weights((cz, fz), ((zi == zm, 0.75), (zi == zn, 0.25))).astype(bf16)
    refine_z = jnp.concatenate([refine_z, refine_z], axis=0)
    yo = iota((fw, yw), 0) + ystart
    yi = iota((fw, yw), 1) + wstart
    ym = yo >> 1
    yn = ym + ((yo & 1) << 1) - 1
    grid = jnp.logical_and(yo >= 0, yo < fy)
    refine_y = weights(
        (fw, yw), ((jnp.logical_and(grid, yi == ym), 0.75), (jnp.logical_and(grid, yi == yn), 0.25))
    )
    refine_y = jnp.concatenate([refine_y, refine_y], axis=1).astype(bf16)

    def in_grid(x):
        g = d * fx + x
        return jnp.where(jnp.logical_and(g >= 0, g < N * fx), 1.0, 0.0).astype(f32)

    def refine_pair(i, carry):
        low_cell, high_cell = cext[i], cext[i + 1]
        odd = 0.75 * low_cell + 0.25 * high_cell
        even = 0.75 * high_cell + 0.25 * low_cell
        both = jnp.concatenate([odd, even], axis=1)
        right = jnp.concatenate(split(both), axis=0).astype(bf16)
        value = jnp.dot(refine_y, right, preferred_element_type=f32)
        value = jnp.concatenate([value[:, :cz], value[:, cz:]], axis=0)
        lined_coarse[pl.ds(pl.multiple_of(i * (2 * fw), 2 * fw), 2 * fw), :] = jnp.concatenate(
            split(value), axis=1
        ).astype(bf16)
        return carry

    lax.fori_loop(0, count_x // 2, refine_pair, 0, unroll=3)
    for start in range(0, count_x, 3):
        value = jnp.dot(
            lined_coarse[start * fw : (start + 3) * fw, :], refine_z, preferred_element_type=f32
        ).reshape(3, fw, fz)
        for i in range(3):
            dens[start + i] = (dens[start + i] + value[i]) * in_grid(start + i - HALO)

    lanes = iota((fw, fz), 1)
    first_lane, last_lane = lanes == 0, lanes == fz - 1

    def diff_z(f):
        after = jnp.where(last_lane, 0.0, pltpu.roll(f, fz - 1, 1))
        before = jnp.where(first_lane, 0.0, pltpu.roll(f, 1, 1))
        return after - before

    def diff_y(f):
        return pltpu.roll(f, fw - 1, 0) - pltpu.roll(f, 1, 0)

    def exchange_row(i, carry):
        n = dens[i + 1]
        gx = dens[i + 2] - dens[i]
        gy = diff_y(n)
        gz = diff_z(n)
        sigma = gx * gx + gy * gy + gz * gz
        live = n > 0.0
        log_n = jnp.log(jnp.where(live, n, 1.0))
        cube_root = jnp.exp(log_n * (1.0 / 3.0))
        inv_ft = jnp.exp(log_n * (-4.0 / 3.0))
        reduced = sigma * (inv_ft * inv_ft) * (half_inverse * half_inverse / gradient_scale)
        inv_d = 1.0 / (1.0 + (mu_pbe / kappa_pbe) * reduced)
        slope = mu_pbe * inv_d * inv_d
        by_density = (exchange_prefactor * cube_root) * (
            (4.0 / 3.0) * (1.0 + kappa_pbe - kappa_pbe * inv_d) - (8.0 / 3.0) * reduced * slope
        )
        twice = jnp.where(live, (2.0 * exchange_prefactor * half_inverse * half_inverse / gradient_scale) * slope * inv_ft, 0.0)
        flux[i] = twice * gx
        pot[i] = by_density - (diff_y(twice * gy) + diff_z(twice * gz))
        return carry


    ro, ri = iota((yc, fw), 0), iota((yc, fw), 1)
    at = ri - 4 - 2 * ro
    grid = jnp.logical_and(ri + ystart >= 0, ri + ystart < fy)
    inner = jnp.logical_and(grid, jnp.logical_or(at == 0, at == 1))
    outer = jnp.logical_and(grid, jnp.logical_or(at == -1, at == 2))
    restrict_y = weights((yc, fw), ((inner, 0.375), (outer, 0.125)))
    restrict_y = jnp.concatenate([restrict_y, restrict_y], axis=1).astype(bf16)
    at = iota((fz, cz), 0) - 2 * iota((fz, cz), 1)
    inner = jnp.logical_or(at == 0, at == 1)
    outer = jnp.logical_or(at == -1, at == 2)
    restrict_z = weights((fz, cz), ((inner, 0.375), (outer, 0.125))).astype(bf16)
    restrict_z = jnp.concatenate([restrict_z, restrict_z], axis=0)

    def full(x):
        return (pot[x + 2] - (flux[x + 3] - flux[x + 1])) * in_grid(x)

    ymine = pl.multiple_of(q * yc, 8)

    def restrict_rows(low_row, high_row):
        pieces = []
        for i in range(low_row, high_row):
            x = 2 * i
            mixed = 0.125 * (full(x - 1) + full(x + 2)) + 0.375 * (full(x) + full(x + 1))
            high, low = split(mixed)
            pieces.append(jnp.dot(
                restrict_y,
                jnp.concatenate([high, low], axis=0).astype(bf16),
                preferred_element_type=f32,
            ))
        high, low = split(jnp.concatenate(pieces, axis=0))
        result = jnp.dot(
            jnp.concatenate([high, low], axis=1).astype(bf16), restrict_z, preferred_element_type=f32
        )
        out[low_row:high_row, pl.ds(ymine, yc), :] = result.reshape(high_row - low_row, yc, cz)

    base = j - q
    half = cx // 2
    gather = []
    done = 0
    for piece, (low_row, high_row) in enumerate(((0, half), (half, cx))):
        lax.fori_loop(done, 2 * high_row + 4, exchange_row, 0)
        done = 2 * high_row + 4
        restrict_rows(low_row, high_row)
        for k in range(1, Q):
            at = (pl.ds(low_row, high_row - low_row), pl.ds(ymine, yc), slice(None))
            copy = pltpu.make_async_remote_copy(
                src_ref=out.at[at],
                dst_ref=out.at[at],
                send_sem=gs_sem.at[piece, k - 1], recv_sem=gr_sem.at[piece, k - 1],
                device_id=(base + lax.rem(q + k, Q), d), device_id_type=MESH,
            )
            copy.start()
            gather.append(copy)
    for copy in part_copies:
        copy.wait_send()
    for k in (1, 2, 3):

        @pl.when(inside[-plan[k][6]])
        def _(k=k):
            offset_copies[k].wait_send()
            block_copies[k].wait_send()

    @pl.when(inside[1])
    def _():
        rise.wait_send()

    @pl.when(inside[-1])
    def _():
        sink.wait_send()

    for copy in gather:
        copy.wait()


def body(G, N, Q, partial_density, moments, shape_functions, sphere_offsets, owned_count):
    _, cx, cy, cz = partial_density.shape
    slots, channels, block = shape_functions.shape
    fx, fz = 2 * cx, 2 * cz
    yc = cy // Q
    yw, fw = yc + 16, 2 * yc + 8
    plan = sources(fx)
    hbm = pl.BlockSpec(memory_space=pltpu.HBM)
    vmem = pl.BlockSpec(memory_space=pltpu.VMEM)
    smem = pl.BlockSpec(memory_space=pltpu.SMEM)
    return pl.pallas_call(
        functools.partial(kernel, G, N, Q),
        out_shape=jax.ShapeDtypeStruct((cx, cy, cz), f32),
        in_specs=[hbm, vmem, hbm, smem, smem],
        out_specs=vmem,
        scratch_shapes=[
            pltpu.VMEM((channels, slots, block), bf16),
            pltpu.VMEM((cx, yw, cz), f32),
            pltpu.VMEM((G - 1, cx, yw, cz), f32),
            pltpu.VMEM((cx + 4, yw, cz), f32),
        ]
        + [pltpu.VMEM((slots, p[1] * GROUP), f32) for p in plan]
        + [pltpu.VMEM((slots, 26 * GROUP), f32)] * 2
        + [pltpu.SMEM((4,) + sphere_offsets.shape, jnp.int32)]
        + [pltpu.VMEM((2, slots, SPAN, SPAN), bf16), pltpu.VMEM((2, 26 * LINES, slots * 2 * SPAN), bf16)]
        + [pltpu.VMEM((p[2] + 1, 2 * SBY, SPAN), bf16) for p in plan]
        + [
            pltpu.VMEM(((fx + 4) * fw, 2 * SPAN), bf16),
            pltpu.VMEM(((fx + 2 * HALO) * fw, 2 * cz), bf16),
            pltpu.VMEM((fx + 2 * HALO + 1, fw, fz), f32),
            pltpu.VMEM((fx + 4, fw, fz), f32),
            pltpu.VMEM((fx + 4, fw, fz), f32),
            pltpu.SemaphoreType.DMA(()),
            pltpu.SemaphoreType.DMA(()),
            pltpu.SemaphoreType.DMA((G - 1,)),
            pltpu.SemaphoreType.DMA((G - 1,)),
            pltpu.SemaphoreType.DMA((2,)),
            pltpu.SemaphoreType.DMA((2,)),
            pltpu.SemaphoreType.DMA((4,)),
            pltpu.SemaphoreType.DMA((4,)),
            pltpu.SemaphoreType.DMA((4,)),
            pltpu.SemaphoreType.DMA((4,)),
            pltpu.SemaphoreType.DMA((2, Q - 1)),
            pltpu.SemaphoreType.DMA((2, Q - 1)),
        ],
        compiler_params=pltpu.CompilerParams(
            collective_id=0, has_side_effects=True, vmem_limit_bytes=40 * 1024 * 1024
        ),
    )(partial_density, moments.T, shape_functions.transpose(1, 0, 2), sphere_offsets, owned_count)


def solution(mesh):
    G, N = mesh.shape["band"], mesh.shape["dom"]

    def run(partial_density, *rest):
        cy = partial_density.shape[2]
        Q = max(c for c in range(1, G + 1) if G % c == 0 and cy % (8 * c) == 0)
        return jax.shard_map(
            functools.partial(body, G, N, Q),
            mesh=mesh,
            in_specs=(
                P("band", "dom", None, None),
                P(None, "dom"),
                P("dom", None, None),
                P(None, "dom"),
                P("dom"),
            ),
            out_specs=P("dom", None, None),
            check_vma=False,
        )(partial_density, *rest)

    return run
```

```python
import functools

import jax
import jax.numpy as jnp
from jax import lax
from jax.experimental import pallas as pl
from jax.experimental.pallas import tpu as pltpu
from jax.sharding import PartitionSpec as P

SBX = 12
SBY = 24
SBZ = 24
GROUP = 384
LINES = 8
SPAN = 256
SLOT_LANES = 32
HALO = 3

kappa_pbe = 0.804
mu_pbe = 0.2195
exchange_prefactor = -0.75 * (3.0 / 3.141592653589793) ** (1.0 / 3.0)
gradient_scale = 4.0 * (3.0 * 3.141592653589793**2) ** (2.0 / 3.0)
half_inverse = 0.5 / 0.2

f32 = jnp.float32
bf16 = jnp.bfloat16
MESH = pl.DeviceIdType.MESH


def iota(shape, dim):
    return lax.broadcasted_iota(jnp.int32, shape, dim)


def split(x):
    high = x.astype(bf16).astype(f32)
    return high, x - high


def weights(shape, terms):
    total = jnp.zeros(shape, f32)
    for mask, value in terms:
        total = jnp.where(mask, value, total)
    return total


def sources(fx):
    return (
        (0, 18, SBX, 0, 0, fx + HALO, 0),
        (0, 18, SBX, 0, -HALO, SBX - 1 + HALO, -1),
        (5760, 3, 2, 10, -HALO, 2, -2),
        (0, 5, 3, 0, fx, HALO, 1),
    )


def kernel(
    G, N, Q,
    part, mom, shp_hbm, off, cnt,
    out,
    shp, win, recv, cext, v0, v1, v2, v3, vh, vl, offs, unfolder, wide, u0, u1, u2, u3, lined, lined_coarse, dens, flux, pot, mine,
    shp_sem, win_sem, ps_sem, pr_sem, cs_sem, cr_sem, vs_sem, vr_sem, os_sem, or_sem, gs_sem, gr_sem, keep_sem,
):
    _, cx, cy, cz = part.shape
    fx, fy, fz = 2 * cx, 2 * cy, 2 * cz
    yc = cy // Q
    yw = yc + 16
    fw = 2 * yc + 8
    j = lax.axis_index("band")
    d = lax.axis_index("dom")
    q = lax.rem(j, Q)

    def chunk_of(index):
        return pl.ds(pl.multiple_of(lax.rem(index, Q) * yc, 8), yc)

    own = pltpu.make_async_copy(part.at[0, :, chunk_of(j), :], win, win_sem)
    own.start()
    fetch = pltpu.make_async_copy(shp_hbm, shp, shp_sem)
    fetch.start()
    cext[...] = jnp.zeros(cext.shape, f32)
    base = j - q
    ystart = 2 * yc * q - 4
    slots = shp.shape[1]

    barrier = pltpu.get_barrier_semaphore()
    for k in range(1, G):
        pl.semaphore_signal(barrier, inc=1, device_id=(lax.rem(j + k, G), d), device_id_type=MESH)
    inside = {}
    for step in (-2, -1, 1, 2):
        inside[step] = jnp.logical_and(d + step >= 0, d + step < N)

        @pl.when(inside[step])
        def _(step=step):
            pl.semaphore_signal(barrier, inc=1, device_id=(j, d + step), device_id_type=MESH)

    sides = [(dj, dd) for dj in (-1, 0, 1) for dd in (-1, 0, 1) if dj or dd]
    beside = {}
    for dj, dd in sides:
        there = jnp.logical_and(q + dj >= 0, q + dj < Q)
        if dd:
            there = jnp.logical_and(there, inside[dd])
        beside[dj, dd] = there
        if dj and dd:

            @pl.when(there)
            def _(dj=dj, dd=dd):
                pl.semaphore_signal(barrier, inc=1, device_id=(j + dj, d + dd), device_id_type=MESH)

    count = G - 1
    for there in [inside[step] for step in (-2, -1, 1, 2)] + [
        beside[dj, dd] for dj, dd in sides if dj and dd
    ]:
        count = count + jnp.where(there, 1, 0)
    pl.semaphore_wait(barrier, count)

    part_copies = []
    for k in range(1, G):
        peer = lax.rem(j + k, G)
        copy = pltpu.make_async_remote_copy(
            src_ref=part.at[0, :, chunk_of(peer), :],
            dst_ref=recv.at[k - 1],
            send_sem=ps_sem.at[k - 1],
            recv_sem=pr_sem.at[k - 1],
            device_id=(peer, d),
            device_id_type=MESH,
        )
        copy.start()
        part_copies.append(copy)

    channels = shp.shape[0]
    moments = mom[...].astype(f32)
    moments = jnp.where(iota(moments.shape, 0) < cnt[0], moments, 0.0)
    scales = [jnp.broadcast_to(moments[:, l : l + 1], (slots, GROUP)) for l in range(channels)]
    fetch.wait()
    for g in range(v0.shape[1] // GROUP):
        at = slice(g * GROUP, (g + 1) * GROUP)
        total = shp[0, :, at].astype(f32) * scales[0]
        for l in range(1, channels):
            total = total + shp[l, :, at].astype(f32) * scales[l]
        v0[:, at] = total

    plan = sources(fx)
    blocks = (v0, v1, v2, v3)
    folded = (u0, u1, u2, u3)
    block_copies = [None]
    offset_copies = [None]
    for k in (1, 2, 3):
        lane, groups = plan[k][0], plan[k][1]
        step = -plan[k][6]
        block_copies.append(pltpu.make_async_remote_copy(
            src_ref=v0.at[:, pl.ds(lane, groups * GROUP)],
            dst_ref=blocks[k],
            send_sem=vs_sem.at[k], recv_sem=vr_sem.at[k],
            device_id=(j, d + step), device_id_type=MESH,
        ))
        offset_copies.append(pltpu.make_async_remote_copy(
            src_ref=off,
            dst_ref=offs.at[k],
            send_sem=os_sem.at[k], recv_sem=or_sem.at[k],
            device_id=(j, d + step), device_id_type=MESH,
        ))

        @pl.when(inside[step])
        def _(k=k):
            offset_copies[k].start()
            block_copies[k].start()

    line_masks = []
    for h in range(2):
        lane = iota((LINES, SPAN), 1) + 128 * h
        line_masks.append(((lane * 2731) >> 16) == iota((LINES, SPAN), 0) + LINES * h)
    k_rows, k_lanes = iota((SPAN, 128), 0), iota((SPAN, 128), 1)
    for h in range(2):
        k_rows_h = k_rows + 128 * h
        shift = k_lanes - (k_rows_h - ((k_rows_h * 2731) >> 16) * SBZ)
        for s in range(4):
            unfolder[h, s] = jnp.where(shift == SLOT_LANES * s, 1.0, 0.0).astype(bf16)

    def offset_of(k, row, s):
        return off[row, s] if k == 0 else offs[k, row, s]

    def unfold(which):
        starts = []
        total = 0
        for k in which:
            starts.append(total)
            width = plan[k][1] * GROUP
            high, low = split(blocks[k][...])
            vh[:, total : total + width] = high
            vl[:, total : total + width] = low
            total += width
        groups = total // GROUP

        def one(s, carry):
            for h in range(2):
                for t, source in enumerate((vh, vl)):
                    pieces = []
                    for g in range(groups):
                        at = g * GROUP + 128 * h
                        line = source[pl.ds(s, 1), at : at + SPAN]
                        pieces.append(
                            jnp.where(line_masks[h], jnp.broadcast_to(line, (LINES, SPAN)), 0.0)
                        )
                    lane = pl.multiple_of(s * (2 * SPAN) + t * SPAN, SPAN)
                    wide[h, : groups * LINES, pl.ds(lane, SPAN)] = jnp.concatenate(
                        pieces, axis=0
                    ).astype(bf16)
            return carry

        lax.fori_loop(0, slots, one, 0, unroll=2)
        halves = []
        for h in range(2):
            right = []
            for s in range(4):
                right += [unfolder[h, s]] * 2
            right = jnp.concatenate(right, axis=0)
            value = [
                jnp.dot(
                    wide[h, : groups * LINES, t * 8 * SPAN : (t + 1) * 8 * SPAN], right,
                    preferred_element_type=f32,
                )
                for t in range(2)
            ]
            value = jnp.concatenate(value, axis=1)
            halves.append(value.reshape(groups, LINES, SPAN))
        lines = jnp.stack(halves, axis=1).reshape(groups * 2 * LINES, SPAN)
        for k, start in zip(which, starts):
            na = plan[k][2]
            at = start // GROUP * 2 * LINES
            high, low = split(lines[at : at + na * SBY].reshape(na, SBY, SPAN))
            folded[k][0:na] = jnp.concatenate([high, low], axis=1).astype(bf16)
            folded[k][na] = jnp.zeros((2 * SBY, SPAN), bf16)

    lane_tile = iota((16, 128), 1) >> 5
    slot_masks = []
    for s in range(4):
        mask = jnp.where(lane_tile == s, 1.0, 0.0).astype(bf16)
        slot_masks.append(jnp.concatenate([mask] * 3, axis=0))

    def place(k, first):
        _, _, na, a0, x0, rows, slab = plan[k]
        rows += rows % 2
        width = 4 * 2 * SBY
        lane = iota((1, width), 1)
        in_slot = (lane * 1366) >> 16
        b = lane - ((lane * 2731) >> 16) * SBY
        picks = []
        for h in range(2):
            target = b
            for s in range(4):
                target = target + jnp.where(in_slot == s, offset_of(k, 1, 4 * h + s), 0)
            picks.append(
                jnp.where(iota((fw, width), 0) + ystart == target, 1.0, 0.0).astype(bf16)
            )

        def one(i, carry):
            halves = []
            for h in range(2):
                columns = []
                for step in range(2):
                    local = x0 + 2 * i + step - slab * fx - a0
                    pieces = []
                    for s in range(4):
                        at = local - offset_of(k, 0, 4 * h + s)
                        at = jnp.where(jnp.logical_and(at >= 0, at < na), at, na)
                        pieces.append(folded[k][at, :, 128 * h : 128 * h + 128] * slot_masks[s])
                    columns.append(jnp.concatenate(pieces, axis=0))
                halves.append(jnp.dot(
                    picks[h], jnp.concatenate(columns, axis=1), preferred_element_type=f32
                ))
            parts = []
            for step in range(2):
                at = slice(128 * step, 128 * step + 128)
                value = jnp.concatenate([halves[0][:, at], halves[1][:, at]], axis=1)
                parts.append(jnp.concatenate(split(value), axis=1))
            lined[pl.ds(pl.multiple_of(i * (2 * fw), 2 * fw), 2 * fw), :] = jnp.concatenate(
                parts, axis=0
            ).astype(bf16)
            return carry

        lax.fori_loop(0, rows // 2, one, 0, unroll=2 if rows % 4 == 0 else 1)
        lane_row = iota((SPAN, fz), 0)
        depth = lane_row & (SLOT_LANES - 1)
        for s in range(slots):
            depth = depth + jnp.where((lane_row >> 5) == s, offset_of(k, 2, s), 0)
        inside_line = (lane_row & (SLOT_LANES - 1)) < SBZ
        hit = jnp.logical_and(inside_line, iota((SPAN, fz), 1) == depth)
        pick = jnp.where(hit, 1.0, 0.0).astype(bf16)
        pick = jnp.concatenate([pick, pick], axis=0)
        for start in range(0, rows, 4):
            size = min(4, rows - start)
            value = jnp.dot(
                lined[start * fw : (start + size) * fw, :], pick, preferred_element_type=f32
            ).reshape(size, fw, fz)
            at = x0 + HALO + start
            if first:
                dens[at : at + size] = value
            else:
                dens[at : at + size] = dens[at : at + size] + value

    dens[0:HALO] = jnp.zeros((HALO, fw, fz), f32)
    unfold((0,))
    place(0, True)

    for k in (1, 2, 3):

        @pl.when(inside[plan[k][6]])
        def _(k=k):
            offset_copies[k].wait_recv()
            block_copies[k].wait_recv()

        @pl.when(jnp.logical_not(inside[plan[k][6]]))
        def _(k=k):
            blocks[k][...] = jnp.zeros(blocks[k].shape, f32)
            for row in range(3):
                for s in range(slots):
                    offs[k, row, s] = 0

    unfold((1, 2, 3))

    own.wait()
    for copy in part_copies:
        copy.wait_recv()
    total = win[...]
    for k in range(1, G):
        total = total + recv[k - 1]
    cext[2 : cx + 2, 8 : 8 + yc] = total
    rows_from = {-1: pl.ds(2, 2), 0: pl.ds(2, cx), 1: pl.ds(cx, 2)}
    rows_to = {-1: pl.ds(cx + 2, 2), 0: pl.ds(2, cx), 1: pl.ds(0, 2)}
    cols_from = {-1: pl.ds(8, 8), 0: pl.ds(8, yc), 1: pl.ds(yc, 8)}
    cols_to = {-1: pl.ds(yc + 8, 8), 0: pl.ds(8, yc), 1: pl.ds(0, 8)}
    halo_copies = {}
    for n, (dj, dd) in enumerate(sides):
        halo_copies[dj, dd] = pltpu.make_async_remote_copy(
            src_ref=cext.at[rows_from[dd], cols_from[dj]],
            dst_ref=cext.at[rows_to[dd], cols_to[dj]],
            send_sem=cs_sem.at[n], recv_sem=cr_sem.at[n],
            device_id=(j + dj, d + dd), device_id_type=MESH,
        )

        @pl.when(beside[dj, dd])
        def _(dj=dj, dd=dd):
            halo_copies[dj, dd].start()

    for k in (1, 2, 3):
        place(k, False)

    for dj, dd in sides:

        @pl.when(beside[-dj, -dd])
        def _(dj=dj, dd=dd):
            halo_copies[dj, dd].wait_recv()

    count_x = fx + 2 * HALO
    zi, zo = iota((cz, fz), 0), iota((cz, fz), 1)
    zm = zo >> 1
    zn = zm + ((zo & 1) << 1) - 1
    refine_z = weights((cz, fz), ((zi == zm, 0.75), (zi == zn, 0.25))).astype(bf16)
    refine_z = jnp.concatenate([refine_z, refine_z], axis=0)
    yo = iota((fw, yw), 0) + ystart
    yi = iota((fw, yw), 1) + (yc * q - 8)
    ym = yo >> 1
    yn = ym + ((yo & 1) << 1) - 1
    grid = jnp.logical_and(yo >= 0, yo < fy)
    refine_y = weights(
        (fw, yw), ((jnp.logical_and(grid, yi == ym), 0.75), (jnp.logical_and(grid, yi == yn), 0.25))
    )
    refine_y = jnp.concatenate([refine_y, refine_y], axis=1).astype(bf16)

    def in_grid(x):
        g = d * fx + x
        return jnp.where(jnp.logical_and(g >= 0, g < N * fx), 1.0, 0.0).astype(f32)

    def refine_pair(i, carry):
        low_cell, high_cell = cext[i], cext[i + 1]
        odd = 0.75 * low_cell + 0.25 * high_cell
        even = 0.75 * high_cell + 0.25 * low_cell
        both = jnp.concatenate([odd, even], axis=1)
        right = jnp.concatenate(split(both), axis=0).astype(bf16)
        value = jnp.dot(refine_y, right, preferred_element_type=f32)
        value = jnp.concatenate([value[:, :cz], value[:, cz:]], axis=0)
        lined_coarse[pl.ds(pl.multiple_of(i * (2 * fw), 2 * fw), 2 * fw), :] = jnp.concatenate(
            split(value), axis=1
        ).astype(bf16)
        return carry

    lax.fori_loop(0, count_x // 2, refine_pair, 0, unroll=3)
    for start in range(0, count_x, 3):
        value = jnp.dot(
            lined_coarse[start * fw : (start + 3) * fw, :], refine_z, preferred_element_type=f32
        ).reshape(3, fw, fz)
        for i in range(3):
            dens[start + i] = (dens[start + i] + value[i]) * in_grid(start + i - HALO)

    lanes = iota((fw, fz), 1)
    first_lane, last_lane = lanes == 0, lanes == fz - 1

    def diff_z(f):
        after = jnp.where(last_lane, 0.0, pltpu.roll(f, fz - 1, 1))
        before = jnp.where(first_lane, 0.0, pltpu.roll(f, 1, 1))
        return after - before

    def diff_y(f):
        return pltpu.roll(f, fw - 1, 0) - pltpu.roll(f, 1, 0)

    def exchange_row(i, carry):
        n = dens[i + 1]
        gx = dens[i + 2] - dens[i]
        gy = diff_y(n)
        gz = diff_z(n)
        sigma = gx * gx + gy * gy + gz * gz
        live = n > 0.0
        log_n = jnp.log(jnp.where(live, n, 1.0))
        cube_root = jnp.exp(log_n * (1.0 / 3.0))
        inv_ft = jnp.exp(log_n * (-4.0 / 3.0))
        reduced = sigma * (inv_ft * inv_ft) * (half_inverse * half_inverse / gradient_scale)
        inv_d = 1.0 / (1.0 + (mu_pbe / kappa_pbe) * reduced)
        slope = mu_pbe * inv_d * inv_d
        by_density = (exchange_prefactor * cube_root) * (
            (4.0 / 3.0) * (1.0 + kappa_pbe - kappa_pbe * inv_d) - (8.0 / 3.0) * reduced * slope
        )
        twice = jnp.where(live, (2.0 * exchange_prefactor * half_inverse * half_inverse / gradient_scale) * slope * inv_ft, 0.0)
        flux[i] = twice * gx
        pot[i] = by_density - (diff_y(twice * gy) + diff_z(twice * gz))
        return carry


    ro, ri = iota((yc, fw), 0), iota((yc, fw), 1)
    at = ri - 4 - 2 * ro
    grid = jnp.logical_and(ri + ystart >= 0, ri + ystart < fy)
    inner = jnp.logical_and(grid, jnp.logical_or(at == 0, at == 1))
    outer = jnp.logical_and(grid, jnp.logical_or(at == -1, at == 2))
    restrict_y = weights((yc, fw), ((inner, 0.375), (outer, 0.125)))
    restrict_y = jnp.concatenate([restrict_y, restrict_y], axis=1).astype(bf16)
    at = iota((fz, cz), 0) - 2 * iota((fz, cz), 1)
    inner = jnp.logical_or(at == 0, at == 1)
    outer = jnp.logical_or(at == -1, at == 2)
    restrict_z = weights((fz, cz), ((inner, 0.375), (outer, 0.125))).astype(bf16)
    restrict_z = jnp.concatenate([restrict_z, restrict_z], axis=0)

    def full(x):
        return (pot[x + 2] - (flux[x + 3] - flux[x + 1])) * in_grid(x)

    ymine = pl.multiple_of(q * yc, 8)

    def restrict_rows(low_row, high_row):
        pieces = []
        for i in range(low_row, high_row):
            x = 2 * i
            mixed = 0.125 * (full(x - 1) + full(x + 2)) + 0.375 * (full(x) + full(x + 1))
            high, low = split(mixed)
            pieces.append(jnp.dot(
                restrict_y,
                jnp.concatenate([high, low], axis=0).astype(bf16),
                preferred_element_type=f32,
            ))
        high, low = split(jnp.concatenate(pieces, axis=0))
        result = jnp.dot(
            jnp.concatenate([high, low], axis=1).astype(bf16), restrict_z, preferred_element_type=f32
        )
        mine[low_row:high_row] = result.reshape(high_row - low_row, yc, cz)

    half = cx // 2
    gather = []
    keep = []
    done = 0
    for piece, (low_row, high_row) in enumerate(((0, half), (half, cx))):
        lax.fori_loop(done, 2 * high_row + 4, exchange_row, 0, unroll=2)
        done = 2 * high_row + 4
        restrict_rows(low_row, high_row)
        rows = pl.ds(low_row, high_row - low_row)
        at = (rows, pl.ds(ymine, yc), slice(None))
        for k in range(1, Q):
            copy = pltpu.make_async_remote_copy(
                src_ref=mine.at[rows],
                dst_ref=out.at[at],
                send_sem=gs_sem.at[piece, k - 1], recv_sem=gr_sem.at[piece, k - 1],
                device_id=(base + lax.rem(q + k, Q), d), device_id_type=MESH,
            )
            copy.start()
            gather.append(copy)
        copy = pltpu.make_async_copy(mine.at[rows], out.at[at], keep_sem.at[piece])
        copy.start()
        keep.append(copy)
    for copy in part_copies:
        copy.wait_send()
    for k in (1, 2, 3):

        @pl.when(inside[-plan[k][6]])
        def _(k=k):
            offset_copies[k].wait_send()
            block_copies[k].wait_send()

    for dj, dd in sides:

        @pl.when(beside[dj, dd])
        def _(dj=dj, dd=dd):
            halo_copies[dj, dd].wait_send()

    for copy in gather + keep:
        copy.wait()


def body(G, N, Q, partial_density, moments, shape_functions, sphere_offsets, owned_count):
    _, cx, cy, cz = partial_density.shape
    slots, channels, block = shape_functions.shape
    fx, fz = 2 * cx, 2 * cz
    yc = cy // Q
    yw, fw = yc + 16, 2 * yc + 8
    plan = sources(fx)
    hbm = pl.BlockSpec(memory_space=pltpu.HBM)
    vmem = pl.BlockSpec(memory_space=pltpu.VMEM)
    smem = pl.BlockSpec(memory_space=pltpu.SMEM)
    return pl.pallas_call(
        functools.partial(kernel, G, N, Q),
        out_shape=jax.ShapeDtypeStruct((cx, cy, cz), f32),
        in_specs=[hbm, vmem, hbm, smem, smem],
        out_specs=hbm,
        scratch_shapes=[
            pltpu.VMEM((channels, slots, block), bf16),
            pltpu.VMEM((cx, yc, cz), f32),
            pltpu.VMEM((G - 1, cx, yc, cz), f32),
            pltpu.VMEM((cx + 4, yw, cz), f32),
        ]
        + [pltpu.VMEM((slots, p[1] * GROUP), f32) for p in plan]
        + [pltpu.VMEM((slots, 26 * GROUP), f32)] * 2
        + [pltpu.SMEM((4,) + sphere_offsets.shape, jnp.int32)]
        + [pltpu.VMEM((2, 4, SPAN, 128), bf16), pltpu.VMEM((2, 26 * LINES, slots * 2 * SPAN), bf16)]
        + [pltpu.VMEM((p[2] + 1, 2 * SBY, SPAN), bf16) for p in plan]
        + [
            pltpu.VMEM(((fx + 4) * fw, 2 * SPAN), bf16),
            pltpu.VMEM(((fx + 2 * HALO) * fw, 2 * cz), bf16),
            pltpu.VMEM((fx + 2 * HALO + 1, fw, fz), f32),
            pltpu.VMEM((fx + 4, fw, fz), f32),
            pltpu.VMEM((fx + 4, fw, fz), f32),
            pltpu.VMEM((cx, yc, cz), f32),
            pltpu.SemaphoreType.DMA(()),
            pltpu.SemaphoreType.DMA(()),
            pltpu.SemaphoreType.DMA((G - 1,)),
            pltpu.SemaphoreType.DMA((G - 1,)),
            pltpu.SemaphoreType.DMA((8,)),
            pltpu.SemaphoreType.DMA((8,)),
            pltpu.SemaphoreType.DMA((4,)),
            pltpu.SemaphoreType.DMA((4,)),
            pltpu.SemaphoreType.DMA((4,)),
            pltpu.SemaphoreType.DMA((4,)),
            pltpu.SemaphoreType.DMA((2, Q - 1)),
            pltpu.SemaphoreType.DMA((2, Q - 1)),
            pltpu.SemaphoreType.DMA((2,)),
        ],
        compiler_params=pltpu.CompilerParams(
            collective_id=0, has_side_effects=True, vmem_limit_bytes=58 * 1024 * 1024
        ),
    )(partial_density, moments.T, shape_functions.transpose(1, 0, 2), sphere_offsets, owned_count)


def solution(mesh):
    G, N = mesh.shape["band"], mesh.shape["dom"]

    def run(partial_density, *rest):
        cy = partial_density.shape[2]
        Q = max(c for c in range(1, G + 1) if G % c == 0 and cy % (8 * c) == 0)
        return jax.shard_map(
            functools.partial(body, G, N, Q),
            mesh=mesh,
            in_specs=(
                P("band", "dom", None, None),
                P(None, "dom"),
                P("dom", None, None),
                P(None, "dom"),
                P("dom"),
            ),
            out_specs=P("dom", None, None),
            check_vma=False,
        )(partial_density, *rest)

    return run
```

```python
import functools

import jax
import jax.numpy as jnp
from jax import lax
from jax.experimental import pallas as pl
from jax.experimental.pallas import tpu as pltpu
from jax.sharding import PartitionSpec as P

SBX = 12
SBY = 24
SBZ = 24
GROUP = 384
LINES = 8
SPAN = 256
SLOT_LANES = 32
PIECES = 3
HALO = 3

kappa_pbe = 0.804
mu_pbe = 0.2195
exchange_prefactor = -0.75 * (3.0 / 3.141592653589793) ** (1.0 / 3.0)
gradient_scale = 4.0 * (3.0 * 3.141592653589793**2) ** (2.0 / 3.0)
half_inverse = 0.5 / 0.2

f32 = jnp.float32
bf16 = jnp.bfloat16
MESH = pl.DeviceIdType.MESH


def iota(shape, dim):
    return lax.broadcasted_iota(jnp.int32, shape, dim)


def split(x):
    high = x.astype(bf16).astype(f32)
    return high, x - high


def weights(shape, terms):
    total = jnp.zeros(shape, f32)
    for mask, value in terms:
        total = jnp.where(mask, value, total)
    return total


def sources(fx):
    return (
        (0, 18, SBX, 0, 0, fx + HALO, 0),
        (0, 18, SBX, 0, -HALO, SBX - 1 + HALO, -1),
        (5760, 3, 2, 10, -HALO, 2, -2),
        (0, 5, 3, 0, fx, HALO, 1),
    )


def kernel(
    G, N, Q,
    part, mom_hbm, shp_hbm, off_hbm, cnt_hbm,
    out,
    mom, off, cnt, shp, win, recv, cext, v0, v1, v2, v3, vh, vl, offs, unfolder, wide, u0, u1, u2, u3, lined, lined_coarse, dens, flux, pot, mine,
    small_sem, shp_sem, win_sem, ps_sem, pr_sem, cs_sem, cr_sem, vs_sem, vr_sem, os_sem, or_sem, gs_sem, gr_sem, keep_sem,
):
    _, cx, cy, cz = part.shape
    fx, fy, fz = 2 * cx, 2 * cy, 2 * cz
    yc = cy // Q
    yw = yc + 16
    fw = 2 * yc + 8
    j = lax.axis_index("band")
    d = lax.axis_index("dom")
    q = lax.rem(j, Q)

    def chunk_of(index):
        return pl.ds(pl.multiple_of(lax.rem(index, Q) * yc, 8), yc)

    own = pltpu.make_async_copy(part.at[0, :, chunk_of(j), :], win, win_sem)
    own.start()
    small = []
    for n, (source, target) in enumerate(((mom_hbm, mom), (off_hbm, off), (cnt_hbm, cnt))):
        small.append(pltpu.make_async_copy(source, target, small_sem.at[n]))
        small[-1].start()
    piece_lanes = shp.shape[2] // PIECES
    fetches = []
    for n in range(PIECES):
        at = (slice(None), slice(None), pl.ds(n * piece_lanes, piece_lanes))
        fetches.append(pltpu.make_async_copy(shp_hbm.at[at], shp.at[at], shp_sem.at[n]))
        fetches[-1].start()
    cext[...] = jnp.zeros(cext.shape, f32)
    base = j - q
    ystart = 2 * yc * q - 4
    slots = shp.shape[1]

    barrier = pltpu.get_barrier_semaphore()
    for k in range(1, G):
        pl.semaphore_signal(barrier, inc=1, device_id=(lax.rem(j + k, G), d), device_id_type=MESH)
    inside = {}
    for step in (-2, -1, 1, 2):
        inside[step] = jnp.logical_and(d + step >= 0, d + step < N)

        @pl.when(inside[step])
        def _(step=step):
            pl.semaphore_signal(barrier, inc=1, device_id=(j, d + step), device_id_type=MESH)

    sides = [(dj, dd) for dj in (-1, 0, 1) for dd in (-1, 0, 1) if dj or dd]
    beside = {}
    for dj, dd in sides:
        there = jnp.logical_and(q + dj >= 0, q + dj < Q)
        if dd:
            there = jnp.logical_and(there, inside[dd])
        beside[dj, dd] = there
        if dj and dd:

            @pl.when(there)
            def _(dj=dj, dd=dd):
                pl.semaphore_signal(barrier, inc=1, device_id=(j + dj, d + dd), device_id_type=MESH)

    count = G - 1
    for there in [inside[step] for step in (-2, -1, 1, 2)] + [
        beside[dj, dd] for dj, dd in sides if dj and dd
    ]:
        count = count + jnp.where(there, 1, 0)
    pl.semaphore_wait(barrier, count)

    part_copies = []
    for k in range(1, G):
        peer = lax.rem(j + k, G)
        copy = pltpu.make_async_remote_copy(
            src_ref=part.at[0, :, chunk_of(peer), :],
            dst_ref=recv.at[k - 1],
            send_sem=ps_sem.at[k - 1],
            recv_sem=pr_sem.at[k - 1],
            device_id=(peer, d),
            device_id_type=MESH,
        )
        copy.start()
        part_copies.append(copy)

    channels = shp.shape[0]
    for copy in small:
        copy.wait()
    plan = sources(fx)
    blocks = (v0, v1, v2, v3)
    folded = (u0, u1, u2, u3)
    offset_copies = [None]
    for k in (1, 2, 3):
        step = -plan[k][6]
        offset_copies.append(pltpu.make_async_remote_copy(
            src_ref=off,
            dst_ref=offs.at[k],
            send_sem=os_sem.at[k], recv_sem=or_sem.at[k],
            device_id=(j, d + step), device_id_type=MESH,
        ))

        @pl.when(inside[step])
        def _(k=k):
            offset_copies[k].start()

    last = shp.shape[2] - plan[2][1] * GROUP
    cuts = [[(1, n * piece_lanes, n * piece_lanes, piece_lanes)] for n in range(PIECES)]
    cuts[0].append((3, 0, 0, plan[3][1] * GROUP))
    cuts[PIECES - 1].append((2, last, 0, plan[2][1] * GROUP))
    block_copies = {1: [], 2: [], 3: []}
    moments = mom[...].astype(f32)
    moments = jnp.where(iota(moments.shape, 0) < cnt[0], moments, 0.0)
    scales = [jnp.broadcast_to(moments[:, l : l + 1], (slots, GROUP)) for l in range(channels)]
    sent = 0
    for n in range(PIECES):
        fetches[n].wait()
        for g in range(n * piece_lanes // GROUP, (n + 1) * piece_lanes // GROUP):
            at = slice(g * GROUP, (g + 1) * GROUP)
            total = shp[0, :, at].astype(f32) * scales[0]
            for l in range(1, channels):
                total = total + shp[l, :, at].astype(f32) * scales[l]
            v0[:, at] = total
        for k, lane, there, lanes in cuts[n]:
            step = -plan[k][6]
            copy = pltpu.make_async_remote_copy(
                src_ref=v0.at[:, pl.ds(lane, lanes)],
                dst_ref=blocks[k].at[:, pl.ds(there, lanes)],
                send_sem=vs_sem.at[sent], recv_sem=vr_sem.at[sent],
                device_id=(j, d + step), device_id_type=MESH,
            )
            block_copies[k].append(copy)
            sent += 1

            @pl.when(inside[step])
            def _(copy=copy):
                copy.start()

    line_masks = []
    for h in range(2):
        lane = iota((LINES, SPAN), 1) + 128 * h
        line_masks.append(((lane * 2731) >> 16) == iota((LINES, SPAN), 0) + LINES * h)
    k_rows, k_lanes = iota((SPAN, 128), 0), iota((SPAN, 128), 1)
    for h in range(2):
        k_rows_h = k_rows + 128 * h
        shift = k_lanes - (k_rows_h - ((k_rows_h * 2731) >> 16) * SBZ)
        for s in range(4):
            unfolder[h, s] = jnp.where(shift == SLOT_LANES * s, 1.0, 0.0).astype(bf16)

    def offset_of(k, row, s):
        return off[row, s] if k == 0 else offs[k, row, s]

    def unfold(which):
        starts = []
        total = 0
        for k in which:
            starts.append(total)
            width = plan[k][1] * GROUP
            high, low = split(blocks[k][...])
            vh[:, total : total + width] = high
            vl[:, total : total + width] = low
            total += width
        groups = total // GROUP

        def one(s, carry):
            for h in range(2):
                for t, source in enumerate((vh, vl)):
                    pieces = []
                    for g in range(groups):
                        at = g * GROUP + 128 * h
                        line = source[pl.ds(s, 1), at : at + SPAN]
                        pieces.append(
                            jnp.where(line_masks[h], jnp.broadcast_to(line, (LINES, SPAN)), 0.0)
                        )
                    lane = pl.multiple_of(s * (2 * SPAN) + t * SPAN, SPAN)
                    wide[h, : groups * LINES, pl.ds(lane, SPAN)] = jnp.concatenate(
                        pieces, axis=0
                    ).astype(bf16)
            return carry

        lax.fori_loop(0, slots, one, 0, unroll=2)
        halves = []
        for h in range(2):
            right = []
            for s in range(4):
                right += [unfolder[h, s]] * 2
            right = jnp.concatenate(right, axis=0)
            value = [
                jnp.dot(
                    wide[h, : groups * LINES, t * 8 * SPAN : (t + 1) * 8 * SPAN], right,
                    preferred_element_type=f32,
                )
                for t in range(2)
            ]
            value = jnp.concatenate(value, axis=1)
            halves.append(value.reshape(groups, LINES, SPAN))
        lines = jnp.stack(halves, axis=1).reshape(groups * 2 * LINES, SPAN)
        for k, start in zip(which, starts):
            na = plan[k][2]
            at = start // GROUP * 2 * LINES
            high, low = split(lines[at : at + na * SBY].reshape(na, SBY, SPAN))
            folded[k][0:na] = jnp.concatenate([high, low], axis=1).astype(bf16)
            folded[k][na] = jnp.zeros((2 * SBY, SPAN), bf16)

    lane_tile = iota((16, 128), 1) >> 5
    slot_masks = []
    for s in range(4):
        mask = jnp.where(lane_tile == s, 1.0, 0.0).astype(bf16)
        slot_masks.append(jnp.concatenate([mask] * 3, axis=0))

    def place(k, first):
        _, _, na, a0, x0, rows, slab = plan[k]
        rows += rows % 2
        width = 4 * 2 * SBY
        lane = iota((1, width), 1)
        in_slot = (lane * 1366) >> 16
        b = lane - ((lane * 2731) >> 16) * SBY
        picks = []
        for h in range(2):
            target = b
            for s in range(4):
                target = target + jnp.where(in_slot == s, offset_of(k, 1, 4 * h + s), 0)
            picks.append(
                jnp.where(iota((fw, width), 0) + ystart == target, 1.0, 0.0).astype(bf16)
            )

        def one(i, carry):
            halves = []
            for h in range(2):
                columns = []
                for step in range(2):
                    local = x0 + 2 * i + step - slab * fx - a0
                    pieces = []
                    for s in range(4):
                        at = local - offset_of(k, 0, 4 * h + s)
                        at = jnp.where(jnp.logical_and(at >= 0, at < na), at, na)
                        pieces.append(folded[k][at, :, 128 * h : 128 * h + 128] * slot_masks[s])
                    columns.append(jnp.concatenate(pieces, axis=0))
                halves.append(jnp.dot(
                    picks[h], jnp.concatenate(columns, axis=1), preferred_element_type=f32
                ))
            parts = []
            for step in range(2):
                at = slice(128 * step, 128 * step + 128)
                value = jnp.concatenate([halves[0][:, at], halves[1][:, at]], axis=1)
                parts.append(jnp.concatenate(split(value), axis=1))
            lined[pl.ds(pl.multiple_of(i * (2 * fw), 2 * fw), 2 * fw), :] = jnp.concatenate(
                parts, axis=0
            ).astype(bf16)
            return carry

        lax.fori_loop(0, rows // 2, one, 0, unroll=2 if rows % 4 == 0 else 1)
        lane_row = iota((SPAN, fz), 0)
        depth = lane_row & (SLOT_LANES - 1)
        for s in range(slots):
            depth = depth + jnp.where((lane_row >> 5) == s, offset_of(k, 2, s), 0)
        inside_line = (lane_row & (SLOT_LANES - 1)) < SBZ
        hit = jnp.logical_and(inside_line, iota((SPAN, fz), 1) == depth)
        pick = jnp.where(hit, 1.0, 0.0).astype(bf16)
        pick = jnp.concatenate([pick, pick], axis=0)
        for start in range(0, rows, 4):
            size = min(4, rows - start)
            value = jnp.dot(
                lined[start * fw : (start + size) * fw, :], pick, preferred_element_type=f32
            ).reshape(size, fw, fz)
            at = x0 + HALO + start
            if first:
                dens[at : at + size] = value
            else:
                dens[at : at + size] = dens[at : at + size] + value

    dens[0:HALO] = jnp.zeros((HALO, fw, fz), f32)
    unfold((0,))
    place(0, True)

    own.wait()
    for copy in part_copies:
        copy.wait_recv()
    total = win[...]
    for k in range(1, G):
        total = total + recv[k - 1]
    cext[2 : cx + 2, 8 : 8 + yc] = total
    rows_from = {-1: pl.ds(2, 2), 0: pl.ds(2, cx), 1: pl.ds(cx, 2)}
    rows_to = {-1: pl.ds(cx + 2, 2), 0: pl.ds(2, cx), 1: pl.ds(0, 2)}
    cols_from = {-1: pl.ds(8, 8), 0: pl.ds(8, yc), 1: pl.ds(yc, 8)}
    cols_to = {-1: pl.ds(yc + 8, 8), 0: pl.ds(8, yc), 1: pl.ds(0, 8)}
    halo_copies = {}
    for n, (dj, dd) in enumerate(sides):
        halo_copies[dj, dd] = pltpu.make_async_remote_copy(
            src_ref=cext.at[rows_from[dd], cols_from[dj]],
            dst_ref=cext.at[rows_to[dd], cols_to[dj]],
            send_sem=cs_sem.at[n], recv_sem=cr_sem.at[n],
            device_id=(j + dj, d + dd), device_id_type=MESH,
        )

        @pl.when(beside[dj, dd])
        def _(dj=dj, dd=dd):
            halo_copies[dj, dd].start()

    for k in (1, 2, 3):

        @pl.when(inside[plan[k][6]])
        def _(k=k):
            offset_copies[k].wait_recv()
            for copy in block_copies[k]:
                copy.wait_recv()

        @pl.when(jnp.logical_not(inside[plan[k][6]]))
        def _(k=k):
            blocks[k][...] = jnp.zeros(blocks[k].shape, f32)
            for row in range(3):
                for s in range(slots):
                    offs[k, row, s] = 0

    unfold((1, 2, 3))

    for k in (1, 2, 3):
        place(k, False)

    for dj, dd in sides:

        @pl.when(beside[-dj, -dd])
        def _(dj=dj, dd=dd):
            halo_copies[dj, dd].wait_recv()

    count_x = fx + 2 * HALO
    zi, zo = iota((cz, fz), 0), iota((cz, fz), 1)
    zm = zo >> 1
    zn = zm + ((zo & 1) << 1) - 1
    refine_z = weights((cz, fz), ((zi == zm, 0.75), (zi == zn, 0.25))).astype(bf16)
    refine_z = jnp.concatenate([refine_z, refine_z], axis=0)
    yo = iota((fw, yw), 0) + ystart
    yi = iota((fw, yw), 1) + (yc * q - 8)
    ym = yo >> 1
    yn = ym + ((yo & 1) << 1) - 1
    grid = jnp.logical_and(yo >= 0, yo < fy)
    refine_y = weights(
        (fw, yw), ((jnp.logical_and(grid, yi == ym), 0.75), (jnp.logical_and(grid, yi == yn), 0.25))
    )
    refine_y = jnp.concatenate([refine_y, refine_y], axis=1).astype(bf16)

    def in_grid(x):
        g = d * fx + x
        return jnp.where(jnp.logical_and(g >= 0, g < N * fx), 1.0, 0.0).astype(f32)

    def refine_pair(i, carry):
        low_cell, high_cell = cext[i], cext[i + 1]
        odd = 0.75 * low_cell + 0.25 * high_cell
        even = 0.75 * high_cell + 0.25 * low_cell
        both = jnp.concatenate([odd, even], axis=1)
        right = jnp.concatenate(split(both), axis=0).astype(bf16)
        value = jnp.dot(refine_y, right, preferred_element_type=f32)
        value = jnp.concatenate([value[:, :cz], value[:, cz:]], axis=0)
        lined_coarse[pl.ds(pl.multiple_of(i * (2 * fw), 2 * fw), 2 * fw), :] = jnp.concatenate(
            split(value), axis=1
        ).astype(bf16)
        return carry

    lax.fori_loop(0, count_x // 2, refine_pair, 0, unroll=3)
    for start in range(0, count_x, 3):
        value = jnp.dot(
            lined_coarse[start * fw : (start + 3) * fw, :], refine_z, preferred_element_type=f32
        ).reshape(3, fw, fz)
        for i in range(3):
            dens[start + i] = (dens[start + i] + value[i]) * in_grid(start + i - HALO)

    lanes = iota((fw, fz), 1)
    first_lane, last_lane = lanes == 0, lanes == fz - 1

    def diff_z(f):
        after = jnp.where(last_lane, 0.0, pltpu.roll(f, fz - 1, 1))
        before = jnp.where(first_lane, 0.0, pltpu.roll(f, 1, 1))
        return after - before

    def diff_y(f):
        return pltpu.roll(f, fw - 1, 0) - pltpu.roll(f, 1, 0)

    def exchange_row(i, carry):
        n = dens[i + 1]
        gx = dens[i + 2] - dens[i]
        gy = diff_y(n)
        gz = diff_z(n)
        sigma = gx * gx + gy * gy + gz * gz
        live = n > 0.0
        log_n = jnp.log(jnp.where(live, n, 1.0))
        cube_root = jnp.exp(log_n * (1.0 / 3.0))
        inv_ft = jnp.exp(log_n * (-4.0 / 3.0))
        reduced = sigma * (inv_ft * inv_ft) * (half_inverse * half_inverse / gradient_scale)
        inv_d = 1.0 / (1.0 + (mu_pbe / kappa_pbe) * reduced)
        slope = mu_pbe * inv_d * inv_d
        by_density = (exchange_prefactor * cube_root) * (
            (4.0 / 3.0) * (1.0 + kappa_pbe - kappa_pbe * inv_d) - (8.0 / 3.0) * reduced * slope
        )
        twice = jnp.where(live, (2.0 * exchange_prefactor * half_inverse * half_inverse / gradient_scale) * slope * inv_ft, 0.0)
        flux[i] = twice * gx
        pot[i] = by_density - (diff_y(twice * gy) + diff_z(twice * gz))
        return carry


    ro, ri = iota((yc, fw), 0), iota((yc, fw), 1)
    at = ri - 4 - 2 * ro
    grid = jnp.logical_and(ri + ystart >= 0, ri + ystart < fy)
    inner = jnp.logical_and(grid, jnp.logical_or(at == 0, at == 1))
    outer = jnp.logical_and(grid, jnp.logical_or(at == -1, at == 2))
    restrict_y = weights((yc, fw), ((inner, 0.375), (outer, 0.125)))
    restrict_y = jnp.concatenate([restrict_y, restrict_y], axis=1).astype(bf16)
    at = iota((fz, cz), 0) - 2 * iota((fz, cz), 1)
    inner = jnp.logical_or(at == 0, at == 1)
    outer = jnp.logical_or(at == -1, at == 2)
    restrict_z = weights((fz, cz), ((inner, 0.375), (outer, 0.125))).astype(bf16)
    restrict_z = jnp.concatenate([restrict_z, restrict_z], axis=0)

    def full(x):
        return (pot[x + 2] - (flux[x + 3] - flux[x + 1])) * in_grid(x)

    ymine = pl.multiple_of(q * yc, 8)

    def restrict_rows(low_row, high_row):
        pieces = []
        for i in range(low_row, high_row):
            x = 2 * i
            mixed = 0.125 * (full(x - 1) + full(x + 2)) + 0.375 * (full(x) + full(x + 1))
            high, low = split(mixed)
            pieces.append(jnp.dot(
                restrict_y,
                jnp.concatenate([high, low], axis=0).astype(bf16),
                preferred_element_type=f32,
            ))
        high, low = split(jnp.concatenate(pieces, axis=0))
        result = jnp.dot(
            jnp.concatenate([high, low], axis=1).astype(bf16), restrict_z, preferred_element_type=f32
        )
        mine[low_row:high_row] = result.reshape(high_row - low_row, yc, cz)

    gather = []
    keep = []
    done = 0
    for piece, (low_row, high_row) in enumerate(
        (cx * n // PIECES, cx * (n + 1) // PIECES) for n in range(PIECES)
    ):
        lax.fori_loop(done, 2 * high_row + 4, exchange_row, 0, unroll=2)
        done = 2 * high_row + 4
        restrict_rows(low_row, high_row)
        rows = pl.ds(low_row, high_row - low_row)
        at = (rows, pl.ds(ymine, yc), slice(None))
        for k in range(1, Q):
            copy = pltpu.make_async_remote_copy(
                src_ref=mine.at[rows],
                dst_ref=out.at[at],
                send_sem=gs_sem.at[piece, k - 1], recv_sem=gr_sem.at[piece, k - 1],
                device_id=(base + lax.rem(q + k, Q), d), device_id_type=MESH,
            )
            copy.start()
            gather.append(copy)
        copy = pltpu.make_async_copy(mine.at[rows], out.at[at], keep_sem.at[piece])
        copy.start()
        keep.append(copy)
    for copy in part_copies:
        copy.wait_send()
    for k in (1, 2, 3):

        @pl.when(inside[-plan[k][6]])
        def _(k=k):
            offset_copies[k].wait_send()
            for copy in block_copies[k]:
                copy.wait_send()

    for dj, dd in sides:

        @pl.when(beside[dj, dd])
        def _(dj=dj, dd=dd):
            halo_copies[dj, dd].wait_send()

    for copy in gather + keep:
        copy.wait()


def body(G, N, Q, partial_density, moments, shape_functions, sphere_offsets, owned_count):
    _, cx, cy, cz = partial_density.shape
    slots, channels, block = shape_functions.shape
    fx, fz = 2 * cx, 2 * cz
    yc = cy // Q
    yw, fw = yc + 16, 2 * yc + 8
    plan = sources(fx)
    hbm = pl.BlockSpec(memory_space=pl.ANY)
    return pl.pallas_call(
        functools.partial(kernel, G, N, Q),
        out_shape=jax.ShapeDtypeStruct((cx, cy, cz), f32),
        in_specs=[hbm] * 5,
        out_specs=hbm,
        scratch_shapes=[
            pltpu.VMEM((slots, channels), bf16),
            pltpu.SMEM(sphere_offsets.shape, jnp.int32),
            pltpu.SMEM((1,), jnp.int32),
            pltpu.VMEM((channels, slots, block), bf16),
            pltpu.VMEM((cx, yc, cz), f32),
            pltpu.VMEM((G - 1, cx, yc, cz), f32),
            pltpu.VMEM((cx + 4, yw, cz), f32),
        ]
        + [pltpu.VMEM((slots, p[1] * GROUP), f32) for p in plan]
        + [pltpu.VMEM((slots, 26 * GROUP), f32)] * 2
        + [pltpu.SMEM((4,) + sphere_offsets.shape, jnp.int32)]
        + [pltpu.VMEM((2, 4, SPAN, 128), bf16), pltpu.VMEM((2, 26 * LINES, slots * 2 * SPAN), bf16)]
        + [pltpu.VMEM((p[2] + 1, 2 * SBY, SPAN), bf16) for p in plan]
        + [
            pltpu.VMEM(((fx + 4) * fw, 2 * SPAN), bf16),
            pltpu.VMEM(((fx + 2 * HALO) * fw, 2 * cz), bf16),
            pltpu.VMEM((fx + 2 * HALO + 1, fw, fz), f32),
            pltpu.VMEM((fx + 4, fw, fz), f32),
            pltpu.VMEM((fx + 4, fw, fz), f32),
            pltpu.VMEM((cx, yc, cz), f32),
            pltpu.SemaphoreType.DMA((3,)),
            pltpu.SemaphoreType.DMA((PIECES,)),
            pltpu.SemaphoreType.DMA(()),
            pltpu.SemaphoreType.DMA((G - 1,)),
            pltpu.SemaphoreType.DMA((G - 1,)),
            pltpu.SemaphoreType.DMA((8,)),
            pltpu.SemaphoreType.DMA((8,)),
            pltpu.SemaphoreType.DMA((PIECES + 2,)),
            pltpu.SemaphoreType.DMA((PIECES + 2,)),
            pltpu.SemaphoreType.DMA((4,)),
            pltpu.SemaphoreType.DMA((4,)),
            pltpu.SemaphoreType.DMA((PIECES, Q - 1)),
            pltpu.SemaphoreType.DMA((PIECES, Q - 1)),
            pltpu.SemaphoreType.DMA((PIECES,)),
        ],
        compiler_params=pltpu.CompilerParams(
            collective_id=0, has_side_effects=True, vmem_limit_bytes=58 * 1024 * 1024
        ),
    )(partial_density, moments.T, shape_functions.transpose(1, 0, 2), sphere_offsets, owned_count)


def solution(mesh):
    G, N = mesh.shape["band"], mesh.shape["dom"]

    def run(partial_density, *rest):
        cy = partial_density.shape[2]
        Q = max(c for c in range(1, G + 1) if G % c == 0 and cy % (8 * c) == 0)
        return jax.shard_map(
            functools.partial(body, G, N, Q),
            mesh=mesh,
            in_specs=(
                P("band", "dom", None, None),
                P(None, "dom"),
                P("dom", None, None),
                P(None, "dom"),
                P("dom"),
            ),
            out_specs=P("dom", None, None),
            check_vma=False,
        )(partial_density, *rest)

    return run
```

```python
import functools

import jax
import jax.numpy as jnp
from jax import lax
from jax.experimental import pallas as pl
from jax.experimental.pallas import tpu as pltpu
from jax.sharding import PartitionSpec as P

SBX = 12
SBY = 24
SBZ = 24
GROUP = 384
LINES = 8
SPAN = 256
SLOT_LANES = 32
PIECES = 3
HALO = 3

kappa_pbe = 0.804
mu_pbe = 0.2195
exchange_prefactor = -0.75 * (3.0 / 3.141592653589793) ** (1.0 / 3.0)
gradient_scale = 4.0 * (3.0 * 3.141592653589793**2) ** (2.0 / 3.0)
half_inverse = 0.5 / 0.2
log2_e = 1.4426950408889634

f32 = jnp.float32
bf16 = jnp.bfloat16
MESH = pl.DeviceIdType.MESH


def iota(shape, dim):
    return lax.broadcasted_iota(jnp.int32, shape, dim)


def split(x):
    high = x.astype(bf16).astype(f32)
    return high, x - high


def weights(shape, terms):
    total = jnp.zeros(shape, f32)
    for mask, value in terms:
        total = jnp.where(mask, value, total)
    return total


def sources(fx):
    return (
        (0, 18, SBX, 0, 0, fx + HALO, 0),
        (0, 18, SBX, 0, -HALO, SBX - 1 + HALO, -1),
        (5760, 3, 2, 10, -HALO, 2, -2),
        (0, 5, 3, 0, fx, HALO, 1),
    )


def kernel(
    G, N, Q,
    part, mom_hbm, shp_hbm, off_hbm, cnt_hbm,
    out,
    mom, off, cnt, shp, win, recv, cext, v0, v1, v2, v3, vh, vl, offs, unfolder, wide, u0, u1, u2, u3, lined, lined_coarse, dens, flux, pot, mine,
    small_sem, shp_sem, win_sem, ps_sem, pr_sem, cs_sem, cr_sem, vs_sem, vr_sem, os_sem, or_sem, gs_sem, gr_sem, keep_sem,
):
    _, cx, cy, cz = part.shape
    fx, fy, fz = 2 * cx, 2 * cy, 2 * cz
    yc = cy // Q
    yw = yc + 16
    fw = 2 * yc + 8
    j = lax.axis_index("band")
    d = lax.axis_index("dom")
    q = lax.rem(j, Q)

    def chunk_of(index):
        return pl.ds(pl.multiple_of(lax.rem(index, Q) * yc, 8), yc)

    own = pltpu.make_async_copy(part.at[0, :, chunk_of(j), :], win, win_sem)
    own.start()
    small = []
    for n, (source, target) in enumerate(((mom_hbm, mom), (off_hbm, off), (cnt_hbm, cnt))):
        small.append(pltpu.make_async_copy(source, target, small_sem.at[n]))
        small[-1].start()
    piece_lanes = shp.shape[2] // PIECES
    fetches = []
    for n in range(PIECES):
        at = (slice(None), slice(None), pl.ds(n * piece_lanes, piece_lanes))
        fetches.append(pltpu.make_async_copy(shp_hbm.at[at], shp.at[at], shp_sem.at[n]))
        fetches[-1].start()
    cext[...] = jnp.zeros(cext.shape, f32)
    base = j - q
    ystart = 2 * yc * q - 4
    slots = shp.shape[1]

    barrier = pltpu.get_barrier_semaphore()
    for k in range(1, G):
        pl.semaphore_signal(barrier, inc=1, device_id=(lax.rem(j + k, G), d), device_id_type=MESH)
    inside = {}
    for step in (-2, -1, 1, 2):
        inside[step] = jnp.logical_and(d + step >= 0, d + step < N)

        @pl.when(inside[step])
        def _(step=step):
            pl.semaphore_signal(barrier, inc=1, device_id=(j, d + step), device_id_type=MESH)

    sides = [(dj, dd) for dj in (-1, 0, 1) for dd in (-1, 0, 1) if dj or dd]
    beside = {}
    for dj, dd in sides:
        there = jnp.logical_and(q + dj >= 0, q + dj < Q)
        if dd:
            there = jnp.logical_and(there, inside[dd])
        beside[dj, dd] = there
        if dj and dd:

            @pl.when(there)
            def _(dj=dj, dd=dd):
                pl.semaphore_signal(barrier, inc=1, device_id=(j + dj, d + dd), device_id_type=MESH)

    count = G - 1
    for there in [inside[step] for step in (-2, -1, 1, 2)] + [
        beside[dj, dd] for dj, dd in sides if dj and dd
    ]:
        count = count + jnp.where(there, 1, 0)
    pl.semaphore_wait(barrier, count)

    part_copies = []
    for k in range(1, G):
        peer = lax.rem(j + k, G)
        copy = pltpu.make_async_remote_copy(
            src_ref=part.at[0, :, chunk_of(peer), :],
            dst_ref=recv.at[k - 1],
            send_sem=ps_sem.at[k - 1],
            recv_sem=pr_sem.at[k - 1],
            device_id=(peer, d),
            device_id_type=MESH,
        )
        copy.start()
        part_copies.append(copy)

    channels = shp.shape[0]
    for copy in small:
        copy.wait()
    plan = sources(fx)
    blocks = (v0, v1, v2, v3)
    folded = (u0, u1, u2, u3)
    offset_copies = [None]
    for k in (1, 2, 3):
        step = -plan[k][6]
        offset_copies.append(pltpu.make_async_remote_copy(
            src_ref=off,
            dst_ref=offs.at[k],
            send_sem=os_sem.at[k], recv_sem=or_sem.at[k],
            device_id=(j, d + step), device_id_type=MESH,
        ))

        @pl.when(inside[step])
        def _(k=k):
            offset_copies[k].start()

    last = shp.shape[2] - plan[2][1] * GROUP
    cuts = [[(1, n * piece_lanes, n * piece_lanes, piece_lanes)] for n in range(PIECES)]
    cuts[0].append((3, 0, 0, plan[3][1] * GROUP))
    cuts[PIECES - 1].append((2, last, 0, plan[2][1] * GROUP))
    block_copies = {1: [], 2: [], 3: []}
    moments = mom[...].astype(f32)
    moments = jnp.where(iota(moments.shape, 0) < cnt[0], moments, 0.0)
    scales = [jnp.broadcast_to(moments[:, l : l + 1], (slots, GROUP)) for l in range(channels)]
    sent = 0
    for n in range(PIECES):
        fetches[n].wait()
        for g in range(n * piece_lanes // GROUP, (n + 1) * piece_lanes // GROUP):
            at = slice(g * GROUP, (g + 1) * GROUP)
            total = shp[0, :, at].astype(f32) * scales[0]
            for l in range(1, channels):
                total = total + shp[l, :, at].astype(f32) * scales[l]
            v0[:, at] = total
        for k, lane, there, lanes in cuts[n]:
            step = -plan[k][6]
            copy = pltpu.make_async_remote_copy(
                src_ref=v0.at[:, pl.ds(lane, lanes)],
                dst_ref=blocks[k].at[:, pl.ds(there, lanes)],
                send_sem=vs_sem.at[sent], recv_sem=vr_sem.at[sent],
                device_id=(j, d + step), device_id_type=MESH,
            )
            block_copies[k].append(copy)
            sent += 1

            @pl.when(inside[step])
            def _(copy=copy):
                copy.start()

    line_masks = []
    for h in range(2):
        lane = iota((LINES, SPAN), 1) + 128 * h
        line_masks.append(((lane * 2731) >> 16) == iota((LINES, SPAN), 0) + LINES * h)
    k_rows, k_lanes = iota((SPAN, 128), 0), iota((SPAN, 128), 1)
    for h in range(2):
        k_rows_h = k_rows + 128 * h
        shift = k_lanes - (k_rows_h - ((k_rows_h * 2731) >> 16) * SBZ)
        for s in range(4):
            unfolder[h, s] = jnp.where(shift == SLOT_LANES * s, 1.0, 0.0).astype(bf16)

    def offset_of(k, row, s):
        return off[row, s] if k == 0 else offs[k, row, s]

    def unfold(which):
        starts = []
        total = 0
        for k in which:
            starts.append(total)
            width = plan[k][1] * GROUP
            high, low = split(blocks[k][...])
            vh[:, total : total + width] = high
            vl[:, total : total + width] = low
            total += width
        groups = total // GROUP

        def one(s, carry):
            for h in range(2):
                for t, source in enumerate((vh, vl)):
                    pieces = []
                    for g in range(groups):
                        at = g * GROUP + 128 * h
                        line = source[pl.ds(s, 1), at : at + SPAN]
                        pieces.append(
                            jnp.where(line_masks[h], jnp.broadcast_to(line, (LINES, SPAN)), 0.0)
                        )
                    lane = pl.multiple_of(s * (2 * SPAN) + t * SPAN, SPAN)
                    wide[h, : groups * LINES, pl.ds(lane, SPAN)] = jnp.concatenate(
                        pieces, axis=0
                    ).astype(bf16)
            return carry

        lax.fori_loop(0, slots, one, 0, unroll=2)
        halves = []
        for h in range(2):
            right = []
            for s in range(4):
                right += [unfolder[h, s]] * 2
            right = jnp.concatenate(right, axis=0)
            value = [
                jnp.dot(
                    wide[h, : groups * LINES, t * 8 * SPAN : (t + 1) * 8 * SPAN], right,
                    preferred_element_type=f32,
                )
                for t in range(2)
            ]
            value = jnp.concatenate(value, axis=1)
            halves.append(value.reshape(groups, LINES, SPAN))
        lines = jnp.stack(halves, axis=1).reshape(groups * 2 * LINES, SPAN)
        for k, start in zip(which, starts):
            na = plan[k][2]
            at = start // GROUP * 2 * LINES
            high, low = split(lines[at : at + na * SBY].reshape(na, SBY, SPAN))
            folded[k][0:na] = jnp.concatenate([high, low], axis=1).astype(bf16)
            folded[k][na] = jnp.zeros((2 * SBY, SPAN), bf16)

    lane_tile = iota((16, 128), 1) >> 5
    slot_masks = []
    for s in range(4):
        mask = jnp.where(lane_tile == s, 1.0, 0.0).astype(bf16)
        slot_masks.append(jnp.concatenate([mask] * 3, axis=0))

    def place(k, first):
        _, _, na, a0, x0, rows, slab = plan[k]
        rows += rows % 2
        width = 4 * 2 * SBY
        lane = iota((1, width), 1)
        in_slot = (lane * 1366) >> 16
        b = lane - ((lane * 2731) >> 16) * SBY
        picks = []
        for h in range(2):
            target = b
            for s in range(4):
                target = target + jnp.where(in_slot == s, offset_of(k, 1, 4 * h + s), 0)
            picks.append(
                jnp.where(iota((fw, width), 0) + ystart == target, 1.0, 0.0).astype(bf16)
            )

        def one(i, carry):
            halves = []
            for h in range(2):
                columns = []
                for step in range(2):
                    local = x0 + 2 * i + step - slab * fx - a0
                    pieces = []
                    for s in range(4):
                        at = local - offset_of(k, 0, 4 * h + s)
                        at = jnp.where(jnp.logical_and(at >= 0, at < na), at, na)
                        pieces.append(folded[k][at, :, 128 * h : 128 * h + 128] * slot_masks[s])
                    columns.append(jnp.concatenate(pieces, axis=0))
                halves.append(jnp.dot(
                    picks[h], jnp.concatenate(columns, axis=1), preferred_element_type=f32
                ))
            parts = []
            for step in range(2):
                at = slice(128 * step, 128 * step + 128)
                value = jnp.concatenate([halves[0][:, at], halves[1][:, at]], axis=1)
                parts.append(jnp.concatenate(split(value), axis=1))
            lined[pl.ds(pl.multiple_of(i * (2 * fw), 2 * fw), 2 * fw), :] = jnp.concatenate(
                parts, axis=0
            ).astype(bf16)
            return carry

        lax.fori_loop(0, rows // 2, one, 0, unroll=2 if rows % 4 == 0 else 1)
        lane_row = iota((SPAN, fz), 0)
        depth = lane_row & (SLOT_LANES - 1)
        for s in range(slots):
            depth = depth + jnp.where((lane_row >> 5) == s, offset_of(k, 2, s), 0)
        inside_line = (lane_row & (SLOT_LANES - 1)) < SBZ
        hit = jnp.logical_and(inside_line, iota((SPAN, fz), 1) == depth)
        pick = jnp.where(hit, 1.0, 0.0).astype(bf16)
        pick = jnp.concatenate([pick, pick], axis=0)
        for start in range(0, rows, 4):
            size = min(4, rows - start)
            value = jnp.dot(
                lined[start * fw : (start + size) * fw, :], pick, preferred_element_type=f32
            ).reshape(size, fw, fz)
            at = x0 + HALO + start
            if first:
                dens[at : at + size] = value
            else:
                dens[at : at + size] = dens[at : at + size] + value

    dens[0:HALO] = jnp.zeros((HALO, fw, fz), f32)
    unfold((0,))
    place(0, True)

    own.wait()
    for copy in part_copies:
        copy.wait_recv()
    total = win[...]
    for k in range(1, G):
        total = total + recv[k - 1]
    cext[2 : cx + 2, 8 : 8 + yc] = total
    rows_from = {-1: pl.ds(2, 2), 0: pl.ds(2, cx), 1: pl.ds(cx, 2)}
    rows_to = {-1: pl.ds(cx + 2, 2), 0: pl.ds(2, cx), 1: pl.ds(0, 2)}
    cols_from = {-1: pl.ds(8, 8), 0: pl.ds(8, yc), 1: pl.ds(yc, 8)}
    cols_to = {-1: pl.ds(yc + 8, 8), 0: pl.ds(8, yc), 1: pl.ds(0, 8)}
    halo_copies = {}
    for n, (dj, dd) in enumerate(sides):
        halo_copies[dj, dd] = pltpu.make_async_remote_copy(
            src_ref=cext.at[rows_from[dd], cols_from[dj]],
            dst_ref=cext.at[rows_to[dd], cols_to[dj]],
            send_sem=cs_sem.at[n], recv_sem=cr_sem.at[n],
            device_id=(j + dj, d + dd), device_id_type=MESH,
        )

        @pl.when(beside[dj, dd])
        def _(dj=dj, dd=dd):
            halo_copies[dj, dd].start()

    for k in (1, 2, 3):

        @pl.when(inside[plan[k][6]])
        def _(k=k):
            offset_copies[k].wait_recv()
            for copy in block_copies[k]:
                copy.wait_recv()

        @pl.when(jnp.logical_not(inside[plan[k][6]]))
        def _(k=k):
            blocks[k][...] = jnp.zeros(blocks[k].shape, f32)
            for row in range(3):
                for s in range(slots):
                    offs[k, row, s] = 0

    unfold((1, 2, 3))

    for k in (1, 2, 3):
        place(k, False)

    for dj, dd in sides:

        @pl.when(beside[-dj, -dd])
        def _(dj=dj, dd=dd):
            halo_copies[dj, dd].wait_recv()

    count_x = fx + 2 * HALO
    zi, zo = iota((cz, fz), 0), iota((cz, fz), 1)
    zm = zo >> 1
    zn = zm + ((zo & 1) << 1) - 1
    refine_z = weights((cz, fz), ((zi == zm, 0.75), (zi == zn, 0.25))).astype(bf16)
    refine_z = jnp.concatenate([refine_z, refine_z], axis=0)
    yo = iota((fw, yw), 0) + ystart
    yi = iota((fw, yw), 1) + (yc * q - 8)
    ym = yo >> 1
    yn = ym + ((yo & 1) << 1) - 1
    grid = jnp.logical_and(yo >= 0, yo < fy)
    refine_y = weights(
        (fw, yw), ((jnp.logical_and(grid, yi == ym), 0.75), (jnp.logical_and(grid, yi == yn), 0.25))
    )
    refine_y = jnp.concatenate([refine_y, refine_y], axis=1).astype(bf16)

    def in_grid(x):
        g = d * fx + x
        return jnp.where(jnp.logical_and(g >= 0, g < N * fx), 1.0, 0.0).astype(f32)

    def refine_pair(i, carry):
        low_cell, high_cell = cext[i], cext[i + 1]
        odd = 0.75 * low_cell + 0.25 * high_cell
        even = 0.75 * high_cell + 0.25 * low_cell
        both = jnp.concatenate([odd, even], axis=1)
        right = jnp.concatenate(split(both), axis=0).astype(bf16)
        value = jnp.dot(refine_y, right, preferred_element_type=f32)
        value = jnp.concatenate([value[:, :cz], value[:, cz:]], axis=0)
        lined_coarse[pl.ds(pl.multiple_of(i * (2 * fw), 2 * fw), 2 * fw), :] = jnp.concatenate(
            split(value), axis=1
        ).astype(bf16)
        return carry

    lax.fori_loop(0, count_x // 2, refine_pair, 0, unroll=3)
    for start in range(0, count_x, 3):
        value = jnp.dot(
            lined_coarse[start * fw : (start + 3) * fw, :], refine_z, preferred_element_type=f32
        ).reshape(3, fw, fz)
        for i in range(3):
            dens[start + i] = (dens[start + i] + value[i]) * in_grid(start + i - HALO)

    lanes = iota((fw, 128), 1)
    first_lane, last_lane = lanes == 0, lanes == 127
    tiles = fz // 128

    def diff_z(f):
        parts = [f[:, 128 * t : 128 * t + 128] for t in range(tiles)]
        ahead = [pltpu.roll(part, 127, 1) for part in parts] + [0.0]
        behind = [0.0] + [pltpu.roll(part, 1, 1) for part in parts]
        return jnp.concatenate(
            [
                jnp.where(last_lane, ahead[t + 1], ahead[t])
                - jnp.where(first_lane, behind[t], behind[t + 1])
                for t in range(tiles)
            ],
            axis=1,
        )

    def diff_y(f):
        return pltpu.roll(f, fw - 1, 0) - pltpu.roll(f, 1, 0)

    def exchange_row(i, carry):
        n = dens[i + 1]
        gx = dens[i + 2] - dens[i]
        gy = diff_y(n)
        gz = diff_z(n)
        sigma = gx * gx + gy * gy + gz * gz
        live = n > 0.0
        log_n = jnp.log(jnp.where(live, n, 1.0))
        cube_root = jnp.exp2(log_n * (log2_e / 3.0))
        inv_ft = jnp.exp2(log_n * (-4.0 * log2_e / 3.0))
        scale = half_inverse * half_inverse * mu_pbe / (kappa_pbe * gradient_scale)
        inv_d = 1.0 / (1.0 + sigma * (inv_ft * inv_ft * scale))
        inv_d2 = inv_d * inv_d
        by_density = cube_root * (
            exchange_prefactor * 4.0 / 3.0 * (1.0 + kappa_pbe)
            - (exchange_prefactor * 4.0 * kappa_pbe) * inv_d
            + (exchange_prefactor * 8.0 / 3.0 * kappa_pbe) * inv_d2
        )
        twice = 2.0 * exchange_prefactor * half_inverse * half_inverse * mu_pbe / gradient_scale
        twice = jnp.where(live, (twice * inv_ft) * inv_d2, 0.0)
        flux[i] = twice * gx
        pot[i] = by_density - (diff_y(twice * gy) + diff_z(twice * gz))
        return carry


    ro, ri = iota((yc, fw), 0), iota((yc, fw), 1)
    at = ri - 4 - 2 * ro
    grid = jnp.logical_and(ri + ystart >= 0, ri + ystart < fy)
    inner = jnp.logical_and(grid, jnp.logical_or(at == 0, at == 1))
    outer = jnp.logical_and(grid, jnp.logical_or(at == -1, at == 2))
    restrict_y = weights((yc, fw), ((inner, 0.375), (outer, 0.125)))
    restrict_y = jnp.concatenate([restrict_y, restrict_y], axis=1).astype(bf16)
    at = iota((fz, cz), 0) - 2 * iota((fz, cz), 1)
    inner = jnp.logical_or(at == 0, at == 1)
    outer = jnp.logical_or(at == -1, at == 2)
    restrict_z = weights((fz, cz), ((inner, 0.375), (outer, 0.125))).astype(bf16)
    restrict_z = jnp.concatenate([restrict_z, restrict_z], axis=0)

    def full(x):
        return (pot[x + 2] - (flux[x + 3] - flux[x + 1])) * in_grid(x)

    ymine = pl.multiple_of(q * yc, 8)

    def restrict_rows(low_row, high_row):
        pieces = []
        for i in range(low_row, high_row):
            x = 2 * i
            mixed = 0.125 * (full(x - 1) + full(x + 2)) + 0.375 * (full(x) + full(x + 1))
            high, low = split(mixed)
            pieces.append(jnp.dot(
                restrict_y,
                jnp.concatenate([high, low], axis=0).astype(bf16),
                preferred_element_type=f32,
            ))
        high, low = split(jnp.concatenate(pieces, axis=0))
        result = jnp.dot(
            jnp.concatenate([high, low], axis=1).astype(bf16), restrict_z, preferred_element_type=f32
        )
        mine[low_row:high_row] = result.reshape(high_row - low_row, yc, cz)

    gather = []
    keep = []
    done = 0
    for piece, (low_row, high_row) in enumerate(
        (cx * n // PIECES, cx * (n + 1) // PIECES) for n in range(PIECES)
    ):
        lax.fori_loop(done, 2 * high_row + 4, exchange_row, 0, unroll=2)
        done = 2 * high_row + 4
        restrict_rows(low_row, high_row)
        rows = pl.ds(low_row, high_row - low_row)
        at = (rows, pl.ds(ymine, yc), slice(None))
        for k in range(1, Q):
            copy = pltpu.make_async_remote_copy(
                src_ref=mine.at[rows],
                dst_ref=out.at[at],
                send_sem=gs_sem.at[piece, k - 1], recv_sem=gr_sem.at[piece, k - 1],
                device_id=(base + lax.rem(q + k, Q), d), device_id_type=MESH,
            )
            copy.start()
            gather.append(copy)
        copy = pltpu.make_async_copy(mine.at[rows], out.at[at], keep_sem.at[piece])
        copy.start()
        keep.append(copy)
    for copy in part_copies:
        copy.wait_send()
    for k in (1, 2, 3):

        @pl.when(inside[-plan[k][6]])
        def _(k=k):
            offset_copies[k].wait_send()
            for copy in block_copies[k]:
                copy.wait_send()

    for dj, dd in sides:

        @pl.when(beside[dj, dd])
        def _(dj=dj, dd=dd):
            halo_copies[dj, dd].wait_send()

    for copy in gather + keep:
        copy.wait()


def body(G, N, Q, partial_density, moments, shape_functions, sphere_offsets, owned_count):
    _, cx, cy, cz = partial_density.shape
    slots, channels, block = shape_functions.shape
    fx, fz = 2 * cx, 2 * cz
    yc = cy // Q
    yw, fw = yc + 16, 2 * yc + 8
    plan = sources(fx)
    hbm = pl.BlockSpec(memory_space=pl.ANY)
    return pl.pallas_call(
        functools.partial(kernel, G, N, Q),
        out_shape=jax.ShapeDtypeStruct((cx, cy, cz), f32),
        in_specs=[hbm] * 5,
        out_specs=hbm,
        scratch_shapes=[
            pltpu.VMEM((slots, channels), bf16),
            pltpu.SMEM(sphere_offsets.shape, jnp.int32),
            pltpu.SMEM((1,), jnp.int32),
            pltpu.VMEM((channels, slots, block), bf16),
            pltpu.VMEM((cx, yc, cz), f32),
            pltpu.VMEM((G - 1, cx, yc, cz), f32),
            pltpu.VMEM((cx + 4, yw, cz), f32),
        ]
        + [pltpu.VMEM((slots, p[1] * GROUP), f32) for p in plan]
        + [pltpu.VMEM((slots, 26 * GROUP), f32)] * 2
        + [pltpu.SMEM((4,) + sphere_offsets.shape, jnp.int32)]
        + [pltpu.VMEM((2, 4, SPAN, 128), bf16), pltpu.VMEM((2, 26 * LINES, slots * 2 * SPAN), bf16)]
        + [pltpu.VMEM((p[2] + 1, 2 * SBY, SPAN), bf16) for p in plan]
        + [
            pltpu.VMEM(((fx + 4) * fw, 2 * SPAN), bf16),
            pltpu.VMEM(((fx + 2 * HALO) * fw, 2 * cz), bf16),
            pltpu.VMEM((fx + 2 * HALO + 1, fw, fz), f32),
            pltpu.VMEM((fx + 4, fw, fz), f32),
            pltpu.VMEM((fx + 4, fw, fz), f32),
            pltpu.VMEM((cx, yc, cz), f32),
            pltpu.SemaphoreType.DMA((3,)),
            pltpu.SemaphoreType.DMA((PIECES,)),
            pltpu.SemaphoreType.DMA(()),
            pltpu.SemaphoreType.DMA((G - 1,)),
            pltpu.SemaphoreType.DMA((G - 1,)),
            pltpu.SemaphoreType.DMA((8,)),
            pltpu.SemaphoreType.DMA((8,)),
            pltpu.SemaphoreType.DMA((PIECES + 2,)),
            pltpu.SemaphoreType.DMA((PIECES + 2,)),
            pltpu.SemaphoreType.DMA((4,)),
            pltpu.SemaphoreType.DMA((4,)),
            pltpu.SemaphoreType.DMA((PIECES, Q - 1)),
            pltpu.SemaphoreType.DMA((PIECES, Q - 1)),
            pltpu.SemaphoreType.DMA((PIECES,)),
        ],
        compiler_params=pltpu.CompilerParams(
            collective_id=0, has_side_effects=True, vmem_limit_bytes=54900 * 1024
        ),
    )(partial_density, moments.T, shape_functions.transpose(1, 0, 2), sphere_offsets, owned_count)


def solution(mesh):
    G, N = mesh.shape["band"], mesh.shape["dom"]

    def run(partial_density, *rest):
        cy = partial_density.shape[2]
        Q = max(c for c in range(1, G + 1) if G % c == 0 and cy % (8 * c) == 0)
        return jax.shard_map(
            functools.partial(body, G, N, Q),
            mesh=mesh,
            in_specs=(
                P("band", "dom", None, None),
                P(None, "dom"),
                P("dom", None, None),
                P(None, "dom"),
                P("dom"),
            ),
            out_specs=P("dom", None, None),
            check_vma=False,
        )(partial_density, *rest)

    return run
```

```python
import functools

import jax
import jax.numpy as jnp
from jax import lax
from jax.experimental import pallas as pl
from jax.experimental.pallas import tpu as pltpu
from jax.sharding import PartitionSpec as P

SBX = 12
SBY = 24
SBZ = 24
GROUP = 384
LINES = 8
SPAN = 256
SLOT_LANES = 32
PIECES = 3
HALO = 3

kappa_pbe = 0.804
mu_pbe = 0.2195
exchange_prefactor = -0.75 * (3.0 / 3.141592653589793) ** (1.0 / 3.0)
gradient_scale = 4.0 * (3.0 * 3.141592653589793**2) ** (2.0 / 3.0)
half_inverse = 0.5 / 0.2
log2_e = 1.4426950408889634

f32 = jnp.float32
bf16 = jnp.bfloat16
MESH = pl.DeviceIdType.MESH


def iota(shape, dim):
    return lax.broadcasted_iota(jnp.int32, shape, dim)


def split(x):
    high = x.astype(bf16).astype(f32)
    return high, x - high


def weights(shape, terms):
    total = jnp.zeros(shape, f32)
    for mask, value in terms:
        total = jnp.where(mask, value, total)
    return total


def sources(fx):
    return (
        (0, 18, SBX, 0, 0, fx + HALO, 0),
        (0, 18, SBX, 0, -HALO, SBX - 1 + HALO, -1),
        (5760, 3, 2, 10, -HALO, 2, -2),
        (0, 5, 3, 0, fx, HALO, 1),
    )


def kernel(
    G, N, Q,
    part, mom_hbm, shp_hbm, off_hbm, cnt_hbm,
    out,
    mom, off, cnt, shp, win, recv, cext, v0, v1, v2, v3, vh, vl, offs, unfolder, wide, u0, u1, u2, u3, lined, lined_coarse, dens, flux, flux_y, pot, mine,
    small_sem, shp_sem, win_sem, ps_sem, pr_sem, cs_sem, cr_sem, vs_sem, vr_sem, os_sem, or_sem, gs_sem, gr_sem, keep_sem,
):
    _, cx, cy, cz = part.shape
    fx, fy, fz = 2 * cx, 2 * cy, 2 * cz
    yc = cy // Q
    yw = yc + 16
    fw = 2 * yc + 8
    j = lax.axis_index("band")
    d = lax.axis_index("dom")
    q = lax.rem(j, Q)

    def chunk_of(index):
        return pl.ds(pl.multiple_of(lax.rem(index, Q) * yc, 8), yc)

    own = pltpu.make_async_copy(part.at[0, :, chunk_of(j), :], win, win_sem)
    own.start()
    small = []
    for n, (source, target) in enumerate(((mom_hbm, mom), (off_hbm, off), (cnt_hbm, cnt))):
        small.append(pltpu.make_async_copy(source, target, small_sem.at[n]))
        small[-1].start()
    piece_lanes = shp.shape[2] // PIECES
    fetches = []
    for n in range(PIECES):
        at = (slice(None), slice(None), pl.ds(n * piece_lanes, piece_lanes))
        fetches.append(pltpu.make_async_copy(shp_hbm.at[at], shp.at[at], shp_sem.at[n]))
        fetches[-1].start()
    cext[...] = jnp.zeros(cext.shape, f32)
    for lines in (dens, flux_y):
        edge = jnp.zeros((lines.shape[0], 8, fz), f32)
        lines[:, 0:8] = edge
        lines[:, fw + 8 : fw + 16] = edge
    base = j - q
    ystart = 2 * yc * q - 4
    slots = shp.shape[1]

    barrier = pltpu.get_barrier_semaphore()
    for k in range(1, G):
        pl.semaphore_signal(barrier, inc=1, device_id=(lax.rem(j + k, G), d), device_id_type=MESH)
    inside = {}
    for step in (-2, -1, 1, 2):
        inside[step] = jnp.logical_and(d + step >= 0, d + step < N)

        @pl.when(inside[step])
        def _(step=step):
            pl.semaphore_signal(barrier, inc=1, device_id=(j, d + step), device_id_type=MESH)

    sides = [(dj, dd) for dj in (-1, 0, 1) for dd in (-1, 0, 1) if dj or dd]
    beside = {}
    for dj, dd in sides:
        there = jnp.logical_and(q + dj >= 0, q + dj < Q)
        if dd:
            there = jnp.logical_and(there, inside[dd])
        beside[dj, dd] = there
        if dj and dd:

            @pl.when(there)
            def _(dj=dj, dd=dd):
                pl.semaphore_signal(barrier, inc=1, device_id=(j + dj, d + dd), device_id_type=MESH)

    count = G - 1
    for there in [inside[step] for step in (-2, -1, 1, 2)] + [
        beside[dj, dd] for dj, dd in sides if dj and dd
    ]:
        count = count + jnp.where(there, 1, 0)
    pl.semaphore_wait(barrier, count)

    part_copies = []
    for k in range(1, G):
        peer = lax.rem(j + k, G)
        copy = pltpu.make_async_remote_copy(
            src_ref=part.at[0, :, chunk_of(peer), :],
            dst_ref=recv.at[k - 1],
            send_sem=ps_sem.at[k - 1],
            recv_sem=pr_sem.at[k - 1],
            device_id=(peer, d),
            device_id_type=MESH,
        )
        copy.start()
        part_copies.append(copy)

    channels = shp.shape[0]
    for copy in small:
        copy.wait()
    plan = sources(fx)
    blocks = (v0, v1, v2, v3)
    folded = (u0, u1, u2, u3)
    offset_copies = [None]
    for k in (1, 2, 3):
        step = -plan[k][6]
        offset_copies.append(pltpu.make_async_remote_copy(
            src_ref=off,
            dst_ref=offs.at[k],
            send_sem=os_sem.at[k], recv_sem=or_sem.at[k],
            device_id=(j, d + step), device_id_type=MESH,
        ))

        @pl.when(inside[step])
        def _(k=k):
            offset_copies[k].start()

    last = shp.shape[2] - plan[2][1] * GROUP
    cuts = [[(1, n * piece_lanes, n * piece_lanes, piece_lanes)] for n in range(PIECES)]
    cuts[0].append((3, 0, 0, plan[3][1] * GROUP))
    cuts[PIECES - 1].append((2, last, 0, plan[2][1] * GROUP))
    block_copies = {1: [], 2: [], 3: []}
    moments = mom[...].astype(f32)
    moments = jnp.where(iota(moments.shape, 0) < cnt[0], moments, 0.0)
    scales = [jnp.broadcast_to(moments[:, l : l + 1], (slots, GROUP)) for l in range(channels)]
    sent = 0
    for n in range(PIECES):
        fetches[n].wait()
        for g in range(n * piece_lanes // GROUP, (n + 1) * piece_lanes // GROUP):
            at = slice(g * GROUP, (g + 1) * GROUP)
            total = shp[0, :, at].astype(f32) * scales[0]
            for l in range(1, channels):
                total = total + shp[l, :, at].astype(f32) * scales[l]
            v0[:, at] = total
        for k, lane, there, lanes in cuts[n]:
            step = -plan[k][6]
            copy = pltpu.make_async_remote_copy(
                src_ref=v0.at[:, pl.ds(lane, lanes)],
                dst_ref=blocks[k].at[:, pl.ds(there, lanes)],
                send_sem=vs_sem.at[sent], recv_sem=vr_sem.at[sent],
                device_id=(j, d + step), device_id_type=MESH,
            )
            block_copies[k].append(copy)
            sent += 1

            @pl.when(inside[step])
            def _(copy=copy):
                copy.start()

    line_masks = []
    for h in range(2):
        lane = iota((LINES, SPAN), 1) + 128 * h
        line_masks.append(((lane * 2731) >> 16) == iota((LINES, SPAN), 0) + LINES * h)
    k_rows, k_lanes = iota((SPAN, 128), 0), iota((SPAN, 128), 1)
    for h in range(2):
        k_rows_h = k_rows + 128 * h
        shift = k_lanes - (k_rows_h - ((k_rows_h * 2731) >> 16) * SBZ)
        for s in range(4):
            unfolder[h, s] = jnp.where(shift == SLOT_LANES * s, 1.0, 0.0).astype(bf16)

    def offset_of(k, row, s):
        return off[row, s] if k == 0 else offs[k, row, s]

    def unfold(which):
        starts = []
        total = 0
        for k in which:
            starts.append(total)
            width = plan[k][1] * GROUP
            high, low = split(blocks[k][...])
            vh[:, total : total + width] = high
            vl[:, total : total + width] = low
            total += width
        groups = total // GROUP

        def one(s, carry):
            for h in range(2):
                for t, source in enumerate((vh, vl)):
                    pieces = []
                    for g in range(groups):
                        at = g * GROUP + 128 * h
                        line = source[pl.ds(s, 1), at : at + SPAN]
                        pieces.append(
                            jnp.where(line_masks[h], jnp.broadcast_to(line, (LINES, SPAN)), 0.0)
                        )
                    lane = pl.multiple_of(s * (2 * SPAN) + t * SPAN, SPAN)
                    wide[h, : groups * LINES, pl.ds(lane, SPAN)] = jnp.concatenate(
                        pieces, axis=0
                    ).astype(bf16)
            return carry

        lax.fori_loop(0, slots, one, 0, unroll=2)
        halves = []
        for h in range(2):
            right = []
            for s in range(4):
                right += [unfolder[h, s]] * 2
            right = jnp.concatenate(right, axis=0)
            value = [
                jnp.dot(
                    wide[h, : groups * LINES, t * 8 * SPAN : (t + 1) * 8 * SPAN], right,
                    preferred_element_type=f32,
                )
                for t in range(2)
            ]
            value = jnp.concatenate(value, axis=1)
            halves.append(value.reshape(groups, LINES, SPAN))
        lines = jnp.stack(halves, axis=1).reshape(groups * 2 * LINES, SPAN)
        for k, start in zip(which, starts):
            na = plan[k][2]
            at = start // GROUP * 2 * LINES
            high, low = split(lines[at : at + na * SBY].reshape(na, SBY, SPAN))
            folded[k][0:na] = jnp.concatenate([high, low], axis=1).astype(bf16)
            folded[k][na] = jnp.zeros((2 * SBY, SPAN), bf16)

    lane_tile = iota((16, 128), 1) >> 5
    slot_masks = []
    for s in range(4):
        mask = jnp.where(lane_tile == s, 1.0, 0.0).astype(bf16)
        slot_masks.append(jnp.concatenate([mask] * 3, axis=0))

    def place(k, first):
        _, _, na, a0, x0, rows, slab = plan[k]
        rows += rows % 2
        width = 4 * 2 * SBY
        lane = iota((1, width), 1)
        in_slot = (lane * 1366) >> 16
        b = lane - ((lane * 2731) >> 16) * SBY
        picks = []
        for h in range(2):
            target = b
            for s in range(4):
                target = target + jnp.where(in_slot == s, offset_of(k, 1, 4 * h + s), 0)
            picks.append(
                jnp.where(iota((fw, width), 0) + ystart == target, 1.0, 0.0).astype(bf16)
            )

        def one(i, carry):
            halves = []
            for h in range(2):
                columns = []
                for step in range(2):
                    local = x0 + 2 * i + step - slab * fx - a0
                    pieces = []
                    for s in range(4):
                        at = local - offset_of(k, 0, 4 * h + s)
                        at = jnp.where(jnp.logical_and(at >= 0, at < na), at, na)
                        pieces.append(folded[k][at, :, 128 * h : 128 * h + 128] * slot_masks[s])
                    columns.append(jnp.concatenate(pieces, axis=0))
                halves.append(jnp.dot(
                    picks[h], jnp.concatenate(columns, axis=1), preferred_element_type=f32
                ))
            parts = []
            for step in range(2):
                at = slice(128 * step, 128 * step + 128)
                value = jnp.concatenate([halves[0][:, at], halves[1][:, at]], axis=1)
                parts.append(jnp.concatenate(split(value), axis=1))
            lined[pl.ds(pl.multiple_of(i * (2 * fw), 2 * fw), 2 * fw), :] = jnp.concatenate(
                parts, axis=0
            ).astype(bf16)
            return carry

        lax.fori_loop(0, rows // 2, one, 0, unroll=2 if rows % 4 == 0 else 1)
        lane_row = iota((SPAN, fz), 0)
        depth = lane_row & (SLOT_LANES - 1)
        for s in range(slots):
            depth = depth + jnp.where((lane_row >> 5) == s, offset_of(k, 2, s), 0)
        inside_line = (lane_row & (SLOT_LANES - 1)) < SBZ
        hit = jnp.logical_and(inside_line, iota((SPAN, fz), 1) == depth)
        pick = jnp.where(hit, 1.0, 0.0).astype(bf16)
        pick = jnp.concatenate([pick, pick], axis=0)
        for start in range(0, rows, 4):
            size = min(4, rows - start)
            value = jnp.dot(
                lined[start * fw : (start + size) * fw, :], pick, preferred_element_type=f32
            ).reshape(size, fw, fz)
            at = x0 + HALO + start
            if first:
                dens[at : at + size, window] = value
            else:
                dens[at : at + size, window] = dens[at : at + size, window] + value

    window = slice(8, fw + 8)
    dens[0:HALO, window] = jnp.zeros((HALO, fw, fz), f32)
    unfold((0,))
    place(0, True)

    own.wait()
    for copy in part_copies:
        copy.wait_recv()
    total = win[...]
    for k in range(1, G):
        total = total + recv[k - 1]
    cext[2 : cx + 2, 8 : 8 + yc] = total
    rows_from = {-1: pl.ds(2, 2), 0: pl.ds(2, cx), 1: pl.ds(cx, 2)}
    rows_to = {-1: pl.ds(cx + 2, 2), 0: pl.ds(2, cx), 1: pl.ds(0, 2)}
    cols_from = {-1: pl.ds(8, 8), 0: pl.ds(8, yc), 1: pl.ds(yc, 8)}
    cols_to = {-1: pl.ds(yc + 8, 8), 0: pl.ds(8, yc), 1: pl.ds(0, 8)}
    halo_copies = {}
    for n, (dj, dd) in enumerate(sides):
        halo_copies[dj, dd] = pltpu.make_async_remote_copy(
            src_ref=cext.at[rows_from[dd], cols_from[dj]],
            dst_ref=cext.at[rows_to[dd], cols_to[dj]],
            send_sem=cs_sem.at[n], recv_sem=cr_sem.at[n],
            device_id=(j + dj, d + dd), device_id_type=MESH,
        )

        @pl.when(beside[dj, dd])
        def _(dj=dj, dd=dd):
            halo_copies[dj, dd].start()

    for k in (1, 2, 3):

        @pl.when(inside[plan[k][6]])
        def _(k=k):
            offset_copies[k].wait_recv()
            for copy in block_copies[k]:
                copy.wait_recv()

        @pl.when(jnp.logical_not(inside[plan[k][6]]))
        def _(k=k):
            blocks[k][...] = jnp.zeros(blocks[k].shape, f32)
            for row in range(3):
                for s in range(slots):
                    offs[k, row, s] = 0

    unfold((1, 2, 3))

    for k in (1, 2, 3):
        place(k, False)

    for dj, dd in sides:

        @pl.when(beside[-dj, -dd])
        def _(dj=dj, dd=dd):
            halo_copies[dj, dd].wait_recv()

    count_x = fx + 2 * HALO
    zi, zo = iota((cz, fz), 0), iota((cz, fz), 1)
    zm = zo >> 1
    zn = zm + ((zo & 1) << 1) - 1
    refine_z = weights((cz, fz), ((zi == zm, 0.75), (zi == zn, 0.25))).astype(bf16)
    refine_z = jnp.concatenate([refine_z, refine_z], axis=0)
    yo = iota((fw, yw), 0) + ystart
    yi = iota((fw, yw), 1) + (yc * q - 8)
    ym = yo >> 1
    yn = ym + ((yo & 1) << 1) - 1
    grid = jnp.logical_and(yo >= 0, yo < fy)
    refine_y = weights(
        (fw, yw), ((jnp.logical_and(grid, yi == ym), 0.75), (jnp.logical_and(grid, yi == yn), 0.25))
    )
    refine_y = jnp.concatenate([refine_y, refine_y], axis=1).astype(bf16)

    def in_grid(x):
        g = d * fx + x
        return jnp.where(jnp.logical_and(g >= 0, g < N * fx), 1.0, 0.0).astype(f32)

    def refine_pair(i, carry):
        low_cell, high_cell = cext[i], cext[i + 1]
        odd = 0.75 * low_cell + 0.25 * high_cell
        even = 0.75 * high_cell + 0.25 * low_cell
        both = jnp.concatenate([odd, even], axis=1)
        right = jnp.concatenate(split(both), axis=0).astype(bf16)
        value = jnp.dot(refine_y, right, preferred_element_type=f32)
        value = jnp.concatenate([value[:, :cz], value[:, cz:]], axis=0)
        lined_coarse[pl.ds(pl.multiple_of(i * (2 * fw), 2 * fw), 2 * fw), :] = jnp.concatenate(
            split(value), axis=1
        ).astype(bf16)
        return carry

    lax.fori_loop(0, count_x // 2, refine_pair, 0, unroll=3)
    for start in range(0, count_x, 3):
        value = jnp.dot(
            lined_coarse[start * fw : (start + 3) * fw, :], refine_z, preferred_element_type=f32
        ).reshape(3, fw, fz)
        for i in range(3):
            dens[start + i, window] = (dens[start + i, window] + value[i]) * in_grid(start + i - HALO)

    lanes = iota((8, 128), 1)
    first_lane, last_lane = lanes == 0, lanes == 127
    tiles = fz // 128

    def diff_z(f):
        parts = [f[:, 128 * t : 128 * t + 128] for t in range(tiles)]
        ahead = [pltpu.roll(part, 127, 1) for part in parts] + [0.0]
        behind = [0.0] + [pltpu.roll(part, 1, 1) for part in parts]
        return jnp.concatenate(
            [
                jnp.where(last_lane, ahead[t + 1], ahead[t])
                - jnp.where(first_lane, behind[t], behind[t + 1])
                for t in range(tiles)
            ],
            axis=1,
        )

    def exchange_row(i, carry):
        for line in range(0, fw, 8):
            exchange_tile(i, line)
        return carry

    def exchange_tile(i, line):
        at = slice(line, line + 8)
        here = slice(line + 8, line + 16)
        n = dens[i + 1, here]
        gx = dens[i + 2, here] - dens[i, here]
        gy = dens[i + 1, line + 9 : line + 17] - dens[i + 1, line + 7 : line + 15]
        gz = diff_z(n)
        sigma = gx * gx + gy * gy + gz * gz
        live = n > 0.0
        log_n = jnp.log(jnp.where(live, n, 1.0))
        cube_root = jnp.exp2(log_n * (log2_e / 3.0))
        inv_ft = jnp.exp2(log_n * (-4.0 * log2_e / 3.0))
        scale = half_inverse * half_inverse * mu_pbe / (kappa_pbe * gradient_scale)
        inv_d = 1.0 / (1.0 + sigma * (inv_ft * inv_ft * scale))
        inv_d2 = inv_d * inv_d
        by_density = cube_root * (
            exchange_prefactor * 4.0 / 3.0 * (1.0 + kappa_pbe)
            - (exchange_prefactor * 4.0 * kappa_pbe) * inv_d
            + (exchange_prefactor * 8.0 / 3.0 * kappa_pbe) * inv_d2
        )
        twice = 2.0 * exchange_prefactor * half_inverse * half_inverse * mu_pbe / gradient_scale
        twice = jnp.where(live, (twice * inv_ft) * inv_d2, 0.0)
        flux[i, at] = twice * gx
        flux_y[i, here] = twice * gy
        pot[i, at] = by_density - diff_z(twice * gz)


    ro, ri = iota((yc, fw), 0), iota((yc, fw), 1)
    at = ri - 4 - 2 * ro
    grid = jnp.logical_and(ri + ystart >= 0, ri + ystart < fy)
    inner = jnp.logical_and(grid, jnp.logical_or(at == 0, at == 1))
    outer = jnp.logical_and(grid, jnp.logical_or(at == -1, at == 2))
    restrict_y = weights((yc, fw), ((inner, 0.375), (outer, 0.125)))
    restrict_y = jnp.concatenate([restrict_y, restrict_y], axis=1).astype(bf16)
    at = iota((fz, cz), 0) - 2 * iota((fz, cz), 1)
    inner = jnp.logical_or(at == 0, at == 1)
    outer = jnp.logical_or(at == -1, at == 2)
    restrict_z = weights((fz, cz), ((inner, 0.375), (outer, 0.125))).astype(bf16)
    restrict_z = jnp.concatenate([restrict_z, restrict_z], axis=0)

    def full(x, line):
        at = slice(line, line + 8)
        spread = flux[x + 3, at] - flux[x + 1, at]
        spread = spread + (flux_y[x + 2, line + 9 : line + 17] - flux_y[x + 2, line + 7 : line + 15])
        return (pot[x + 2, at] - spread) * in_grid(x)

    ymine = pl.multiple_of(q * yc, 8)

    def restrict_rows(low_row, high_row):
        pieces = []
        for i in range(low_row, high_row):
            x = 2 * i
            high, low = [], []
            for line in range(0, fw, 8):
                mixed = 0.125 * (full(x - 1, line) + full(x + 2, line))
                mixed = mixed + 0.375 * (full(x, line) + full(x + 1, line))
                upper, lower = split(mixed)
                high.append(upper)
                low.append(lower)
            pieces.append(jnp.dot(
                restrict_y,
                jnp.concatenate(high + low, axis=0).astype(bf16),
                preferred_element_type=f32,
            ))
        high, low = split(jnp.concatenate(pieces, axis=0))
        result = jnp.dot(
            jnp.concatenate([high, low], axis=1).astype(bf16), restrict_z, preferred_element_type=f32
        )
        mine[low_row:high_row] = result.reshape(high_row - low_row, yc, cz)

    gather = []
    keep = []
    done = 0
    for piece, (low_row, high_row) in enumerate(
        (cx * n // PIECES, cx * (n + 1) // PIECES) for n in range(PIECES)
    ):
        lax.fori_loop(done, 2 * high_row + 4, exchange_row, 0, unroll=2)
        done = 2 * high_row + 4
        restrict_rows(low_row, high_row)
        rows = pl.ds(low_row, high_row - low_row)
        at = (rows, pl.ds(ymine, yc), slice(None))
        for k in range(1, Q):
            copy = pltpu.make_async_remote_copy(
                src_ref=mine.at[rows],
                dst_ref=out.at[at],
                send_sem=gs_sem.at[piece, k - 1], recv_sem=gr_sem.at[piece, k - 1],
                device_id=(base + lax.rem(q + k, Q), d), device_id_type=MESH,
            )
            copy.start()
            gather.append(copy)
        copy = pltpu.make_async_copy(mine.at[rows], out.at[at], keep_sem.at[piece])
        copy.start()
        keep.append(copy)
    for copy in part_copies:
        copy.wait_send()
    for k in (1, 2, 3):

        @pl.when(inside[-plan[k][6]])
        def _(k=k):
            offset_copies[k].wait_send()
            for copy in block_copies[k]:
                copy.wait_send()

    for dj, dd in sides:

        @pl.when(beside[dj, dd])
        def _(dj=dj, dd=dd):
            halo_copies[dj, dd].wait_send()

    for copy in gather + keep:
        copy.wait()


def body(G, N, Q, partial_density, moments, shape_functions, sphere_offsets, owned_count):
    _, cx, cy, cz = partial_density.shape
    slots, channels, block = shape_functions.shape
    fx, fz = 2 * cx, 2 * cz
    yc = cy // Q
    yw, fw = yc + 16, 2 * yc + 8
    plan = sources(fx)
    hbm = pl.BlockSpec(memory_space=pl.ANY)
    return pl.pallas_call(
        functools.partial(kernel, G, N, Q),
        out_shape=jax.ShapeDtypeStruct((cx, cy, cz), f32),
        in_specs=[hbm] * 5,
        out_specs=hbm,
        scratch_shapes=[
            pltpu.VMEM((slots, channels), bf16),
            pltpu.SMEM(sphere_offsets.shape, jnp.int32),
            pltpu.SMEM((1,), jnp.int32),
            pltpu.VMEM((channels, slots, block), bf16),
            pltpu.VMEM((cx, yc, cz), f32),
            pltpu.VMEM((G - 1, cx, yc, cz), f32),
            pltpu.VMEM((cx + 4, yw, cz), f32),
        ]
        + [pltpu.VMEM((slots, p[1] * GROUP), f32) for p in plan]
        + [pltpu.VMEM((slots, 26 * GROUP), f32)] * 2
        + [pltpu.SMEM((4,) + sphere_offsets.shape, jnp.int32)]
        + [pltpu.VMEM((2, 4, SPAN, 128), bf16), pltpu.VMEM((2, 26 * LINES, slots * 2 * SPAN), bf16)]
        + [pltpu.VMEM((p[2] + 1, 2 * SBY, SPAN), bf16) for p in plan]
        + [
            pltpu.VMEM(((fx + 4) * fw, 2 * SPAN), bf16),
            pltpu.VMEM(((fx + 2 * HALO) * fw, 2 * cz), bf16),
            pltpu.VMEM((fx + 2 * HALO + 1, fw + 16, fz), f32),
            pltpu.VMEM((fx + 4, fw, fz), f32),
            pltpu.VMEM((fx + 4, fw + 16, fz), f32),
            pltpu.VMEM((fx + 4, fw, fz), f32),
            pltpu.VMEM((cx, yc, cz), f32),
            pltpu.SemaphoreType.DMA((3,)),
            pltpu.SemaphoreType.DMA((PIECES,)),
            pltpu.SemaphoreType.DMA(()),
            pltpu.SemaphoreType.DMA((G - 1,)),
            pltpu.SemaphoreType.DMA((G - 1,)),
            pltpu.SemaphoreType.DMA((8,)),
            pltpu.SemaphoreType.DMA((8,)),
            pltpu.SemaphoreType.DMA((PIECES + 2,)),
            pltpu.SemaphoreType.DMA((PIECES + 2,)),
            pltpu.SemaphoreType.DMA((4,)),
            pltpu.SemaphoreType.DMA((4,)),
            pltpu.SemaphoreType.DMA((PIECES, Q - 1)),
            pltpu.SemaphoreType.DMA((PIECES, Q - 1)),
            pltpu.SemaphoreType.DMA((PIECES,)),
        ],
        compiler_params=pltpu.CompilerParams(
            collective_id=0, has_side_effects=True, vmem_limit_bytes=54900 * 1024
        ),
    )(partial_density, moments.T, shape_functions.transpose(1, 0, 2), sphere_offsets, owned_count)


def solution(mesh):
    G, N = mesh.shape["band"], mesh.shape["dom"]

    def run(partial_density, *rest):
        cy = partial_density.shape[2]
        Q = max(c for c in range(1, G + 1) if G % c == 0 and cy % (8 * c) == 0)
        return jax.shard_map(
            functools.partial(body, G, N, Q),
            mesh=mesh,
            in_specs=(
                P("band", "dom", None, None),
                P(None, "dom"),
                P("dom", None, None),
                P(None, "dom"),
                P("dom"),
            ),
            out_specs=P("dom", None, None),
            check_vma=False,
        )(partial_density, *rest)

    return run
```

```python
import functools

import jax
import jax.numpy as jnp
from jax import lax
from jax.experimental import pallas as pl
from jax.experimental.pallas import tpu as pltpu
from jax.sharding import PartitionSpec as P

SBX = 12
SBY = 24
SBZ = 24
GROUP = 384
LINES = 8
SPAN = 256
SLOT_LANES = 32
PIECES = 3
HALO = 3

kappa_pbe = 0.804
mu_pbe = 0.2195
exchange_prefactor = -0.75 * (3.0 / 3.141592653589793) ** (1.0 / 3.0)
gradient_scale = 4.0 * (3.0 * 3.141592653589793**2) ** (2.0 / 3.0)
half_inverse = 0.5 / 0.2
log2_e = 1.4426950408889634

f32 = jnp.float32
bf16 = jnp.bfloat16
MESH = pl.DeviceIdType.MESH


def iota(shape, dim):
    return lax.broadcasted_iota(jnp.int32, shape, dim)


def split(x):
    high = x.astype(bf16).astype(f32)
    return high, x - high


def weights(shape, terms):
    total = jnp.zeros(shape, f32)
    for mask, value in terms:
        total = jnp.where(mask, value, total)
    return total


def sources(fx):
    return (
        (SBX, 0, 0, fx + HALO, 0),
        (SBX, 0, -HALO, SBX - 1 + HALO, -1),
        (2, SBX - 2, -HALO, 2, -2),
        (HALO, 0, fx, HALO, 1),
    )


def kernel(
    G, N, Q,
    part, mom_hbm, shp_hbm, off_hbm, cnt_hbm,
    out,
    mom, off, cnt, shp, win, recv, cext, vh, vl, offs, unfolder, wide, u0, u1, u2, u3, b0, b1, b2, b3, lined, lined_coarse, dens, flux, pot, mine,
    small_sem, shp_sem, win_sem, ps_sem, pr_sem, cs_sem, cr_sem, vs_sem, vr_sem, os_sem, or_sem, gs_sem, gr_sem, keep_sem,
):
    _, cx, cy, cz = part.shape
    fx, fy, fz = 2 * cx, 2 * cy, 2 * cz
    yc = cy // Q
    yw = yc + 16
    fw = 2 * yc + 8
    j = lax.axis_index("band")
    d = lax.axis_index("dom")
    q = lax.rem(j, Q)

    def chunk_of(index):
        return pl.ds(pl.multiple_of(lax.rem(index, Q) * yc, 8), yc)

    own = pltpu.make_async_copy(part.at[0, :, chunk_of(j), :], win, win_sem)
    own.start()
    small = []
    for n, (source, target) in enumerate(((mom_hbm, mom), (off_hbm, off), (cnt_hbm, cnt))):
        small.append(pltpu.make_async_copy(source, target, small_sem.at[n]))
        small[-1].start()
    piece_lanes = shp.shape[2] // PIECES
    fetches = []
    for n in range(PIECES):
        at = (slice(None), slice(None), pl.ds(n * piece_lanes, piece_lanes))
        fetches.append(pltpu.make_async_copy(shp_hbm.at[at], shp.at[at], shp_sem.at[n]))
        fetches[-1].start()
    cext[...] = jnp.zeros(cext.shape, f32)
    base = j - q
    ystart = 2 * yc * q - 4
    slots = shp.shape[1]

    barrier = pltpu.get_barrier_semaphore()
    for k in range(1, G):
        pl.semaphore_signal(barrier, inc=1, device_id=(lax.rem(j + k, G), d), device_id_type=MESH)
    inside = {}
    for step in (-2, -1, 1, 2):
        inside[step] = jnp.logical_and(d + step >= 0, d + step < N)

        @pl.when(inside[step])
        def _(step=step):
            pl.semaphore_signal(barrier, inc=1, device_id=(j, d + step), device_id_type=MESH)

    sides = [(dj, dd) for dj in (-1, 0, 1) for dd in (-1, 0, 1) if dj or dd]
    beside = {}
    for dj, dd in sides:
        there = jnp.logical_and(q + dj >= 0, q + dj < Q)
        if dd:
            there = jnp.logical_and(there, inside[dd])
        beside[dj, dd] = there
        if dj and dd:

            @pl.when(there)
            def _(dj=dj, dd=dd):
                pl.semaphore_signal(barrier, inc=1, device_id=(j + dj, d + dd), device_id_type=MESH)

    count = G - 1
    for there in [inside[step] for step in (-2, -1, 1, 2)] + [
        beside[dj, dd] for dj, dd in sides if dj and dd
    ]:
        count = count + jnp.where(there, 1, 0)
    pl.semaphore_wait(barrier, count)

    part_copies = []
    for k in range(1, G):
        peer = lax.rem(j + k, G)
        copy = pltpu.make_async_remote_copy(
            src_ref=part.at[0, :, chunk_of(peer), :],
            dst_ref=recv.at[k - 1],
            send_sem=ps_sem.at[k - 1],
            recv_sem=pr_sem.at[k - 1],
            device_id=(peer, d),
            device_id_type=MESH,
        )
        copy.start()
        part_copies.append(copy)

    channels = shp.shape[0]
    for copy in small:
        copy.wait()
    plan = sources(fx)
    blocks = (b0, b1, b2, b3)
    folded = (u0, u1, u2, u3)
    offset_copies = [None]
    for k in (1, 2, 3):
        step = -plan[k][4]
        offset_copies.append(pltpu.make_async_remote_copy(
            src_ref=off,
            dst_ref=offs.at[k],
            send_sem=os_sem.at[k], recv_sem=or_sem.at[k],
            device_id=(j, d + step), device_id_type=MESH,
        ))

        @pl.when(inside[step])
        def _(k=k):
            offset_copies[k].start()

    moments = mom[...].astype(f32)
    moments = jnp.where(iota(moments.shape, 0) < cnt[0], moments, 0.0)
    scales = [jnp.broadcast_to(moments[:, l : l + 1], (slots, GROUP)) for l in range(channels)]
    for n in range(PIECES):
        fetches[n].wait()
        for g in range(n * piece_lanes // GROUP, (n + 1) * piece_lanes // GROUP):
            at = slice(g * GROUP, (g + 1) * GROUP)
            total = shp[0, :, at].astype(f32) * scales[0]
            for l in range(1, channels):
                total = total + shp[l, :, at].astype(f32) * scales[l]
            vh[:, at], vl[:, at] = split(total)

    line_masks = []
    for h in range(2):
        lane = iota((LINES, SPAN), 1) + 128 * h
        line_masks.append(((lane * 2731) >> 16) == iota((LINES, SPAN), 0) + LINES * h)
    k_rows, k_lanes = iota((SPAN, 128), 0), iota((SPAN, 128), 1)
    for h in range(2):
        k_rows_h = k_rows + 128 * h
        shift = k_lanes - (k_rows_h - ((k_rows_h * 2731) >> 16) * SBZ)
        for s in range(4):
            unfolder[h, s] = jnp.where(shift == SLOT_LANES * s, 1.0, 0.0).astype(bf16)

    def offset_of(k, row, s):
        return off[row, s] if k == 0 else offs[k, row, s]

    def fold(k):
        na = plan[k][0]
        high, low = split(blocks[k][...])
        folded[k][0:na] = jnp.concatenate([high, low], axis=1).astype(bf16)
        folded[k][na] = jnp.zeros((2 * SBY, SPAN), bf16)

    groups = shp.shape[2] // GROUP

    def unfold():
        def one(s, carry):
            for h in range(2):
                for t, source in enumerate((vh, vl)):
                    pieces = []
                    for g in range(groups):
                        at = g * GROUP + 128 * h
                        line = source[pl.ds(s, 1), at : at + SPAN]
                        pieces.append(
                            jnp.where(line_masks[h], jnp.broadcast_to(line, (LINES, SPAN)), 0.0)
                        )
                    lane = pl.multiple_of(s * (2 * SPAN) + t * SPAN, SPAN)
                    wide[h, : groups * LINES, pl.ds(lane, SPAN)] = jnp.concatenate(
                        pieces, axis=0
                    ).astype(bf16)
            return carry

        lax.fori_loop(0, slots, one, 0, unroll=2)
        halves = []
        for h in range(2):
            right = []
            for s in range(4):
                right += [unfolder[h, s]] * 2
            right = jnp.concatenate(right, axis=0)
            value = [
                jnp.dot(
                    wide[h, : groups * LINES, t * 8 * SPAN : (t + 1) * 8 * SPAN], right,
                    preferred_element_type=f32,
                )
                for t in range(2)
            ]
            value = jnp.concatenate(value, axis=1)
            halves.append(value.reshape(groups, LINES, SPAN))
        lines = jnp.stack(halves, axis=1).reshape(groups * 2 * LINES, SPAN)
        blocks[0][...] = lines.reshape(SBX, SBY, SPAN)

    lane_tile = iota((16, 128), 1) >> 5
    slot_masks = []
    for s in range(4):
        mask = jnp.where(lane_tile == s, 1.0, 0.0).astype(bf16)
        slot_masks.append(jnp.concatenate([mask] * 3, axis=0))

    def place(k, first):
        na, a0, x0, rows, slab = plan[k]
        rows += rows % 2
        width = 4 * 2 * SBY
        lane = iota((1, width), 1)
        in_slot = (lane * 1366) >> 16
        b = lane - ((lane * 2731) >> 16) * SBY
        picks = []
        for h in range(2):
            target = b
            for s in range(4):
                target = target + jnp.where(in_slot == s, offset_of(k, 1, 4 * h + s), 0)
            picks.append(
                jnp.where(iota((fw, width), 0) + ystart == target, 1.0, 0.0).astype(bf16)
            )

        def one(i, carry):
            halves = []
            for h in range(2):
                columns = []
                for step in range(2):
                    local = x0 + 2 * i + step - slab * fx - a0
                    pieces = []
                    for s in range(4):
                        at = local - offset_of(k, 0, 4 * h + s)
                        at = jnp.where(jnp.logical_and(at >= 0, at < na), at, na)
                        pieces.append(folded[k][at, :, 128 * h : 128 * h + 128] * slot_masks[s])
                    columns.append(jnp.concatenate(pieces, axis=0))
                halves.append(jnp.dot(
                    picks[h], jnp.concatenate(columns, axis=1), preferred_element_type=f32
                ))
            parts = []
            for step in range(2):
                at = slice(128 * step, 128 * step + 128)
                value = jnp.concatenate([halves[0][:, at], halves[1][:, at]], axis=1)
                parts.append(jnp.concatenate(split(value), axis=1))
            lined[pl.ds(pl.multiple_of(i * (2 * fw), 2 * fw), 2 * fw), :] = jnp.concatenate(
                parts, axis=0
            ).astype(bf16)
            return carry

        lax.fori_loop(0, rows // 2, one, 0, unroll=2 if rows % 4 == 0 else 1)
        lane_row = iota((SPAN, fz), 0)
        depth = lane_row & (SLOT_LANES - 1)
        for s in range(slots):
            depth = depth + jnp.where((lane_row >> 5) == s, offset_of(k, 2, s), 0)
        inside_line = (lane_row & (SLOT_LANES - 1)) < SBZ
        hit = jnp.logical_and(inside_line, iota((SPAN, fz), 1) == depth)
        pick = jnp.where(hit, 1.0, 0.0).astype(bf16)
        pick = jnp.concatenate([pick, pick], axis=0)
        for start in range(0, rows, 4):
            size = min(4, rows - start)
            value = jnp.dot(
                lined[start * fw : (start + size) * fw, :], pick, preferred_element_type=f32
            ).reshape(size, fw, fz)
            at = x0 + HALO + start
            if first:
                dens[at : at + size] = value
            else:
                dens[at : at + size] = dens[at : at + size] + value

    dens[0:HALO] = jnp.zeros((HALO, fw, fz), f32)
    unfold()
    block_copies = [None]
    for k in (1, 2, 3):
        na, a0, _, _, slab = plan[k]
        block_copies.append(pltpu.make_async_remote_copy(
            src_ref=b0.at[pl.ds(a0, na)],
            dst_ref=blocks[k],
            send_sem=vs_sem.at[k], recv_sem=vr_sem.at[k],
            device_id=(j, d - slab), device_id_type=MESH,
        ))

        @pl.when(inside[-slab])
        def _(k=k):
            block_copies[k].start()

    fold(0)
    place(0, True)

    own.wait()
    for copy in part_copies:
        copy.wait_recv()
    total = win[...]
    for k in range(1, G):
        total = total + recv[k - 1]
    cext[2 : cx + 2, 8 : 8 + yc] = total
    rows_from = {-1: pl.ds(2, 2), 0: pl.ds(2, cx), 1: pl.ds(cx, 2)}
    rows_to = {-1: pl.ds(cx + 2, 2), 0: pl.ds(2, cx), 1: pl.ds(0, 2)}
    cols_from = {-1: pl.ds(8, 8), 0: pl.ds(8, yc), 1: pl.ds(yc, 8)}
    cols_to = {-1: pl.ds(yc + 8, 8), 0: pl.ds(8, yc), 1: pl.ds(0, 8)}
    halo_copies = {}
    for n, (dj, dd) in enumerate(sides):
        halo_copies[dj, dd] = pltpu.make_async_remote_copy(
            src_ref=cext.at[rows_from[dd], cols_from[dj]],
            dst_ref=cext.at[rows_to[dd], cols_to[dj]],
            send_sem=cs_sem.at[n], recv_sem=cr_sem.at[n],
            device_id=(j + dj, d + dd), device_id_type=MESH,
        )

        @pl.when(beside[dj, dd])
        def _(dj=dj, dd=dd):
            halo_copies[dj, dd].start()

    for dj, dd in sides:

        @pl.when(beside[-dj, -dd])
        def _(dj=dj, dd=dd):
            halo_copies[dj, dd].wait_recv()

    count_x = fx + 2 * HALO
    zi, zo = iota((cz, fz), 0), iota((cz, fz), 1)
    zm = zo >> 1
    zn = zm + ((zo & 1) << 1) - 1
    refine_z = weights((cz, fz), ((zi == zm, 0.75), (zi == zn, 0.25))).astype(bf16)
    refine_z = jnp.concatenate([refine_z, refine_z], axis=0)
    yo = iota((fw, yw), 0) + ystart
    yi = iota((fw, yw), 1) + (yc * q - 8)
    ym = yo >> 1
    yn = ym + ((yo & 1) << 1) - 1
    grid = jnp.logical_and(yo >= 0, yo < fy)
    refine_y = weights(
        (fw, yw), ((jnp.logical_and(grid, yi == ym), 0.75), (jnp.logical_and(grid, yi == yn), 0.25))
    )
    refine_y = jnp.concatenate([refine_y, refine_y], axis=1).astype(bf16)

    def in_grid(x):
        g = d * fx + x
        return jnp.where(jnp.logical_and(g >= 0, g < N * fx), 1.0, 0.0).astype(f32)

    def refine_pair(i, carry):
        low_cell, high_cell = cext[i], cext[i + 1]
        odd = 0.75 * low_cell + 0.25 * high_cell
        even = 0.75 * high_cell + 0.25 * low_cell
        both = jnp.concatenate([odd, even], axis=1)
        right = jnp.concatenate(split(both), axis=0).astype(bf16)
        value = jnp.dot(refine_y, right, preferred_element_type=f32)
        value = jnp.concatenate([value[:, :cz], value[:, cz:]], axis=0)
        lined_coarse[pl.ds(pl.multiple_of(i * (2 * fw), 2 * fw), 2 * fw), :] = jnp.concatenate(
            split(value), axis=1
        ).astype(bf16)
        return carry

    lax.fori_loop(0, count_x // 2, refine_pair, 0, unroll=3)
    for start in range(0, count_x, 3):
        value = jnp.dot(
            lined_coarse[start * fw : (start + 3) * fw, :], refine_z, preferred_element_type=f32
        ).reshape(3, fw, fz)
        for i in range(3):
            dens[start + i] = (dens[start + i] + value[i]) * in_grid(start + i - HALO)

    for k in (3, 1, 2):
        slab = plan[k][4]

        @pl.when(inside[slab])
        def _(k=k):
            offset_copies[k].wait_recv()
            block_copies[k].wait_recv()

        @pl.when(jnp.logical_not(inside[slab]))
        def _(k=k):
            blocks[k][...] = jnp.zeros(blocks[k].shape, f32)
            for row in range(3):
                for s in range(slots):
                    offs[k, row, s] = 0

        fold(k)
        place(k, False)

    lanes = iota((fw, 128), 1)
    first_lane, last_lane = lanes == 0, lanes == 127
    tiles = fz // 128

    def diff_z(f):
        parts = [f[:, 128 * t : 128 * t + 128] for t in range(tiles)]
        ahead = [pltpu.roll(part, 127, 1) for part in parts] + [0.0]
        behind = [0.0] + [pltpu.roll(part, 1, 1) for part in parts]
        return jnp.concatenate(
            [
                jnp.where(last_lane, ahead[t + 1], ahead[t])
                - jnp.where(first_lane, behind[t], behind[t + 1])
                for t in range(tiles)
            ],
            axis=1,
        )

    def diff_y(f):
        return pltpu.roll(f, fw - 1, 0) - pltpu.roll(f, 1, 0)

    def exchange_row(i, carry):
        n = dens[i + 1]
        gx = dens[i + 2] - dens[i]
        gy = diff_y(n)
        gz = diff_z(n)
        sigma = gx * gx + gy * gy + gz * gz
        live = n > 0.0
        log_n = jnp.log(jnp.where(live, n, 1.0))
        cube_root = jnp.exp2(log_n * (log2_e / 3.0))
        inv_ft = jnp.exp2(log_n * (-4.0 * log2_e / 3.0))
        scale = half_inverse * half_inverse * mu_pbe / (kappa_pbe * gradient_scale)
        inv_d = 1.0 / (1.0 + sigma * (inv_ft * inv_ft * scale))
        inv_d2 = inv_d * inv_d
        by_density = cube_root * (
            exchange_prefactor * 4.0 / 3.0 * (1.0 + kappa_pbe)
            - (exchange_prefactor * 4.0 * kappa_pbe) * inv_d
            + (exchange_prefactor * 8.0 / 3.0 * kappa_pbe) * inv_d2
        )
        twice = 2.0 * exchange_prefactor * half_inverse * half_inverse * mu_pbe / gradient_scale
        twice = jnp.where(live, (twice * inv_ft) * inv_d2, 0.0)
        flux[i] = twice * gx
        pot[i] = by_density - (diff_y(twice * gy) + diff_z(twice * gz))
        return carry


    ro, ri = iota((yc, fw), 0), iota((yc, fw), 1)
    at = ri - 4 - 2 * ro
    grid = jnp.logical_and(ri + ystart >= 0, ri + ystart < fy)
    inner = jnp.logical_and(grid, jnp.logical_or(at == 0, at == 1))
    outer = jnp.logical_and(grid, jnp.logical_or(at == -1, at == 2))
    restrict_y = weights((yc, fw), ((inner, 0.375), (outer, 0.125)))
    restrict_y = jnp.concatenate([restrict_y, restrict_y], axis=1).astype(bf16)
    at = iota((fz, cz), 0) - 2 * iota((fz, cz), 1)
    inner = jnp.logical_or(at == 0, at == 1)
    outer = jnp.logical_or(at == -1, at == 2)
    restrict_z = weights((fz, cz), ((inner, 0.375), (outer, 0.125))).astype(bf16)
    restrict_z = jnp.concatenate([restrict_z, restrict_z], axis=0)

    def full(x):
        return (pot[x + 2] - (flux[x + 3] - flux[x + 1])) * in_grid(x)

    ymine = pl.multiple_of(q * yc, 8)

    def restrict_rows(low_row, high_row):
        pieces = []
        for i in range(low_row, high_row):
            x = 2 * i
            mixed = 0.125 * (full(x - 1) + full(x + 2)) + 0.375 * (full(x) + full(x + 1))
            high, low = split(mixed)
            pieces.append(jnp.dot(
                restrict_y,
                jnp.concatenate([high, low], axis=0).astype(bf16),
                preferred_element_type=f32,
            ))
        high, low = split(jnp.concatenate(pieces, axis=0))
        result = jnp.dot(
            jnp.concatenate([high, low], axis=1).astype(bf16), restrict_z, preferred_element_type=f32
        )
        mine[low_row:high_row] = result.reshape(high_row - low_row, yc, cz)

    gather = []
    keep = []
    done = 0
    for piece, (low_row, high_row) in enumerate(
        (cx * n // PIECES, cx * (n + 1) // PIECES) for n in range(PIECES)
    ):
        lax.fori_loop(done, 2 * high_row + 4, exchange_row, 0, unroll=2)
        done = 2 * high_row + 4
        restrict_rows(low_row, high_row)
        rows = pl.ds(low_row, high_row - low_row)
        at = (rows, pl.ds(ymine, yc), slice(None))
        for k in range(1, Q):
            copy = pltpu.make_async_remote_copy(
                src_ref=mine.at[rows],
                dst_ref=out.at[at],
                send_sem=gs_sem.at[piece, k - 1], recv_sem=gr_sem.at[piece, k - 1],
                device_id=(base + lax.rem(q + k, Q), d), device_id_type=MESH,
            )
            copy.start()
            gather.append(copy)
        copy = pltpu.make_async_copy(mine.at[rows], out.at[at], keep_sem.at[piece])
        copy.start()
        keep.append(copy)
    for copy in part_copies:
        copy.wait_send()
    for k in (1, 2, 3):

        @pl.when(inside[-plan[k][4]])
        def _(k=k):
            offset_copies[k].wait_send()
            block_copies[k].wait_send()

    for dj, dd in sides:

        @pl.when(beside[dj, dd])
        def _(dj=dj, dd=dd):
            halo_copies[dj, dd].wait_send()

    for copy in gather + keep:
        copy.wait()


def body(G, N, Q, partial_density, moments, shape_functions, sphere_offsets, owned_count):
    _, cx, cy, cz = partial_density.shape
    slots, channels, block = shape_functions.shape
    fx, fz = 2 * cx, 2 * cz
    yc = cy // Q
    yw, fw = yc + 16, 2 * yc + 8
    plan = sources(fx)
    hbm = pl.BlockSpec(memory_space=pl.ANY)
    return pl.pallas_call(
        functools.partial(kernel, G, N, Q),
        out_shape=jax.ShapeDtypeStruct((cx, cy, cz), f32),
        in_specs=[hbm] * 5,
        out_specs=hbm,
        scratch_shapes=[
            pltpu.VMEM((slots, channels), bf16),
            pltpu.SMEM(sphere_offsets.shape, jnp.int32),
            pltpu.SMEM((1,), jnp.int32),
            pltpu.VMEM((channels, slots, block), bf16),
            pltpu.VMEM((cx, yc, cz), f32),
            pltpu.VMEM((G - 1, cx, yc, cz), f32),
            pltpu.VMEM((cx + 4, yw, cz), f32),
        ]
        + [pltpu.VMEM((slots, block), f32)] * 2
        + [pltpu.SMEM((4,) + sphere_offsets.shape, jnp.int32)]
        + [pltpu.VMEM((2, 4, SPAN, 128), bf16), pltpu.VMEM((2, block // GROUP * LINES, slots * 2 * SPAN), bf16)]
        + [pltpu.VMEM((p[0] + 1, 2 * SBY, SPAN), bf16) for p in plan]
        + [pltpu.VMEM((p[0], SBY, SPAN), f32) for p in plan]
        + [
            pltpu.VMEM(((fx + 4) * fw, 2 * SPAN), bf16),
            pltpu.VMEM(((fx + 2 * HALO) * fw, 2 * cz), bf16),
            pltpu.VMEM((fx + 2 * HALO + 1, fw, fz), f32),
            pltpu.VMEM((fx + 4, fw, fz), f32),
            pltpu.VMEM((fx + 4, fw, fz), f32),
            pltpu.VMEM((cx, yc, cz), f32),
            pltpu.SemaphoreType.DMA((3,)),
            pltpu.SemaphoreType.DMA((PIECES,)),
            pltpu.SemaphoreType.DMA(()),
            pltpu.SemaphoreType.DMA((G - 1,)),
            pltpu.SemaphoreType.DMA((G - 1,)),
            pltpu.SemaphoreType.DMA((8,)),
            pltpu.SemaphoreType.DMA((8,)),
            pltpu.SemaphoreType.DMA((4,)),
            pltpu.SemaphoreType.DMA((4,)),
            pltpu.SemaphoreType.DMA((4,)),
            pltpu.SemaphoreType.DMA((4,)),
            pltpu.SemaphoreType.DMA((PIECES, Q - 1)),
            pltpu.SemaphoreType.DMA((PIECES, Q - 1)),
            pltpu.SemaphoreType.DMA((PIECES,)),
        ],
        compiler_params=pltpu.CompilerParams(
            collective_id=0, has_side_effects=True, vmem_limit_bytes=54900 * 1024
        ),
    )(partial_density, moments.T, shape_functions.transpose(1, 0, 2), sphere_offsets, owned_count)


def solution(mesh):
    G, N = mesh.shape["band"], mesh.shape["dom"]

    def run(partial_density, *rest):
        cy = partial_density.shape[2]
        Q = max(c for c in range(1, G + 1) if G % c == 0 and cy % (8 * c) == 0)
        return jax.shard_map(
            functools.partial(body, G, N, Q),
            mesh=mesh,
            in_specs=(
                P("band", "dom", None, None),
                P(None, "dom"),
                P("dom", None, None),
                P(None, "dom"),
                P("dom"),
            ),
            out_specs=P("dom", None, None),
            check_vma=False,
        )(partial_density, *rest)

    return run
```

```python
import functools

import jax
import jax.numpy as jnp
from jax import lax
from jax.experimental import pallas as pl
from jax.experimental.pallas import tpu as pltpu
from jax.sharding import PartitionSpec as P

SBX = 12
SBY = 24
SBZ = 24
GROUP = 384
LINES = 8
SPAN = 256
SLOT_LANES = 32
PIECES = 3
HALO = 3

kappa_pbe = 0.804
mu_pbe = 0.2195
exchange_prefactor = -0.75 * (3.0 / 3.141592653589793) ** (1.0 / 3.0)
gradient_scale = 4.0 * (3.0 * 3.141592653589793**2) ** (2.0 / 3.0)
half_inverse = 0.5 / 0.2
log2_e = 1.4426950408889634

f32 = jnp.float32
bf16 = jnp.bfloat16
MESH = pl.DeviceIdType.MESH


def iota(shape, dim):
    return lax.broadcasted_iota(jnp.int32, shape, dim)


def split(x):
    high = x.astype(bf16).astype(f32)
    return high, x - high


def weights(shape, terms):
    total = jnp.zeros(shape, f32)
    for mask, value in terms:
        total = jnp.where(mask, value, total)
    return total


def sources(fx):
    return (
        (0, 18, SBX, 0, 0, fx + HALO, 0),
        (0, 18, SBX, 0, -HALO, SBX - 1 + HALO, -1),
        (5760, 3, 2, 10, -HALO, 2, -2),
        (0, 5, 3, 0, fx, HALO, 1),
    )


def kernel(
    G, N, Q,
    part, mom_hbm, shp_hbm, off_hbm, cnt_hbm,
    out,
    mom, off, cnt, shp, win, recv, cext, v0, v1, v2, v3, vh, vl, offs, unfolder, wide, u0, u1, u2, u3, lined, lined_coarse, dens, flux, pot, mine,
    small_sem, shp_sem, win_sem, ps_sem, pr_sem, cs_sem, cr_sem, vs_sem, vr_sem, os_sem, or_sem, gs_sem, gr_sem, keep_sem,
):
    _, cx, cy, cz = part.shape
    fx, fy, fz = 2 * cx, 2 * cy, 2 * cz
    yc = cy // Q
    yw = yc + 16
    fw = 2 * yc + 8
    j = lax.axis_index("band")
    d = lax.axis_index("dom")
    q = lax.rem(j, Q)

    def chunk_of(index):
        return pl.ds(pl.multiple_of(lax.rem(index, Q) * yc, 8), yc)

    own = pltpu.make_async_copy(part.at[0, :, chunk_of(j), :], win, win_sem)
    own.start()
    small = []
    for n, (source, target) in enumerate(((mom_hbm, mom), (off_hbm, off), (cnt_hbm, cnt))):
        small.append(pltpu.make_async_copy(source, target, small_sem.at[n]))
        small[-1].start()
    piece_lanes = shp.shape[2] // PIECES
    fetches = []
    for n in range(PIECES):
        at = (slice(None), slice(None), pl.ds(n * piece_lanes, piece_lanes))
        fetches.append(pltpu.make_async_copy(shp_hbm.at[at], shp.at[at], shp_sem.at[n]))
        fetches[-1].start()
    cext[...] = jnp.zeros(cext.shape, f32)
    base = j - q
    ystart = 2 * yc * q - 4
    slots = shp.shape[1]

    barrier = pltpu.get_barrier_semaphore()
    for k in range(1, G):
        pl.semaphore_signal(barrier, inc=1, device_id=(lax.rem(j + k, G), d), device_id_type=MESH)
    inside = {}
    for step in (-2, -1, 1, 2):
        inside[step] = jnp.logical_and(d + step >= 0, d + step < N)

        @pl.when(inside[step])
        def _(step=step):
            pl.semaphore_signal(barrier, inc=1, device_id=(j, d + step), device_id_type=MESH)

    sides = [(dj, dd) for dj in (-1, 0, 1) for dd in (-1, 0, 1) if dj or dd]
    beside = {}
    for dj, dd in sides:
        there = jnp.logical_and(q + dj >= 0, q + dj < Q)
        if dd:
            there = jnp.logical_and(there, inside[dd])
        beside[dj, dd] = there
        if dj and dd:

            @pl.when(there)
            def _(dj=dj, dd=dd):
                pl.semaphore_signal(barrier, inc=1, device_id=(j + dj, d + dd), device_id_type=MESH)

    count = G - 1
    for there in [inside[step] for step in (-2, -1, 1, 2)] + [
        beside[dj, dd] for dj, dd in sides if dj and dd
    ]:
        count = count + jnp.where(there, 1, 0)
    pl.semaphore_wait(barrier, count)

    part_copies = []
    for k in range(1, G):
        peer = lax.rem(j + k, G)
        copy = pltpu.make_async_remote_copy(
            src_ref=part.at[0, :, chunk_of(peer), :],
            dst_ref=recv.at[k - 1],
            send_sem=ps_sem.at[k - 1],
            recv_sem=pr_sem.at[k - 1],
            device_id=(peer, d),
            device_id_type=MESH,
        )
        copy.start()
        part_copies.append(copy)

    channels = shp.shape[0]
    for copy in small:
        copy.wait()
    plan = sources(fx)
    blocks = (v0, v1, v2, v3)
    folded = (u0, u1, u2, u3)
    offset_copies = [None]
    for k in (1, 2, 3):
        step = -plan[k][6]
        offset_copies.append(pltpu.make_async_remote_copy(
            src_ref=off,
            dst_ref=offs.at[k],
            send_sem=os_sem.at[k], recv_sem=or_sem.at[k],
            device_id=(j, d + step), device_id_type=MESH,
        ))

        @pl.when(inside[step])
        def _(k=k):
            offset_copies[k].start()

    last = shp.shape[2] - plan[2][1] * GROUP
    cuts = [[(1, n * piece_lanes, n * piece_lanes, piece_lanes)] for n in range(PIECES)]
    cuts[0].append((3, 0, 0, plan[3][1] * GROUP))
    cuts[PIECES - 1].append((2, last, 0, plan[2][1] * GROUP))
    block_copies = {1: [], 2: [], 3: []}
    moments = mom[...].astype(f32)
    moments = jnp.where(iota(moments.shape, 0) < cnt[0], moments, 0.0)
    scales = [jnp.broadcast_to(moments[:, l : l + 1], (slots, GROUP)) for l in range(channels)]
    sent = 0
    for n in range(PIECES):
        fetches[n].wait()
        for g in range(n * piece_lanes // GROUP, (n + 1) * piece_lanes // GROUP):
            at = slice(g * GROUP, (g + 1) * GROUP)
            total = shp[0, :, at].astype(f32) * scales[0]
            for l in range(1, channels):
                total = total + shp[l, :, at].astype(f32) * scales[l]
            v0[:, at] = total
        for k, lane, there, lanes in cuts[n]:
            step = -plan[k][6]
            copy = pltpu.make_async_remote_copy(
                src_ref=v0.at[:, pl.ds(lane, lanes)],
                dst_ref=blocks[k].at[:, pl.ds(there, lanes)],
                send_sem=vs_sem.at[sent], recv_sem=vr_sem.at[sent],
                device_id=(j, d + step), device_id_type=MESH,
            )
            block_copies[k].append(copy)
            sent += 1

            @pl.when(inside[step])
            def _(copy=copy):
                copy.start()

    line_masks = []
    for h in range(2):
        lane = iota((LINES, SPAN), 1) + 128 * h
        line_masks.append(((lane * 2731) >> 16) == iota((LINES, SPAN), 0) + LINES * h)
    k_rows, k_lanes = iota((SPAN, 128), 0), iota((SPAN, 128), 1)
    for h in range(2):
        k_rows_h = k_rows + 128 * h
        shift = k_lanes - (k_rows_h - ((k_rows_h * 2731) >> 16) * SBZ)
        for s in range(4):
            unfolder[h, s] = jnp.where(shift == SLOT_LANES * s, 1.0, 0.0).astype(bf16)

    def offset_of(k, row, s):
        return off[row, s] if k == 0 else offs[k, row, s]

    def unfold(which):
        starts = []
        total = 0
        for k in which:
            starts.append(total)
            width = plan[k][1] * GROUP
            high, low = split(blocks[k][...])
            vh[:, total : total + width] = high
            vl[:, total : total + width] = low
            total += width
        groups = total // GROUP

        def one(s, carry):
            for h in range(2):
                for t, source in enumerate((vh, vl)):
                    pieces = []
                    for g in range(groups):
                        at = g * GROUP + 128 * h
                        line = source[pl.ds(s, 1), at : at + SPAN]
                        pieces.append(
                            jnp.where(line_masks[h], jnp.broadcast_to(line, (LINES, SPAN)), 0.0)
                        )
                    lane = pl.multiple_of(s * (2 * SPAN) + t * SPAN, SPAN)
                    wide[h, : groups * LINES, pl.ds(lane, SPAN)] = jnp.concatenate(
                        pieces, axis=0
                    ).astype(bf16)
            return carry

        lax.fori_loop(0, slots, one, 0, unroll=2)
        halves = []
        for h in range(2):
            right = []
            for s in range(4):
                right += [unfolder[h, s]] * 2
            right = jnp.concatenate(right, axis=0)
            value = [
                jnp.dot(
                    wide[h, : groups * LINES, t * 8 * SPAN : (t + 1) * 8 * SPAN], right,
                    preferred_element_type=f32,
                )
                for t in range(2)
            ]
            value = jnp.concatenate(value, axis=1)
            halves.append(value.reshape(groups, LINES, SPAN))
        lines = jnp.stack(halves, axis=1).reshape(groups * 2 * LINES, SPAN)
        for k, start in zip(which, starts):
            na = plan[k][2]
            at = start // GROUP * 2 * LINES
            high, low = split(lines[at : at + na * SBY].reshape(na, SBY, SPAN))
            folded[k][0:na] = jnp.concatenate([high, low], axis=1).astype(bf16)
            folded[k][na] = jnp.zeros((2 * SBY, SPAN), bf16)

    lane_tile = iota((16, 128), 1) >> 5
    slot_masks = []
    for s in range(4):
        mask = jnp.where(lane_tile == s, 1.0, 0.0).astype(bf16)
        slot_masks.append(jnp.concatenate([mask] * 3, axis=0))

    def place(k, first):
        _, _, na, a0, x0, rows, slab = plan[k]
        rows += rows % 2
        width = 4 * 2 * SBY
        lane = iota((1, width), 1)
        in_slot = (lane * 1366) >> 16
        b = lane - ((lane * 2731) >> 16) * SBY
        picks = []
        for h in range(2):
            target = b
            for s in range(4):
                target = target + jnp.where(in_slot == s, offset_of(k, 1, 4 * h + s), 0)
            picks.append(
                jnp.where(iota((fw, width), 0) + ystart == target, 1.0, 0.0).astype(bf16)
            )

        def one(i, carry):
            halves = []
            for h in range(2):
                columns = []
                for step in range(2):
                    local = x0 + 2 * i + step - slab * fx - a0
                    pieces = []
                    for s in range(4):
                        at = local - offset_of(k, 0, 4 * h + s)
                        at = jnp.where(jnp.logical_and(at >= 0, at < na), at, na)
                        pieces.append(folded[k][at, :, 128 * h : 128 * h + 128] * slot_masks[s])
                    columns.append(jnp.concatenate(pieces, axis=0))
                halves.append(jnp.dot(
                    picks[h], jnp.concatenate(columns, axis=1), preferred_element_type=f32
                ))
            parts = []
            for step in range(2):
                at = slice(128 * step, 128 * step + 128)
                value = jnp.concatenate([halves[0][:, at], halves[1][:, at]], axis=1)
                parts.append(jnp.concatenate(split(value), axis=1))
            lined[pl.ds(pl.multiple_of(i * (2 * fw), 2 * fw), 2 * fw), :] = jnp.concatenate(
                parts, axis=0
            ).astype(bf16)
            return carry

        lax.fori_loop(0, rows // 2, one, 0, unroll=2 if rows % 4 == 0 else 1)
        lane_row = iota((SPAN, fz), 0)
        depth = lane_row & (SLOT_LANES - 1)
        for s in range(slots):
            depth = depth + jnp.where((lane_row >> 5) == s, offset_of(k, 2, s), 0)
        inside_line = (lane_row & (SLOT_LANES - 1)) < SBZ
        hit = jnp.logical_and(inside_line, iota((SPAN, fz), 1) == depth)
        pick = jnp.where(hit, 1.0, 0.0).astype(bf16)
        pick = jnp.concatenate([pick, pick], axis=0)
        for start in range(0, rows, 4):
            size = min(4, rows - start)
            value = jnp.dot(
                lined[start * fw : (start + size) * fw, :], pick, preferred_element_type=f32
            ).reshape(size, fw, fz)
            at = x0 + HALO + start
            if first:
                dens[at : at + size] = value
            else:
                dens[at : at + size] = dens[at : at + size] + value

    dens[0:HALO] = jnp.zeros((HALO, fw, fz), f32)
    unfold((0,))
    place(0, True)

    own.wait()
    for copy in part_copies:
        copy.wait_recv()
    total = win[...]
    for k in range(1, G):
        total = total + recv[k - 1]
    cext[2 : cx + 2, 8 : 8 + yc] = total
    rows_from = {-1: pl.ds(2, 2), 0: pl.ds(2, cx), 1: pl.ds(cx, 2)}
    rows_to = {-1: pl.ds(cx + 2, 2), 0: pl.ds(2, cx), 1: pl.ds(0, 2)}
    cols_from = {-1: pl.ds(8, 8), 0: pl.ds(8, yc), 1: pl.ds(yc, 8)}
    cols_to = {-1: pl.ds(yc + 8, 8), 0: pl.ds(8, yc), 1: pl.ds(0, 8)}
    halo_copies = {}
    for n, (dj, dd) in enumerate(sides):
        halo_copies[dj, dd] = pltpu.make_async_remote_copy(
            src_ref=cext.at[rows_from[dd], cols_from[dj]],
            dst_ref=cext.at[rows_to[dd], cols_to[dj]],
            send_sem=cs_sem.at[n], recv_sem=cr_sem.at[n],
            device_id=(j + dj, d + dd), device_id_type=MESH,
        )

        @pl.when(beside[dj, dd])
        def _(dj=dj, dd=dd):
            halo_copies[dj, dd].start()

    for dj, dd in sides:

        @pl.when(beside[-dj, -dd])
        def _(dj=dj, dd=dd):
            halo_copies[dj, dd].wait_recv()

    count_x = fx + 2 * HALO
    zi, zo = iota((cz, fz), 0), iota((cz, fz), 1)
    zm = zo >> 1
    zn = zm + ((zo & 1) << 1) - 1
    refine_z = weights((cz, fz), ((zi == zm, 0.75), (zi == zn, 0.25))).astype(bf16)
    refine_z = jnp.concatenate([refine_z, refine_z], axis=0)
    yo = iota((fw, yw), 0) + ystart
    yi = iota((fw, yw), 1) + (yc * q - 8)
    ym = yo >> 1
    yn = ym + ((yo & 1) << 1) - 1
    grid = jnp.logical_and(yo >= 0, yo < fy)
    refine_y = weights(
        (fw, yw), ((jnp.logical_and(grid, yi == ym), 0.75), (jnp.logical_and(grid, yi == yn), 0.25))
    )
    refine_y = jnp.concatenate([refine_y, refine_y], axis=1).astype(bf16)

    def in_grid(x):
        g = d * fx + x
        return jnp.where(jnp.logical_and(g >= 0, g < N * fx), 1.0, 0.0).astype(f32)

    def refine_pair(i, carry):
        low_cell, high_cell = cext[i], cext[i + 1]
        odd = 0.75 * low_cell + 0.25 * high_cell
        even = 0.75 * high_cell + 0.25 * low_cell
        both = jnp.concatenate([odd, even], axis=1)
        right = jnp.concatenate(split(both), axis=0).astype(bf16)
        value = jnp.dot(refine_y, right, preferred_element_type=f32)
        value = jnp.concatenate([value[:, :cz], value[:, cz:]], axis=0)
        lined_coarse[pl.ds(pl.multiple_of(i * (2 * fw), 2 * fw), 2 * fw), :] = jnp.concatenate(
            split(value), axis=1
        ).astype(bf16)
        return carry

    lax.fori_loop(0, count_x // 2, refine_pair, 0, unroll=3)
    for start in range(0, count_x, 3):
        value = jnp.dot(
            lined_coarse[start * fw : (start + 3) * fw, :], refine_z, preferred_element_type=f32
        ).reshape(3, fw, fz)
        for i in range(3):
            dens[start + i] = (dens[start + i] + value[i]) * in_grid(start + i - HALO)

    for k in (1, 2, 3):

        @pl.when(inside[plan[k][6]])
        def _(k=k):
            offset_copies[k].wait_recv()
            for copy in block_copies[k]:
                copy.wait_recv()

        @pl.when(jnp.logical_not(inside[plan[k][6]]))
        def _(k=k):
            blocks[k][...] = jnp.zeros(blocks[k].shape, f32)
            for row in range(3):
                for s in range(slots):
                    offs[k, row, s] = 0

    unfold((1, 2, 3))

    for k in (1, 2, 3):
        place(k, False)

    lanes = iota((fw, 128), 1)
    first_lane, last_lane = lanes == 0, lanes == 127
    tiles = fz // 128

    def diff_z(f):
        parts = [f[:, 128 * t : 128 * t + 128] for t in range(tiles)]
        ahead = [pltpu.roll(part, 127, 1) for part in parts] + [0.0]
        behind = [0.0] + [pltpu.roll(part, 1, 1) for part in parts]
        return jnp.concatenate(
            [
                jnp.where(last_lane, ahead[t + 1], ahead[t])
                - jnp.where(first_lane, behind[t], behind[t + 1])
                for t in range(tiles)
            ],
            axis=1,
        )

    def diff_y(f):
        return pltpu.roll(f, fw - 1, 0) - pltpu.roll(f, 1, 0)

    def exchange_row(i, carry):
        n = dens[i + 1]
        gx = dens[i + 2] - dens[i]
        gy = diff_y(n)
        gz = diff_z(n)
        sigma = gx * gx + gy * gy + gz * gz
        live = n > 0.0
        log_n = jnp.log(jnp.where(live, n, 1.0))
        cube_root = jnp.exp2(log_n * (log2_e / 3.0))
        inv_ft = jnp.exp2(log_n * (-4.0 * log2_e / 3.0))
        scale = half_inverse * half_inverse * mu_pbe / (kappa_pbe * gradient_scale)
        inv_d = 1.0 / (1.0 + sigma * (inv_ft * inv_ft * scale))
        inv_d2 = inv_d * inv_d
        by_density = cube_root * (
            exchange_prefactor * 4.0 / 3.0 * (1.0 + kappa_pbe)
            - (exchange_prefactor * 4.0 * kappa_pbe) * inv_d
            + (exchange_prefactor * 8.0 / 3.0 * kappa_pbe) * inv_d2
        )
        twice = 2.0 * exchange_prefactor * half_inverse * half_inverse * mu_pbe / gradient_scale
        twice = jnp.where(live, (twice * inv_ft) * inv_d2, 0.0)
        flux[i] = twice * gx
        pot[i] = by_density - (diff_y(twice * gy) + diff_z(twice * gz))
        return carry


    ro, ri = iota((yc, fw), 0), iota((yc, fw), 1)
    at = ri - 4 - 2 * ro
    grid = jnp.logical_and(ri + ystart >= 0, ri + ystart < fy)
    inner = jnp.logical_and(grid, jnp.logical_or(at == 0, at == 1))
    outer = jnp.logical_and(grid, jnp.logical_or(at == -1, at == 2))
    restrict_y = weights((yc, fw), ((inner, 0.375), (outer, 0.125)))
    restrict_y = jnp.concatenate([restrict_y, restrict_y], axis=1).astype(bf16)
    at = iota((fz, cz), 0) - 2 * iota((fz, cz), 1)
    inner = jnp.logical_or(at == 0, at == 1)
    outer = jnp.logical_or(at == -1, at == 2)
    restrict_z = weights((fz, cz), ((inner, 0.375), (outer, 0.125))).astype(bf16)
    restrict_z = jnp.concatenate([restrict_z, restrict_z], axis=0)

    def full(x):
        return (pot[x + 2] - (flux[x + 3] - flux[x + 1])) * in_grid(x)

    ymine = pl.multiple_of(q * yc, 8)

    def restrict_rows(low_row, high_row):
        pieces = []
        for i in range(low_row, high_row):
            x = 2 * i
            mixed = 0.125 * (full(x - 1) + full(x + 2)) + 0.375 * (full(x) + full(x + 1))
            high, low = split(mixed)
            pieces.append(jnp.dot(
                restrict_y,
                jnp.concatenate([high, low], axis=0).astype(bf16),
                preferred_element_type=f32,
            ))
        high, low = split(jnp.concatenate(pieces, axis=0))
        result = jnp.dot(
            jnp.concatenate([high, low], axis=1).astype(bf16), restrict_z, preferred_element_type=f32
        )
        mine[low_row:high_row] = result.reshape(high_row - low_row, yc, cz)

    gather = []
    keep = []
    done = 0
    for piece, (low_row, high_row) in enumerate(
        (cx * n // PIECES, cx * (n + 1) // PIECES) for n in range(PIECES)
    ):
        lax.fori_loop(done, 2 * high_row + 4, exchange_row, 0, unroll=2)
        done = 2 * high_row + 4
        restrict_rows(low_row, high_row)
        rows = pl.ds(low_row, high_row - low_row)
        at = (rows, pl.ds(ymine, yc), slice(None))
        for k in range(1, Q):
            copy = pltpu.make_async_remote_copy(
                src_ref=mine.at[rows],
                dst_ref=out.at[at],
                send_sem=gs_sem.at[piece, k - 1], recv_sem=gr_sem.at[piece, k - 1],
                device_id=(base + lax.rem(q + k, Q), d), device_id_type=MESH,
            )
            copy.start()
            gather.append(copy)
        copy = pltpu.make_async_copy(mine.at[rows], out.at[at], keep_sem.at[piece])
        copy.start()
        keep.append(copy)
    for copy in part_copies:
        copy.wait_send()
    for k in (1, 2, 3):

        @pl.when(inside[-plan[k][6]])
        def _(k=k):
            offset_copies[k].wait_send()
            for copy in block_copies[k]:
                copy.wait_send()

    for dj, dd in sides:

        @pl.when(beside[dj, dd])
        def _(dj=dj, dd=dd):
            halo_copies[dj, dd].wait_send()

    for copy in gather + keep:
        copy.wait()


def body(G, N, Q, partial_density, moments, shape_functions, sphere_offsets, owned_count):
    _, cx, cy, cz = partial_density.shape
    slots, channels, block = shape_functions.shape
    fx, fz = 2 * cx, 2 * cz
    yc = cy // Q
    yw, fw = yc + 16, 2 * yc + 8
    plan = sources(fx)
    hbm = pl.BlockSpec(memory_space=pl.ANY)
    return pl.pallas_call(
        functools.partial(kernel, G, N, Q),
        out_shape=jax.ShapeDtypeStruct((cx, cy, cz), f32),
        in_specs=[hbm] * 5,
        out_specs=hbm,
        scratch_shapes=[
            pltpu.VMEM((slots, channels), bf16),
            pltpu.SMEM(sphere_offsets.shape, jnp.int32),
            pltpu.SMEM((1,), jnp.int32),
            pltpu.VMEM((channels, slots, block), bf16),
            pltpu.VMEM((cx, yc, cz), f32),
            pltpu.VMEM((G - 1, cx, yc, cz), f32),
            pltpu.VMEM((cx + 4, yw, cz), f32),
        ]
        + [pltpu.VMEM((slots, p[1] * GROUP), f32) for p in plan]
        + [pltpu.VMEM((slots, 26 * GROUP), f32)] * 2
        + [pltpu.SMEM((4,) + sphere_offsets.shape, jnp.int32)]
        + [pltpu.VMEM((2, 4, SPAN, 128), bf16), pltpu.VMEM((2, 26 * LINES, slots * 2 * SPAN), bf16)]
        + [pltpu.VMEM((p[2] + 1, 2 * SBY, SPAN), bf16) for p in plan]
        + [
            pltpu.VMEM(((fx + 4) * fw, 2 * SPAN), bf16),
            pltpu.VMEM(((fx + 2 * HALO) * fw, 2 * cz), bf16),
            pltpu.VMEM((fx + 2 * HALO + 1, fw, fz), f32),
            pltpu.VMEM((fx + 4, fw, fz), f32),
            pltpu.VMEM((fx + 4, fw, fz), f32),
            pltpu.VMEM((cx, yc, cz), f32),
            pltpu.SemaphoreType.DMA((3,)),
            pltpu.SemaphoreType.DMA((PIECES,)),
            pltpu.SemaphoreType.DMA(()),
            pltpu.SemaphoreType.DMA((G - 1,)),
            pltpu.SemaphoreType.DMA((G - 1,)),
            pltpu.SemaphoreType.DMA((8,)),
            pltpu.SemaphoreType.DMA((8,)),
            pltpu.SemaphoreType.DMA((PIECES + 2,)),
            pltpu.SemaphoreType.DMA((PIECES + 2,)),
            pltpu.SemaphoreType.DMA((4,)),
            pltpu.SemaphoreType.DMA((4,)),
            pltpu.SemaphoreType.DMA((PIECES, Q - 1)),
            pltpu.SemaphoreType.DMA((PIECES, Q - 1)),
            pltpu.SemaphoreType.DMA((PIECES,)),
        ],
        compiler_params=pltpu.CompilerParams(
            collective_id=0, has_side_effects=True, vmem_limit_bytes=54900 * 1024
        ),
    )(partial_density, moments.T, shape_functions.transpose(1, 0, 2), sphere_offsets, owned_count)


def solution(mesh):
    G, N = mesh.shape["band"], mesh.shape["dom"]

    def run(partial_density, *rest):
        cy = partial_density.shape[2]
        Q = max(c for c in range(1, G + 1) if G % c == 0 and cy % (8 * c) == 0)
        return jax.shard_map(
            functools.partial(body, G, N, Q),
            mesh=mesh,
            in_specs=(
                P("band", "dom", None, None),
                P(None, "dom"),
                P("dom", None, None),
                P(None, "dom"),
                P("dom"),
            ),
            out_specs=P("dom", None, None),
            check_vma=False,
        )(partial_density, *rest)

    return run
```
